128 devices in a mesh: wide: 16 (over z, y), narrow: 8 (over x, core).
Axes of the slice: x: 4, y: 4, z: 4, core: 2. Of those that a mesh axis runs over, the one named last changes fastest.
Arguments:
- nodes: bfloat16 [131072, 512], P(('wide', 'narrow')), may hold values from -20 to 20
- virtual: bfloat16 [16, 512], replicated, may hold values from -6 to 6
- w_query: bfloat16 [512, 512], replicated, may hold values from -0.25 to 0.25
- w_key: bfloat16 [512, 512], replicated, may hold values from -0.25 to 0.25
- w_value: bfloat16 [512, 512], replicated, may hold values from -0.25 to 0.25
- w_out: bfloat16 [512, 512], replicated, may hold values from -1 to 1
- col_blocks: int32 [1024, 4], P(('wide', 'narrow')), may hold values from 0 to 23, as said below
- col_count: int32 [1024], P(('wide', 'narrow')), may hold values from 2 to 4, as said below
- send_sel: int32 [16, 8, 16], P('wide', 'narrow'), may hold values from 0 to 7
- grad_out: bfloat16 [131072, 512], P(('wide', 'narrow')), may hold values from -6 to 6
- grad_virtual: float32 [16, 512], replicated, may hold values from -6 to 6
Outputs:
- out_nodes: bfloat16 [131072, 512], P(('wide', 'narrow'))
- out_virtual: float32 [16, 512], replicated
- grad_nodes: float32 [131072, 512], P(('wide', 'narrow'))
- virtual_grad: float32 [16, 512], replicated
- grad_query: float32 [512, 512], replicated
- grad_key: float32 [512, 512], replicated
- grad_value: float32 [512, 512], replicated
- grad_wout: float32 [512, 512], replicated
The draws below stay inside these ranges and needn't reach their ends.
Inputs may be any that keep to these rules, and one draw needn't show every extreme that they name: `col_blocks`: index j < 8 names the device's own block j, index 8 + p the block that device (p, same narrow index) provides by send_sel. The first entry of every row block is below 8; on every device each index from 8 to 23 is named by some live entry. Entry t of row block b is live when t < col_count[b]; every device has a row block with 2 and one with 4. send_sel[w, n, p] is the local block that device (w, n) provides to device (p, n).
All inputs are finite; a program needn't handle non-finite values.
Results may differ from the reference program's by a relative error of at most 0.007.
The reference program's roundings to bfloat16 on the way count: a program that leaves them out, or rounds other values in their place, can miss the bound.
Values may be sent and summed in bfloat16 or wider, within the bound.
A program may use at most 192 MiB of HBM per device.

```python
import math
import jax
import jax.numpy as jnp
from jax import lax

D = 512
HEADS = 8
VIRT = 16
BR = 128
KMAX = 4
BLOCKS_DEV = 8
NODES = 131072
N_WIDE = 16
N_NARROW = 8


def shuffle_rows(key):
    return jax.random.permutation(key, BLOCKS_DEV)


def layout_tables(key):
    devs = N_WIDE * N_NARROW
    key_first, key_rest, key_order, key_count = jax.random.split(key, 4)
    first = jax.random.randint(key_first, (devs, BLOCKS_DEV, 1), 0, BLOCKS_DEV, dtype=jnp.int32)
    rest = jax.random.randint(key_rest, (devs, BLOCKS_DEV, KMAX - 1), 0, BLOCKS_DEV + N_WIDE, dtype=jnp.int32)
    row_ids = jnp.arange(BLOCKS_DEV, dtype=jnp.int32)[None, :]
    slot_ids = jnp.arange(KMAX - 1, dtype=jnp.int32)[None, None, :]
    cover_ids = 3 * row_ids[:, :, None] + slot_ids
    covered = (cover_ids < N_WIDE) & (slot_ids < 3)
    rest = jnp.where(covered, BLOCKS_DEV + cover_ids, rest)
    floor = jnp.clip(N_WIDE - 3 * row_ids, 0, 3) + 1
    counts = jax.random.randint(key_count, (devs, BLOCKS_DEV), 2, KMAX + 1, dtype=jnp.int32)
    counts = jnp.maximum(counts, floor)
    counts = jnp.where(row_ids == BLOCKS_DEV - 2, 2, counts)
    counts = jnp.where(row_ids == BLOCKS_DEV - 1, KMAX, counts)
    table = jnp.concatenate([first, rest], axis=2)
    order = jax.vmap(shuffle_rows)(jax.random.split(key_order, devs)).astype(jnp.int32)
    table = jnp.take_along_axis(table, order[:, :, None], axis=1)
    counts = jnp.take_along_axis(counts, order, axis=1)
    return (table.reshape(devs * BLOCKS_DEV, KMAX), counts.reshape(devs * BLOCKS_DEV))


def draw_col_blocks(key, part):
    table, counts = layout_tables(key)
    return table


def draw_col_count(key, part):
    table, counts = layout_tables(key)
    return counts


def draw_nodes(key, part):
    key = jax.random.fold_in(key, 7)
    key_base, key_scale = jax.random.split(key)
    base = jax.random.truncated_normal(key_base, -4.0, 4.0, (NODES, D), jnp.float32)
    row_scale = jnp.exp(jax.random.uniform(key_scale, (NODES, 1), jnp.float32, math.log(0.5), math.log(5.0)))
    return (base * row_scale).astype(jnp.bfloat16)


def place_ends(drawn, own_key, smallest, largest):
    longest = drawn.shape.index(max(drawn.shape))
    spots = []
    for shift in (0, 1):
        where = [jax.random.randint(jax.random.fold_in(own_key, axis), (), 0, length) for axis, length in enumerate(drawn.shape)]
        where[longest] = (where[longest] + shift) % drawn.shape[longest]
        spots.append(tuple(where))
    return drawn.at[spots[0]].set(smallest).at[spots[1]].set(largest)


def block_levels(own_key, shape, cuts, smallest, top_value):
    factor_of, own = 1.0, jax.random.fold_in(own_key, 6)
    for axis_at, parts in cuts:
        steps = jnp.exp(jax.random.uniform(jax.random.fold_in(own, axis_at), (parts,), jnp.float32, smallest / len(cuts), top_value / len(cuts)))
        factor_of = factor_of * jnp.repeat(steps, shape[axis_at] // parts).reshape([-1 if axis == axis_at else 1 for axis in range(len(shape))])
    return factor_of


def normal_values(stream_key, extent, width, reach, cuts=(), kind=jnp.bfloat16):
    values = jax.random.normal(stream_key, extent, jnp.float32) * width
    if len(cuts) > 0:
        values = block_levels(stream_key, extent, cuts, -0.22, 0.18) * values
    return jnp.clip(values, min=-reach, max=reach).astype(kind)


def setup_inputs(seed: int = 0) -> dict:
    seeds = jax.random.split(jax.random.key(seed), 12)
    return {
        "nodes": draw_nodes(jax.random.fold_in(seeds[11], 71), 0),
        "virtual": normal_values(seeds[1], (VIRT, D), 1.0, 6.0),
        "w_query": normal_values(seeds[2], (D, D), D ** -0.5, 0.25),
        "w_key": normal_values(seeds[3], (D, D), D ** -0.5, 0.25),
        "w_value": normal_values(seeds[4], (D, D), D ** -0.5, 0.25),
        "w_out": normal_values(seeds[5], (D, D), (D // 16) ** -0.5, 1.0),
        "col_blocks": draw_col_blocks(jax.random.fold_in(seeds[11], 71), 0),
        "col_count": draw_col_count(jax.random.fold_in(seeds[11], 71), 0),
        "send_sel": place_ends(jax.random.randint(seeds[8], (N_WIDE, N_NARROW, N_WIDE), 0, BLOCKS_DEV), jax.random.fold_in(seeds[8], 1), 0, BLOCKS_DEV - 1).astype(jnp.int32),
        "grad_out": normal_values(seeds[9], (NODES, D), 1.0, 6.0, ((0, 128),)),
        "grad_virtual": normal_values(seeds[10], (VIRT, D), 1.0, 6.0, (), jnp.float32),
    }


SOFT_CAP = 5.0
EPSILON = 1e-06

def capped(scores):
    return SOFT_CAP * jnp.tanh(scores / SOFT_CAP)

def slope(capped_scores):
    return 1.0 - (capped_scores / SOFT_CAP) ** 2

def rounded(array):
    return lax.optimization_barrier(array.astype(jnp.bfloat16)).astype(jnp.float32)

def split_heads(array):
    return array.reshape(array.shape[:-1] + (HEADS, array.shape[-1] // HEADS)).astype(jnp.float32)

def merge_heads(array):
    return array.reshape(array.shape[:-2] + (array.shape[-2] * array.shape[-1],))

def project(left, right):
    return jnp.dot(left, right, preferred_element_type=jnp.float32)

def block_scores(queries, tile_keys, live, virt_keys):
    scale = (D // HEADS) ** (-0.5)
    query_heads = split_heads(queries)
    raw = jnp.einsum('rqhe,rtkhe->rhqtk', query_heads, split_heads(tile_keys)) * scale
    raw_virt = jnp.einsum('rqhe,vhe->rhqv', query_heads, split_heads(virt_keys)) * scale
    capped_tile = capped(raw)
    capped_virt = capped(raw_virt)
    expo = jnp.exp(capped_tile) * live[:, None, None, :, None]
    expo_virt = jnp.exp(capped_virt)
    total = lax.optimization_barrier(jnp.sum(expo, axis=(3, 4))) + lax.optimization_barrier(jnp.sum(expo_virt, axis=3))
    return (capped_tile, capped_virt, expo / total[..., None, None], expo_virt / total[..., None])

def block_output(probs, probs_virt, tile_values, virt_values):
    mixed = jnp.einsum('rhqtk,rtkhe->rqhe', probs.astype(jnp.float32), split_heads(tile_values))
    mixed = mixed + jnp.einsum('rhqv,vhe->rqhe', probs_virt.astype(jnp.float32), split_heads(virt_values))
    return merge_heads(mixed).astype(jnp.bfloat16)

def block_grads(queries, tile_keys, tile_values, virt_keys, virt_values, live, attended, d_attended):
    scale = (D // HEADS) ** (-0.5)
    capped_tile, capped_virt, weights, weights_virt = block_scores(queries, tile_keys, live, virt_keys)
    probs = rounded(weights)
    probs_virt = rounded(weights_virt)
    grad_heads = split_heads(d_attended)
    query_heads = split_heads(queries)
    key_heads = split_heads(tile_keys)
    virt_key_heads = split_heads(virt_keys)
    dprob = jnp.einsum('rqhe,rtkhe->rhqtk', grad_heads, split_heads(tile_values))
    dprob_virt = jnp.einsum('rqhe,vhe->rhqv', grad_heads, split_heads(virt_values))
    delta = jnp.einsum('rqhe,rqhe->rhq', grad_heads, split_heads(attended))
    dscore = rounded(scale * weights * (dprob - delta[..., None, None]) * slope(capped_tile))
    dscore_virt = rounded(scale * weights_virt * (dprob_virt - delta[..., None]) * slope(capped_virt))
    dquery = jnp.einsum('rhqtk,rtkhe->rqhe', dscore, key_heads)
    dquery = dquery + jnp.einsum('rhqv,vhe->rqhe', dscore_virt, virt_key_heads)
    dkey = jnp.einsum('rhqtk,rqhe->rtkhe', dscore, query_heads)
    dvalue = jnp.einsum('rhqtk,rqhe->rtkhe', probs, grad_heads)
    dvirt_key = jnp.einsum('rhqv,rqhe->vhe', dscore_virt, query_heads)
    dvirt_value = jnp.einsum('rhqv,rqhe->vhe', probs_virt, grad_heads)
    return (merge_heads(dquery), merge_heads(dkey), merge_heads(dvalue), merge_heads(dvirt_key), merge_heads(dvirt_value))

def virtual_terms(virt_queries, keys):
    scale = (D // HEADS) ** (-0.5)
    raw = jnp.einsum('vhe,nhe->hvn', split_heads(virt_queries), split_heads(keys)) * scale
    capped_virt = capped(raw)
    return (capped_virt, jnp.exp(capped_virt))

def virtual_grads(virt_queries, keys, values, capped_virt, expo_virt, dnum, dden):
    scale = (D // HEADS) ** (-0.5)
    dnum_heads = split_heads(dnum)
    dexpo = jnp.einsum('vhe,nhe->hvn', dnum_heads, split_heads(values)) + dden[:, :, None]
    dscore = rounded(scale * expo_virt * dexpo * slope(capped_virt))
    vq_part = merge_heads(jnp.einsum('hvn,nhe->vhe', dscore, split_heads(keys)))
    key_part = merge_heads(jnp.einsum('hvn,vhe->nhe', dscore, split_heads(virt_queries)))
    value_part = merge_heads(jnp.einsum('hvn,vhe->nhe', rounded(expo_virt), dnum_heads))
    return (vq_part, key_part, value_part)

def reference(nodes, virtual, w_query, w_key, w_value, w_out, col_blocks, col_count, send_sel, grad_out, grad_virtual):
    devs = N_WIDE * N_NARROW
    rows = BLOCKS_DEV * BR
    pool_size = BLOCKS_DEV + N_WIDE
    head_dim = D // HEADS
    queries = project(nodes, w_query).astype(jnp.bfloat16)
    keys = project(nodes, w_key).astype(jnp.bfloat16)
    values = project(nodes, w_value).astype(jnp.bfloat16)
    virt_q = project(virtual, w_query).astype(jnp.bfloat16)
    virt_k = project(virtual, w_key).astype(jnp.bfloat16)
    virt_v = project(virtual, w_value).astype(jnp.bfloat16)
    dev_ids = jnp.arange(devs, dtype=jnp.int32)
    narrow_of = dev_ids % N_NARROW
    wide_of = dev_ids // N_NARROW
    picks = send_sel.reshape(devs, N_WIDE)
    sources = jnp.arange(N_WIDE, dtype=jnp.int32)[None, :] * N_NARROW + narrow_of[:, None]
    source_blocks = picks[sources, wide_of[:, None]]
    remote_ids = sources * BLOCKS_DEV + source_blocks
    own_ids = dev_ids[:, None] * BLOCKS_DEV + jnp.arange(BLOCKS_DEV, dtype=jnp.int32)[None, :]
    pool_ids = jnp.concatenate([own_ids, remote_ids], axis=1).astype(jnp.int32)
    key_blocks = keys.reshape(-1, BR, D)
    value_blocks = values.reshape(-1, BR, D)
    live = (jnp.arange(KMAX, dtype=jnp.int32)[None, :] < col_count[:, None]).astype(jnp.float32)
    cols_dev = col_blocks.reshape(devs, BLOCKS_DEV, KMAX)
    live_dev = live.reshape(devs, BLOCKS_DEV, KMAX)
    q_dev = queries.reshape(devs, BLOCKS_DEV, BR, D)
    k_dev = keys.reshape(devs, rows, D)
    v_dev = values.reshape(devs, rows, D)

    def forward_one(inputs):
        q_one, k_one, v_one, cols, lv, ids = inputs
        glob = ids[cols]
        capped_tile, capped_virt, weights, weights_virt = block_scores(q_one, key_blocks[glob], lv, virt_k)
        attended = block_output(weights.astype(jnp.bfloat16), weights_virt.astype(jnp.bfloat16), value_blocks[glob], virt_v)
        capped_v, expo_v = virtual_terms(virt_q, k_one)
        den_part = lax.optimization_barrier(jnp.sum(expo_v, axis=2))
        num_part = merge_heads(jnp.einsum('hvn,nhe->vhe', rounded(expo_v), split_heads(v_one)))
        return (attended, den_part, num_part)
    attended_dev, dens, nums = lax.map(forward_one, (q_dev, k_dev, v_dev, cols_dev, live_dev, pool_ids))
    attended = attended_dev.reshape(NODES, D)
    out_nodes = project(attended, w_out).astype(jnp.bfloat16)
    vden = lax.optimization_barrier(jnp.sum(dens, axis=0))
    vnum = lax.optimization_barrier(jnp.sum(nums, axis=0))
    summary = (vnum.reshape(VIRT, HEADS, head_dim) / vden.T[:, :, None]).reshape(VIRT, D)
    summary_b = summary.astype(jnp.bfloat16)
    zeta = project(summary_b, w_out)
    radius = jnp.sqrt(lax.optimization_barrier(jnp.mean(zeta * zeta, axis=-1, keepdims=True)) + EPSILON)
    out_virtual = zeta / radius
    dzeta = grad_virtual / radius - zeta * lax.optimization_barrier(jnp.sum(grad_virtual * zeta, axis=-1, keepdims=True)) / (D * radius ** 3)
    dzeta_b = dzeta.astype(jnp.bfloat16)
    dsummary = project(dzeta_b, w_out.T)
    dnum = (dsummary.reshape(VIRT, HEADS, head_dim) / vden.T[:, :, None]).reshape(VIRT, D).astype(jnp.bfloat16)
    dden = -lax.optimization_barrier(jnp.sum((dsummary * summary).reshape(VIRT, HEADS, head_dim), axis=-1)).T / vden
    d_attended = project(grad_out, w_out.T).astype(jnp.bfloat16)
    x_dev = nodes.reshape(devs, rows, D)
    dy_dev = grad_out.reshape(devs, rows, D)
    da_dev = d_attended.reshape(devs, BLOCKS_DEV, BR, D)

    def backward_one(carry, inputs):
        q_one, k_one, v_one, x_one, att_one, da_one, dy_one, cols, lv, ids = inputs
        glob = ids[cols]
        dquery, dkey, dvalue, dvk, dvv = block_grads(q_one, key_blocks[glob], value_blocks[glob], virt_k, virt_v, lv, att_one, da_one)
        flat_cols = cols.reshape(-1)
        key_pool = jnp.zeros((pool_size, BR * D), jnp.float32).at[flat_cols].add(dkey.reshape(-1, BR * D))
        value_pool = jnp.zeros((pool_size, BR * D), jnp.float32).at[flat_cols].add(dvalue.reshape(-1, BR * D))
        capped_v, expo_v = virtual_terms(virt_q, k_one)
        vq_part, key_virt, value_virt = virtual_grads(virt_q, k_one, v_one, capped_v, expo_v, dnum, dden)
        own_k = (key_pool[:BLOCKS_DEV].reshape(rows, D) + key_virt).astype(jnp.bfloat16)
        own_v = (value_pool[:BLOCKS_DEV].reshape(rows, D) + value_virt).astype(jnp.bfloat16)
        far_k = key_pool[BLOCKS_DEV:].astype(jnp.bfloat16)
        far_v = value_pool[BLOCKS_DEV:].astype(jnp.bfloat16)
        dq_b = dquery.reshape(rows, D).astype(jnp.bfloat16)
        dx_local = project(dq_b, w_query.T) + project(own_k, w_key.T) + project(own_v, w_value.T)
        att_rows = att_one.reshape(rows, D)
        new_carry = (carry[0] + project(x_one.T, dq_b), carry[1] + project(x_one.T, own_k), carry[2] + project(x_one.T, own_v), carry[3] + project(att_rows.T, dy_one), carry[4] + vq_part, carry[5] + dvk, carry[6] + dvv)
        return (new_carry, (dx_local, far_k, far_v))
    square = jnp.zeros((D, D), jnp.float32)
    small = jnp.zeros((VIRT, D), jnp.float32)
    init = (square, square, square, square, small, small, small)
    sums, outs = lax.scan(backward_one, init, (q_dev, k_dev, v_dev, x_dev, attended_dev, da_dev, dy_dev, cols_dev, live_dev, pool_ids))
    dx_local, far_k, far_v = outs
    back_k = jnp.transpose(far_k.reshape(N_WIDE, N_NARROW, N_WIDE, BR * D), (2, 1, 0, 3)).reshape(-1, D)
    back_v = jnp.transpose(far_v.reshape(N_WIDE, N_NARROW, N_WIDE, BR * D), (2, 1, 0, 3)).reshape(-1, D)
    targets = (dev_ids[:, None] * BLOCKS_DEV + picks).reshape(-1).astype(jnp.int32)
    contrib = project(back_k, w_key.T) + project(back_v, w_value.T)
    grad_nodes = dx_local.reshape(-1, BR, D).at[targets].add(contrib.reshape(-1, BR, D)).reshape(NODES, D)
    sent_rows = nodes.reshape(-1, BR, D)[targets].reshape(-1, D)
    vq_grad = sums[4].astype(jnp.bfloat16)
    vk_grad = sums[5].astype(jnp.bfloat16)
    vv_grad = sums[6].astype(jnp.bfloat16)
    grad_query = sums[0] + project(virtual.T, vq_grad)
    grad_key = sums[1] + project(sent_rows.T, back_k) + project(virtual.T, vk_grad)
    grad_value = sums[2] + project(sent_rows.T, back_v) + project(virtual.T, vv_grad)
    grad_wout = sums[3] + project(summary_b.T, dzeta_b)
    virtual_grad = project(vq_grad, w_query.T) + project(vk_grad, w_key.T) + project(vv_grad, w_value.T)
    return (out_nodes, out_virtual, grad_nodes, virtual_grad, grad_query, grad_key, grad_value, grad_wout)
```

```python
import functools

import jax
import jax.numpy as jnp
from jax import lax
from jax.experimental import pallas as pl
from jax.experimental.pallas import tpu as pltpu
from jax.sharding import PartitionSpec as P

D = 512
HEADS = 8
VIRT = 16
BR = 128
HEAD = D // HEADS
HM = HEADS * VIRT
SCALE = HEAD ** (-0.5)
SOFT_CAP = 5.0
EPSILON = 1e-06
IN_CAP = SCALE / SOFT_CAP
BF = jnp.bfloat16
F32 = jnp.float32
MESH = pl.DeviceIdType.MESH
VMEM = pl.BlockSpec(memory_space=pltpu.VMEM)
SMEM = pl.BlockSpec(memory_space=pltpu.SMEM)
GROUP = 4


def dot(a, b):
    return lax.dot_general(a, b, (((1,), (0,)), ((), ())), preferred_element_type=F32)


def dot_nt(a, b):
    return lax.dot_general(a, b, (((1,), (1,)), ((), ())), preferred_element_type=F32)


def dot_tn(a, b):
    return lax.dot_general(a, b, (((0,), (0,)), ((), ())), preferred_element_type=F32)


def lanes(shape, axis=1):
    return lax.broadcasted_iota(jnp.int32, shape, axis)


class Place:
    def __init__(self, nwide, nnarrow):
        self.nwide, self.nnarrow = nwide, nnarrow
        self.ny = 4 if nwide == 16 else 2
        self.nz = nwide // self.ny
        self.nx = nnarrow // 2
        self.w = lax.axis_index("wide")
        self.n = lax.axis_index("narrow")
        self.z, self.y = self.w // self.ny, self.w % self.ny
        self.x, self.c = self.n // 2, self.n % 2

    def ahead(self, slot):
        dz, dy = slot // self.ny, slot % self.ny
        return ((self.z + dz) % self.nz) * self.ny + (self.y + dy) % self.ny

    def behind(self, slot):
        dz, dy = slot // self.ny, slot % self.ny
        return ((self.z + self.nz - dz) % self.nz) * self.ny + (self.y + self.ny - dy) % self.ny

    def narrow_at(self, step):
        return (self.n + step) % self.nnarrow

    def barrier(self):
        barrier = pltpu.get_barrier_semaphore()
        for slot in range(1, self.nwide):
            pl.semaphore_signal(
                barrier, inc=1, device_id={"wide": self.ahead(slot)}, device_id_type=MESH
            )
        for step in range(1, self.nnarrow):
            pl.semaphore_signal(
                barrier, inc=1, device_id={"narrow": self.narrow_at(step)}, device_id_type=MESH
            )
        pl.semaphore_wait(barrier, self.nwide + self.nnarrow - 2)


def push(src, dst, send, recv, device):
    copy = pltpu.make_async_remote_copy(
        src_ref=src, dst_ref=dst, send_sem=send, recv_sem=recv, device_id=device, device_id_type=MESH
    )
    copy.start()
    return copy


class SmallSum:
    def __init__(self, place, part, one, mid, two, out, sems):
        self.place, self.part, self.one, self.mid, self.two, self.out = place, part, one, mid, two, out
        self.sems = sems
        self.per = part.shape[0] // place.nnarrow

    def first(self):
        at, per = self.place, self.per
        self.copies = []
        for step in range(1, at.nnarrow):
            peer = at.narrow_at(step)
            self.copies.append(
                push(
                    self.part.at[pl.ds(peer * per, per)],
                    self.one.at[at.n],
                    self.sems.at[0, 0, step],
                    self.sems.at[0, 1, step],
                    {"narrow": peer},
                )
            )
        self.one[at.n] = self.part[pl.ds(at.n * per, per)]

    def second(self):
        at = self.place
        for copy in self.copies:
            copy.wait()
        total = self.one[0]
        for j in range(1, at.nnarrow):
            total = total + self.one[j]
        self.mid[...] = total
        self.copies = []
        for slot in range(1, at.nwide):
            self.copies.append(
                push(
                    self.mid,
                    self.two.at[at.w],
                    self.sems.at[1, 0, slot],
                    self.sems.at[1, 1, slot],
                    {"wide": at.ahead(slot)},
                )
            )
        self.two[at.w] = total

    def third(self):
        at, per = self.place, self.per
        for copy in self.copies:
            copy.wait()
        total = self.two[0]
        for j in range(1, at.nwide):
            total = total + self.two[j]
        self.out[pl.ds(at.n * per, per)] = total
        self.copies = []
        for step in range(1, at.nnarrow):
            self.copies.append(
                push(
                    self.out.at[pl.ds(at.n * per, per)],
                    self.out.at[pl.ds(at.n * per, per)],
                    self.sems.at[2, 0, step],
                    self.sems.at[2, 1, step],
                    {"narrow": at.narrow_at(step)},
                )
            )

    def finish(self):
        for copy in self.copies:
            copy.wait()


def small_sum_scratch(nwide, nnarrow, rows):
    per = 8 // nnarrow
    return [
        pltpu.VMEM((8, rows, 128), F32),
        pltpu.VMEM((nnarrow, per, rows, 128), F32),
        pltpu.VMEM((per, rows, 128), F32),
        pltpu.VMEM((nwide, per, rows, 128), F32),
        pltpu.VMEM((8, rows, 128), F32),
        pltpu.SemaphoreType.DMA((3, 2, max(nwide, nnarrow))),
    ]


def block_diagonal(rows16):
    tiled = jnp.concatenate([rows16] * HEADS, axis=0)
    head_row = lanes((HM, D), 0) // VIRT
    head_col = lanes((HM, D), 1) // HEAD
    return jnp.where(head_row == head_col, tiled, jnp.zeros_like(tiled))


def diagonal_rows(full):
    head_col = lanes((VIRT, D), 1) // HEAD
    total = jnp.zeros((VIRT, D), F32)
    for h in range(HEADS):
        total = jnp.where(head_col == h, full[h * VIRT : (h + 1) * VIRT], total)
    return total


def exchange_kernel(
    nwide,
    nnarrow,
    picks,
    nodes,
    virtual,
    w_query,
    w_key,
    w_value,
    w_out,
    grad_out,
    grad_virtual,
    queries,
    pool_k,
    pool_v,
    far,
    d_attended,
    vq_bd,
    vk_bd,
    vv_bd,
    dnum_bd,
    dden_out,
    out_virtual,
    summary_out,
    dzeta_out,
    stage,
    part,
    one,
    mid,
    two,
    summed,
    small_sems,
    send_sems,
    recv_sems,
):
    at = Place(nwide, nnarrow)
    rows = nodes.shape[0] * BR
    for slot in range(nwide):
        pick = picks[at.ahead(slot)]
        stage[slot * BR : (slot + 1) * BR, :] = nodes[pick]
    at.barrier()
    copies = [None]
    for slot in range(1, nwide):
        copies.append(
            push(
                stage.at[slot * BR : (slot + 1) * BR],
                far.at[slot * BR : (slot + 1) * BR],
                send_sems.at[slot],
                recv_sems.at[slot],
                {"wide": at.ahead(slot)},
            )
        )
    far[0:BR, :] = stage[0:BR, :]

    chunk = 256

    @pl.loop(0, rows // chunk)
    def _(i):
        here = pl.ds(pl.multiple_of(i * chunk, chunk), chunk)
        block = nodes[pl.ds(i * (chunk // BR), chunk // BR)].reshape(chunk, D)
        pool_k[here, :] = dot(block, w_key[...]).astype(BF)
        pool_v[here, :] = dot(block, w_value[...]).astype(BF)

    virt = virtual[...]
    vq_bd[...] = block_diagonal(dot(virt, w_query[...])).astype(BF)
    vk_bd[...] = block_diagonal(dot(virt, w_key[...])).astype(BF)
    vv_bd[...] = block_diagonal(dot(virt, w_value[...])).astype(BF)

    expo = jnp.exp(SOFT_CAP * jnp.tanh(dot_nt(vq_bd[...], pool_k[0:rows, :]) * IN_CAP))
    den = jnp.sum(expo, axis=1, keepdims=True)
    num = dot(expo.astype(BF), pool_v[0:rows, :])
    half = lanes((VIRT, 128)) // HEAD
    for h in range(HEADS):
        mine = slice(h * VIRT, (h + 1) * VIRT)
        pair = num[mine, (h // 2) * 128 : (h // 2 + 1) * 128]
        part[h] = jnp.where(half == h % 2, pair, jnp.broadcast_to(den[mine], (VIRT, 128)))
    small = SmallSum(at, part, one, mid, two, summed, small_sems)
    small.first()

    @pl.loop(0, rows // chunk)
    def _(i):
        here = pl.ds(pl.multiple_of(i * chunk, chunk), chunk)
        block = nodes[pl.ds(i * (chunk // BR), chunk // BR)].reshape(chunk, D)
        queries[here, :] = dot(block, w_query[...]).astype(BF)
        d_attended[here, :] = dot_nt(grad_out[here, :], w_out[...]).astype(BF)

    small.second()

    def project_far(first, count):
        for slot in range(max(first, 1), first + count):
            copies[slot].wait_recv()
        there = slice(rows + first * BR, rows + (first + count) * BR)
        landed = far[first * BR : (first + count) * BR, :]
        pool_k[there, :] = dot(landed, w_key[...]).astype(BF)
        pool_v[there, :] = dot(landed, w_value[...]).astype(BF)

    groups = list(range(0, nwide, 4))
    project_far(groups[0], 4)
    small.third()
    for first in groups[1:-1]:
        project_far(first, 4)
    small.finish()

    low = half == 0
    numbers, denoms, ddens = [], [], []
    for pair in range(HEADS // 2):
        even, odd = summed[2 * pair], summed[2 * pair + 1]
        numbers.append(jnp.where(low, even, odd))
        denoms.append(pltpu.roll(jnp.where(low, odd, even), HEAD, 1))
    vnum = jnp.concatenate(numbers, axis=1)
    vden = jnp.concatenate(denoms, axis=1)
    summary = vnum / vden
    summary_b = summary.astype(BF)
    zeta = dot(summary_b, w_out[...])
    radius = jnp.sqrt(jnp.mean(zeta * zeta, axis=1, keepdims=True) + EPSILON)
    out_virtual[...] = zeta / radius
    gv = grad_virtual[...]
    dzeta = gv / radius - zeta * jnp.sum(gv * zeta, axis=1, keepdims=True) / (
        D * radius * radius * radius
    )
    dzeta_b = dzeta.astype(BF)
    summary_out[...] = summary_b
    dzeta_out[...] = dzeta_b
    dsummary = dot_nt(dzeta_b, w_out[...])
    dnum_bd[...] = block_diagonal((dsummary / vden).astype(BF).astype(F32)).astype(BF)
    along = dsummary * summary
    for h in range(HEADS):
        lane_tile = slice((h // 2) * 128, (h // 2 + 1) * 128)
        mine = jnp.where(half == h % 2, along[:, lane_tile], 0.0)
        down = -jnp.sum(mine, axis=1, keepdims=True)
        den_h = denoms[h // 2][:, (h % 2) * HEAD : (h % 2) * HEAD + 1]
        dden_out[h * VIRT : (h + 1) * VIRT, :] = jnp.broadcast_to(down / den_h, (VIRT, 128))

    if len(groups) > 1:
        project_far(groups[-1], 4)
    for slot in range(1, nwide):
        copies[slot].wait_send()


def exchange(nwide, nnarrow, picks, nodes, virtual, w_query, w_key, w_value, w_out, grad_out, grad_virtual):
    rows = nodes.shape[0]
    pool = rows + nwide * BR
    shape = jax.ShapeDtypeStruct
    outs = [
        shape((rows, D), BF),
        shape((pool, D), BF),
        shape((pool, D), BF),
        shape((nwide * BR, D), BF),
        shape((rows, D), BF),
        shape((HM, D), BF),
        shape((HM, D), BF),
        shape((HM, D), BF),
        shape((HM, D), BF),
        shape((HM, 128), F32),
        shape((VIRT, D), F32),
        shape((VIRT, D), BF),
        shape((VIRT, D), BF),
    ]
    return pl.pallas_call(
        functools.partial(exchange_kernel, nwide, nnarrow),
        out_shape=outs,
        in_specs=[SMEM] + [VMEM] * 8,
        out_specs=[VMEM] * len(outs),
        scratch_shapes=[pltpu.VMEM((nwide * BR, D), BF)]
        + small_sum_scratch(nwide, nnarrow, VIRT)
        + [pltpu.SemaphoreType.DMA((nwide,)), pltpu.SemaphoreType.DMA((nwide,))],
        compiler_params=pltpu.CompilerParams(
            collective_id=0, has_side_effects=True, vmem_limit_bytes=48 * 1024 * 1024
        ),
        name="exchange",
    )(
        picks,
        nodes.reshape(rows // BR, BR, D),
        virtual,
        w_query,
        w_key,
        w_value,
        w_out,
        grad_out,
        grad_virtual,
    )


def attend_kernel(
    nwide,
    nnarrow,
    cols,
    counts,
    queries,
    d_attended,
    pool_k,
    pool_v,
    vq_bd,
    vk_bd,
    vv_bd,
    dnum_bd,
    dden,
    w_out,
    out_nodes,
    attended,
    dquery,
    part_k,
    part_v,
    vq_part,
    vk_part,
    vv_part,
    sum_k,
    sum_v,
    kcat,
    vcat,
    scores,
    dprob,
    probs,
    dscore,
    acc_vk,
    acc_vv,
):
    at = Place(nwide, nnarrow)
    rows = queries.shape[0]
    blocks = rows // BR
    kmax = kcat.shape[0] // BR
    keys = kmax * BR
    gw = GROUP * HEAD
    gr = GROUP * BR
    chunk = 256

    vq = vq_bd[...]
    dn = dnum_bd[...]
    acc_vk[...] = jnp.zeros_like(acc_vk)
    acc_vv[...] = jnp.zeros_like(acc_vv)
    vq_part[...] = jnp.zeros_like(vq_part)

    @pl.loop(0, rows // chunk)
    def _(i):
        here = pl.ds(pl.multiple_of(i * chunk, chunk), chunk)
        own_k, own_v = pool_k[here, :], pool_v[here, :]
        bend = jnp.tanh(dot_nt(vq, own_k) * IN_CAP)
        expo = jnp.exp(SOFT_CAP * bend)
        dexpo = dot_nt(dn, own_v) + dden[:, 0:1]
        ds = (expo * dexpo * (1.0 - bend * bend)).astype(BF)
        vq_part[...] += diagonal_rows(dot(ds, own_k)) * SCALE
        sum_k[here, :] = dot_tn(ds, vq)
        sum_v[here, :] = dot_tn(expo.astype(BF), dn)

    sum_k[rows:, :] = jnp.zeros((nwide * BR, D), F32)
    sum_v[rows:, :] = jnp.zeros((nwide * BR, D), F32)

    lane_head = lanes((BR, HM)) // VIRT
    group_head = lanes((BR, gw)) // HEAD
    half = lanes((BR, 128)) // HEAD

    def stacked(block):
        zero = jnp.zeros_like(block)
        return jnp.concatenate([jnp.where(group_head == h, block, zero) for h in range(GROUP)], axis=0)

    def gathered(full):
        total = full[0:BR]
        for h in range(1, GROUP):
            total = jnp.where(group_head == h, full[h * BR : (h + 1) * BR], total)
        return total

    def block(b, carry):
        here = pl.ds(pl.multiple_of(b * BR, BR), BR)
        count = counts[b]
        places = []
        for t in range(kmax):
            entry = cols[b * kmax + t]
            source = jnp.maximum(entry - blocks, 0)
            dz = (at.z + at.nz - source // at.ny) % at.nz
            dy = (at.y + at.ny - source % at.ny) % at.ny
            entry = jnp.where(entry < blocks, entry, blocks + dz * at.ny + dy)
            place = pl.ds(pl.multiple_of(entry * BR, BR), BR)
            places.append(place)
            kcat[t * BR : (t + 1) * BR, :] = pool_k[place, :]
            vcat[t * BR : (t + 1) * BR, :] = pool_v[place, :]
        live = [None, None] + [jnp.where(t < count, 1.0, 0.0).astype(F32) for t in range(2, kmax)]
        q = queries[here, :]
        da = d_attended[here, :]
        bend_v = jnp.tanh(dot_nt(q, vk_bd[...]) * IN_CAP)
        expo_v = jnp.exp(SOFT_CAP * bend_v)
        dprob_v = dot_nt(da, vv_bd[...])
        probs_v = jnp.zeros((BR, HM), F32)
        delta_v = jnp.zeros((BR, HM), F32)
        for g in range(HEADS // GROUP):
            wide = slice(g * gw, (g + 1) * gw)
            qm = stacked(q[:, wide])
            dam = stacked(da[:, wide])
            scores[...] = dot_nt(qm, kcat[:, wide])
            dprob[...] = dot_nt(dam, vcat[:, wide])
            step = 32
            for h in range(GROUP):
                head = g * GROUP + h
                virt_sum = jnp.sum(jnp.where(lane_head == head, expo_v, 0.0), axis=1, keepdims=True)
                inverses = []
                for r in range(0, BR, step):
                    at_rows = slice(h * BR + r, h * BR + r + step)
                    bends, expos = [], []
                    total = None
                    for t in range(kmax):
                        bend = jnp.tanh(scores[at_rows, t * BR : (t + 1) * BR] * IN_CAP)
                        expo = jnp.exp(SOFT_CAP * bend)
                        if live[t] is not None:
                            expo = expo * live[t]
                        bends.append(bend)
                        expos.append(expo)
                        total = expo if total is None else total + expo
                    inverse = 1.0 / (jnp.sum(total, axis=1, keepdims=True) + virt_sum[r : r + step])
                    inverses.append(inverse)
                    for t in range(kmax):
                        at_lanes = slice(t * BR, (t + 1) * BR)
                        weight = expos[t] * inverse
                        probs[at_rows, at_lanes] = weight.astype(BF)
                        scores[at_rows, at_lanes] = weight * (1.0 - bends[t] * bends[t])
                probs_v = jnp.where(lane_head == head, expo_v * jnp.concatenate(inverses, axis=0), probs_v)
            pv = probs_v.astype(BF)
            mixed = gathered(dot(probs[...], vcat[:, wide])) + dot(pv, vv_bd[:, wide])
            mixed_b = mixed.astype(BF)
            attended[here, wide] = mixed_b
            along = da[:, wide].astype(F32) * mixed_b.astype(F32)
            for h in range(GROUP):
                head = g * GROUP + h
                lane_tile = slice((h // 2) * 128, (h // 2 + 1) * 128)
                delta = jnp.sum(jnp.where(half == h % 2, along[:, lane_tile], 0.0), axis=1, keepdims=True)
                delta_v = jnp.where(lane_head == head, delta, delta_v)
                for r in range(0, BR, step):
                    at_rows = slice(h * BR + r, h * BR + r + step)
                    dscore[at_rows, :] = (
                        scores[at_rows, :] * (dprob[at_rows, :] - delta[r : r + step])
                    ).astype(BF)
            dk = dot_tn(dscore[...], qm)
            dv = dot_tn(probs[...], dam)
            for t in range(kmax):
                sum_k[places[t], wide] += dk[t * BR : (t + 1) * BR]
                sum_v[places[t], wide] += dv[t * BR : (t + 1) * BR]
            ds_v = (probs_v * (dprob_v - delta_v) * (1.0 - bend_v * bend_v)).astype(BF)
            dq = gathered(dot(dscore[...], kcat[:, wide])) + dot(ds_v, vk_bd[:, wide])
            dquery[here, wide] = (dq * SCALE).astype(BF)
        acc_vk[...] += dot_tn(ds_v, q)
        acc_vv[...] += dot_tn(pv, da)
        out_nodes[here, :] = dot(attended[here, :], w_out[...]).astype(BF)
        return carry

    lax.fori_loop(0, blocks, block, 0)

    @pl.loop(0, sum_k.shape[0] // chunk)
    def _(i):
        here = pl.ds(pl.multiple_of(i * chunk, chunk), chunk)
        part_k[here, :] = (sum_k[here, :] * SCALE).astype(BF)
        part_v[here, :] = sum_v[here, :].astype(BF)

    vk_part[...] = diagonal_rows(acc_vk[...]) * SCALE
    vv_part[...] = diagonal_rows(acc_vv[...])


def attend(nwide, nnarrow, cols, counts, queries, d_attended, pool_k, pool_v, vq_bd, vk_bd, vv_bd, dnum_bd, dden, w_out):
    rows = queries.shape[0]
    pool = pool_k.shape[0]
    keys = cols.shape[0] // counts.shape[0] * BR
    gr = GROUP * BR
    shape = jax.ShapeDtypeStruct
    outs = [
        shape((rows, D), BF),
        shape((rows, D), BF),
        shape((rows, D), BF),
        shape((pool, D), BF),
        shape((pool, D), BF),
        shape((VIRT, D), F32),
        shape((VIRT, D), F32),
        shape((VIRT, D), F32),
    ]
    return pl.pallas_call(
        functools.partial(attend_kernel, nwide, nnarrow),
        out_shape=outs,
        in_specs=[SMEM] * 2 + [VMEM] * 10,
        out_specs=[VMEM] * len(outs),
        scratch_shapes=[
            pltpu.VMEM((pool, D), F32),
            pltpu.VMEM((pool, D), F32),
            pltpu.VMEM((keys, D), BF),
            pltpu.VMEM((keys, D), BF),
            pltpu.VMEM((gr, keys), F32),
            pltpu.VMEM((gr, keys), F32),
            pltpu.VMEM((gr, keys), BF),
            pltpu.VMEM((gr, keys), BF),
            pltpu.VMEM((HM, D), F32),
            pltpu.VMEM((HM, D), F32),
        ],
        compiler_params=pltpu.CompilerParams(vmem_limit_bytes=56 * 1024 * 1024),
        name="attend",
    )(cols, counts, queries, d_attended, pool_k, pool_v, vq_bd, vk_bd, vv_bd, dnum_bd, dden, w_out)


def reduce_kernel(
    nwide,
    nnarrow,
    nodes,
    far,
    part_k,
    part_v,
    dquery,
    attended,
    grad_out,
    w_query,
    w_key,
    w_value,
    vq_part,
    vk_part,
    vv_part,
    local,
    back,
    gathered,
    virt_sums,
    contrib,
    sib_send,
    sib_recv,
    keep,
    x_send,
    x_recv,
    w_send,
    w_recv,
    w_own,
    part,
    one,
    mid,
    two,
    summed,
    small_sems,
    back_send,
    back_recv,
    sib_sems,
    x_sems,
    w_sems,
    gw_sems,
    gx_sems,
    gs_sems,
):
    at = Place(nwide, nnarrow)
    rows = nodes.shape[0]
    halfd = D // 2
    band = halfd // at.nx
    chunk = 4 * band // nwide

    at.barrier()

    for j, ref in enumerate((vq_part, vk_part, vv_part)):
        for lt in range(D // 128):
            tile = ref[:, lt * 128 : (lt + 1) * 128]
            if j == 0:
                part[2 * lt, 0:16] = tile
            elif j == 1:
                part[2 * lt, 16:24] = tile[0:8]
                part[2 * lt + 1, 0:8] = tile[8:16]
            else:
                part[2 * lt + 1, 8:24] = tile
    small = SmallSum(at, part, one, mid, two, summed, small_sems)
    small.first()

    returns = [None]
    for first in range(0, nwide, 4):
        there = slice(first * BR, (first + 4) * BR)
        pooled = slice(rows + first * BR, rows + (first + 4) * BR)
        contrib[there, :] = (
            dot_nt(part_k[pooled, :], w_key[...]) + dot_nt(part_v[pooled, :], w_value[...])
        ).astype(BF)
        for slot in range(max(first, 1), first + 4):
            returns.append(
                push(
                    contrib.at[slot * BR : (slot + 1) * BR],
                    back.at[slot * BR : (slot + 1) * BR],
                    back_send.at[slot],
                    back_recv.at[slot],
                    {"wide": at.behind(slot)},
                )
            )
    back[0:BR, :] = contrib[0:BR, :]

    own_rows = pl.ds(pl.multiple_of(at.c * halfd, halfd), halfd)
    sib_rows = pl.ds(pl.multiple_of((1 - at.c) * halfd, halfd), halfd)
    sibling = {"narrow": at.x * 2 + 1 - at.c}

    def grad_half(g, which):
        if g == 0:
            return dot_tn(attended[:, which], grad_out[...])
        if g == 1:
            return dot_tn(nodes[:, which], dquery[...])
        parts = part_k if g == 2 else part_v
        total = dot_tn(nodes[:, which], parts[0:rows, :])
        for first in range(0, nwide * BR, 1024):
            size = min(1024, nwide * BR - first)
            total = total + dot_tn(
                far[first : first + size, which], parts[rows + first : rows + first + size, :]
            )
        return total

    sib_copies, x_copies = [], []

    def x_stage(g):
        sib_copies[g].wait_recv()
        total = keep[g] + sib_recv[g].astype(F32)
        keep[g] = total
        x_send[g] = total.astype(BF)
        for step in range(1, at.nx):
            peer = (at.x + step) % at.nx
            x_copies.append(
                push(
                    x_send.at[g, pl.ds(pl.multiple_of(peer * band, band), band)],
                    x_recv.at[g, step],
                    x_sems.at[g, 0, step],
                    x_sems.at[g, 1, step],
                    {"narrow": peer * 2 + at.c},
                )
            )

    for g in range(4):
        sib_send[g] = grad_half(g, sib_rows).astype(BF)
        sib_copies.append(
            push(sib_send.at[g], sib_recv.at[g], sib_sems.at[0, g], sib_sems.at[1, g], sibling)
        )
        keep[g] = grad_half(g, own_rows)
        if g > 0:
            x_stage(g - 1)
        if g == 1:
            small.second()
    x_stage(3)
    small.third()

    tile = 256

    @pl.loop(0, rows // tile)
    def _(i):
        here = pl.ds(pl.multiple_of(i * tile, tile), tile)
        local[here, :] = (
            dot_nt(dquery[here, :], w_query[...])
            + dot_nt(part_k[here, :], w_key[...])
            + dot_nt(part_v[here, :], w_value[...])
        )

    mine = pl.ds(pl.multiple_of(at.x * band, band), band)
    for g in range(4):
        total = keep[g, mine]
        for step in range(1, at.nx):
            x_copies[g * (at.nx - 1) + step - 1].wait()
            total = total + x_recv[g, step].astype(F32)
        w_own[g * band : (g + 1) * band, :] = total
        w_send[g * band : (g + 1) * band, :] = total.astype(BF)

    w_copies = []
    for slot in range(1, nwide):
        peer = at.ahead(slot)
        w_copies.append(
            push(
                w_send.at[pl.ds(pl.multiple_of(peer * chunk, chunk), chunk)],
                w_recv.at[slot],
                w_sems.at[0, slot],
                w_sems.at[1, slot],
                {"wide": peer},
            )
        )
    my_chunk = pl.ds(pl.multiple_of(at.w * chunk, chunk), chunk)
    total = w_own[my_chunk, :]
    for slot in range(1, nwide):
        w_copies[slot - 1].wait_recv()
        total = total + w_recv[slot].astype(F32)
    gathered[at.n, my_chunk, :] = total.astype(BF)
    g_copies = []
    for slot in range(1, nwide):
        g_copies.append(
            push(
                gathered.at[at.n, my_chunk],
                gathered.at[at.n, my_chunk],
                gw_sems.at[0, slot],
                gw_sems.at[1, slot],
                {"wide": at.ahead(slot)},
            )
        )
    small.finish()
    virt_sums[...] = summed[...]
    for copy in g_copies:
        copy.wait_recv()
    gx_copies = []
    for step in range(1, at.nx):
        gx_copies.append(
            push(
                gathered.at[at.n],
                gathered.at[at.n],
                gx_sems.at[0, step],
                gx_sems.at[1, step],
                {"narrow": (at.x + step) % at.nx * 2 + at.c},
            )
        )
    gs_copies = [push(gathered.at[at.n], gathered.at[at.n], gs_sems.at[0, 0], gs_sems.at[1, 0], sibling)]
    for step in range(1, at.nx):
        gx_copies[step - 1].wait_recv()
        landed = (at.x + at.nx - step) % at.nx * 2 + at.c
        gs_copies.append(
            push(gathered.at[landed], gathered.at[landed], gs_sems.at[0, step], gs_sems.at[1, step], sibling)
        )
    for copy in gs_copies:
        copy.wait()
    for slot in range(1, nwide):
        returns[slot].wait()
    for copy in gx_copies + g_copies + w_copies + sib_copies:
        copy.wait_send()


def reduce(nwide, nnarrow, *args):
    rows = args[0].shape[0]
    nx = nnarrow // 2
    band = D // 2 // nx
    chunk = 4 * band // nwide
    shape = jax.ShapeDtypeStruct
    outs = [
        shape((rows, D), F32),
        shape((nwide * BR, D), BF),
        shape((nnarrow, 4 * band, D), BF),
        shape((8, 24, 128), F32),
    ]
    sems = pltpu.SemaphoreType.DMA
    return pl.pallas_call(
        functools.partial(reduce_kernel, nwide, nnarrow),
        out_shape=outs,
        in_specs=[VMEM] * len(args),
        out_specs=[VMEM] * len(outs),
        scratch_shapes=[
            pltpu.VMEM((nwide * BR, D), BF),
            pltpu.VMEM((4, D // 2, D), BF),
            pltpu.VMEM((4, D // 2, D), BF),
            pltpu.VMEM((4, D // 2, D), F32),
            pltpu.VMEM((4, D // 2, D), BF),
            pltpu.VMEM((4, nx, band, D), BF),
            pltpu.VMEM((4 * band, D), BF),
            pltpu.VMEM((nwide, chunk, D), BF),
            pltpu.VMEM((4 * band, D), F32),
        ]
        + small_sum_scratch(nwide, nnarrow, 24)
        + [
            sems((nwide,)),
            sems((nwide,)),
            sems((2, 4)),
            sems((4, 2, nx)),
            sems((2, nwide)),
            sems((2, nwide)),
            sems((2, nx)),
            sems((2, nx)),
        ],
        compiler_params=pltpu.CompilerParams(
            collective_id=1, has_side_effects=True, vmem_limit_bytes=56 * 1024 * 1024
        ),
        name="reduce",
    )(*args)


def finish_kernel(
    nwide,
    nnarrow,
    picks,
    local,
    back,
    gathered,
    virt_sums,
    virtual,
    summary_b,
    dzeta_b,
    w_query,
    w_key,
    w_value,
    grad_nodes,
    virtual_grad,
    grad_query,
    grad_key,
    grad_value,
    grad_wout,
):
    at = Place(nwide, nnarrow)
    grad_nodes[...] = local[...]
    for slot in range(nwide):
        place = pl.ds(pl.multiple_of(picks[at.ahead(slot)] * BR, BR), BR)
        grad_nodes[place, :] += back[slot * BR : (slot + 1) * BR, :].astype(F32)
    top = jnp.concatenate([virt_sums[2 * lt] for lt in range(D // 128)], axis=1)
    bottom = jnp.concatenate([virt_sums[2 * lt + 1] for lt in range(D // 128)], axis=1)
    vq_grad = top[0:16].astype(BF)
    vk_grad = jnp.concatenate([top[16:24], bottom[0:8]], axis=0).astype(BF)
    vv_grad = bottom[8:24].astype(BF)
    virtual_grad[...] = (
        dot_nt(vq_grad, w_query[...]) + dot_nt(vk_grad, w_key[...]) + dot_nt(vv_grad, w_value[...])
    )
    band = D // 2 // at.nx
    pairs = (
        (grad_wout, summary_b[...], dzeta_b[...]),
        (grad_query, virtual[...], vq_grad),
        (grad_key, virtual[...], vk_grad),
        (grad_value, virtual[...], vv_grad),
    )
    for g, (out, left, right) in enumerate(pairs):
        out[...] = dot_tn(left, right)
        for n in range(nnarrow):
            first = (n % 2) * (D // 2) + (n // 2) * band
            out[first : first + band, :] += gathered[n, g * band : (g + 1) * band].astype(F32)


def finish(nwide, nnarrow, *args):
    shape = jax.ShapeDtypeStruct
    outs = [shape(args[1].shape, F32), shape((VIRT, D), F32)] + [shape((D, D), F32)] * 4
    return pl.pallas_call(
        functools.partial(finish_kernel, nwide, nnarrow),
        out_shape=outs,
        in_specs=[SMEM] + [VMEM] * (len(args) - 1),
        out_specs=[VMEM] * len(outs),
        compiler_params=pltpu.CompilerParams(vmem_limit_bytes=40 * 1024 * 1024),
        name="finish",
    )(*args)


def shards(
    nwide,
    nnarrow,
    nodes,
    virtual,
    w_query,
    w_key,
    w_value,
    w_out,
    col_blocks,
    col_count,
    send_sel,
    grad_out,
    grad_virtual,
):
    picks = send_sel.reshape(nwide)
    (
        queries,
        pool_k,
        pool_v,
        far,
        d_attended,
        vq_bd,
        vk_bd,
        vv_bd,
        dnum_bd,
        dden,
        out_virtual,
        summary_b,
        dzeta_b,
    ) = exchange(
        nwide, nnarrow, picks, nodes, virtual, w_query, w_key, w_value, w_out, grad_out, grad_virtual
    )
    out_nodes, attended, dquery, part_k, part_v, vq_part, vk_part, vv_part = attend(
        nwide,
        nnarrow,
        col_blocks.reshape(-1),
        col_count,
        queries,
        d_attended,
        pool_k,
        pool_v,
        vq_bd,
        vk_bd,
        vv_bd,
        dnum_bd,
        dden,
        w_out,
    )
    local, back, gathered, virt_sums = reduce(
        nwide,
        nnarrow,
        nodes,
        far,
        part_k,
        part_v,
        dquery,
        attended,
        grad_out,
        w_query,
        w_key,
        w_value,
        vq_part,
        vk_part,
        vv_part,
    )
    grad_nodes, virtual_grad, grad_query, grad_key, grad_value, grad_wout = finish(
        nwide,
        nnarrow,
        picks,
        local,
        back,
        gathered,
        virt_sums,
        virtual,
        summary_b,
        dzeta_b,
        w_query,
        w_key,
        w_value,
    )
    return (
        out_nodes,
        out_virtual,
        grad_nodes,
        virtual_grad,
        grad_query,
        grad_key,
        grad_value,
        grad_wout,
    )


def solution(mesh):
    spread = P(("wide", "narrow"), None)
    in_specs = (
        spread,
        P(),
        P(),
        P(),
        P(),
        P(),
        spread,
        P(("wide", "narrow")),
        P("wide", "narrow", None),
        spread,
        P(),
    )
    out_specs = (spread, P(), spread, P(), P(), P(), P(), P())
    return jax.shard_map(
        functools.partial(shards, mesh.shape["wide"], mesh.shape["narrow"]),
        mesh=mesh,
        in_specs=in_specs,
        out_specs=out_specs,
        check_vma=False,
    )
```

```python
import functools

import jax
import jax.numpy as jnp
from jax import lax
from jax.experimental import pallas as pl
from jax.experimental.pallas import tpu as pltpu
from jax.sharding import PartitionSpec as P

D = 512
HEADS = 8
VIRT = 16
BR = 128
HEAD = D // HEADS
HM = HEADS * VIRT
SCALE = HEAD ** (-0.5)
SOFT_CAP = 5.0
EPSILON = 1e-06
IN_CAP = SCALE / SOFT_CAP
BF = jnp.bfloat16
F32 = jnp.float32
MESH = pl.DeviceIdType.MESH
VMEM = pl.BlockSpec(memory_space=pltpu.VMEM)
SMEM = pl.BlockSpec(memory_space=pltpu.SMEM)
ANY = pl.BlockSpec(memory_space=pl.ANY)
MIB = 1024 * 1024
GROUP = 4


def ring_sizes(nwide):
    ny = 4 if nwide == 16 else 2
    return nwide // ny, ny


def shifts(nwide):
    nz, ny = ring_sizes(nwide)
    every = [(dz, dy) for dz in range(nz) for dy in range(ny)]
    hops = lambda s: min(s[0], nz - s[0]) + min(s[1], ny - s[1])
    return [every[0]] + sorted(every[1:], key=lambda s: -hops(s))


def dot(a, b):
    return lax.dot_general(a, b, (((1,), (0,)), ((), ())), preferred_element_type=F32)


def dot_nt(a, b):
    return lax.dot_general(a, b, (((1,), (1,)), ((), ())), preferred_element_type=F32)


def dot_tn(a, b):
    return lax.dot_general(a, b, (((0,), (0,)), ((), ())), preferred_element_type=F32)


def lanes(shape, axis=1):
    return lax.broadcasted_iota(jnp.int32, shape, axis)


class Place:
    def __init__(self, nwide, nnarrow):
        self.nwide, self.nnarrow = nwide, nnarrow
        self.nz, self.ny = ring_sizes(nwide)
        self.shifts = shifts(nwide)
        self.nx = nnarrow // 2
        self.w = lax.axis_index("wide")
        self.n = lax.axis_index("narrow")
        self.z, self.y = self.w // self.ny, self.w % self.ny
        self.x, self.c = self.n // 2, self.n % 2

    def ahead(self, slot):
        dz, dy = self.shifts[slot]
        return ((self.z + dz) % self.nz) * self.ny + (self.y + dy) % self.ny

    def behind(self, slot):
        dz, dy = self.shifts[slot]
        return ((self.z + self.nz - dz) % self.nz) * self.ny + (self.y + self.ny - dy) % self.ny

    def narrow_at(self, step):
        return (self.n + step) % self.nnarrow

    def greet(self):
        barrier = pltpu.get_barrier_semaphore()
        for slot in range(1, self.nwide):
            pl.semaphore_signal(
                barrier, inc=1, device_id={"wide": self.ahead(slot)}, device_id_type=MESH
            )
        for step in range(1, self.nnarrow):
            pl.semaphore_signal(
                barrier, inc=1, device_id={"narrow": self.narrow_at(step)}, device_id_type=MESH
            )

    def meet(self):
        pl.semaphore_wait(pltpu.get_barrier_semaphore(), self.nwide + self.nnarrow - 2)


def push(src, dst, send, recv, device):
    copy = pltpu.make_async_remote_copy(
        src_ref=src, dst_ref=dst, send_sem=send, recv_sem=recv, device_id=device, device_id_type=MESH
    )
    copy.start()
    return copy


class SmallSum:
    def __init__(self, place, part, one, mid, two, out, sems):
        self.place, self.part, self.one, self.mid, self.two, self.out = place, part, one, mid, two, out
        self.sems = sems
        self.per = part.shape[0] // place.nnarrow

    def first(self):
        at, per = self.place, self.per
        self.copies = []
        for step in range(1, at.nnarrow):
            peer = at.narrow_at(step)
            self.copies.append(
                push(
                    self.part.at[pl.ds(peer * per, per)],
                    self.one.at[at.n],
                    self.sems.at[0, 0, step],
                    self.sems.at[0, 1, step],
                    {"narrow": peer},
                )
            )
        self.one[at.n] = self.part[pl.ds(at.n * per, per)]

    def second(self):
        at = self.place
        for copy in self.copies:
            copy.wait()
        total = self.one[0]
        for j in range(1, at.nnarrow):
            total = total + self.one[j]
        self.mid[...] = total
        self.copies = []
        for slot in range(1, at.nwide):
            self.copies.append(
                push(
                    self.mid,
                    self.two.at[at.w],
                    self.sems.at[1, 0, slot],
                    self.sems.at[1, 1, slot],
                    {"wide": at.ahead(slot)},
                )
            )
        self.two[at.w] = total

    def third(self):
        at, per = self.place, self.per
        for copy in self.copies:
            copy.wait()
        total = self.two[0]
        for j in range(1, at.nwide):
            total = total + self.two[j]
        self.out[pl.ds(at.n * per, per)] = total
        self.copies = []
        for step in range(1, at.nnarrow):
            self.copies.append(
                push(
                    self.out.at[pl.ds(at.n * per, per)],
                    self.out.at[pl.ds(at.n * per, per)],
                    self.sems.at[2, 0, step],
                    self.sems.at[2, 1, step],
                    {"narrow": at.narrow_at(step)},
                )
            )

    def finish(self):
        for copy in self.copies:
            copy.wait()


def small_sum_scratch(nwide, nnarrow, rows):
    per = 8 // nnarrow
    return [
        pltpu.VMEM((8, rows, 128), F32),
        pltpu.VMEM((nnarrow, per, rows, 128), F32),
        pltpu.VMEM((per, rows, 128), F32),
        pltpu.VMEM((nwide, per, rows, 128), F32),
        pltpu.VMEM((8, rows, 128), F32),
        pltpu.SemaphoreType.DMA((3, 2, max(nwide, nnarrow))),
    ]


def block_diagonal(rows16):
    tiled = jnp.concatenate([rows16] * HEADS, axis=0)
    head_row = lanes((HM, D), 0) // VIRT
    head_col = lanes((HM, D), 1) // HEAD
    return jnp.where(head_row == head_col, tiled, jnp.zeros_like(tiled))


def diagonal_rows(full):
    head_col = lanes((VIRT, D), 1) // HEAD
    total = jnp.zeros((VIRT, D), F32)
    for h in range(HEADS):
        total = jnp.where(head_col == h, full[h * VIRT : (h + 1) * VIRT], total)
    return total


def exchange_kernel(
    nwide,
    nnarrow,
    picks,
    nodes_hbm,
    virtual_hbm,
    w_query_hbm,
    w_key_hbm,
    w_value_hbm,
    w_out_hbm,
    grad_out_hbm,
    grad_virtual_hbm,
    queries_hbm,
    pool_k_hbm,
    pool_v_hbm,
    far_hbm,
    d_attended_hbm,
    vq_bd,
    vk_bd,
    vv_bd,
    dnum_bd,
    dden_out,
    out_virtual,
    summary_out,
    dzeta_out,
    nodes,
    virtual,
    w_query,
    w_key,
    w_value,
    w_out,
    grad_out,
    grad_virtual,
    queries,
    pool_k,
    pool_v,
    far,
    d_attended,
    stage,
    part,
    one,
    mid,
    two,
    summed,
    small_sems,
    send_sems,
    recv_sems,
    load_sems,
    store_sems,
):
    at = Place(nwide, nnarrow)
    rows = nodes.shape[0] * BR
    at.greet()
    loads = []
    for src, dst in (
        (nodes_hbm, nodes),
        (w_key_hbm, w_key),
        (w_value_hbm, w_value),
        (virtual_hbm, virtual),
        (w_query_hbm, w_query),
        (grad_out_hbm, grad_out),
        (w_out_hbm, w_out),
        (grad_virtual_hbm, grad_virtual),
    ):
        loads.append(pltpu.make_async_copy(src, dst, load_sems.at[len(loads)]))
        loads[-1].start()
    stores = []

    def store(src, dst):
        stores.append(pltpu.make_async_copy(src, dst, store_sems.at[len(stores)]))
        stores[-1].start()

    loads[0].wait()
    copies = [None] * nwide
    for slot in list(range(1, nwide)) + [0]:
        pick = picks[at.ahead(slot)]
        block = nodes[pick]
        if slot == 0:
            far[0:BR, :] = block
            continue
        stage[slot * BR : (slot + 1) * BR, :] = block
        if slot == 1:
            at.meet()
        copies[slot] = push(
            stage.at[slot * BR : (slot + 1) * BR],
            far.at[slot * BR : (slot + 1) * BR],
            send_sems.at[slot],
            recv_sems.at[slot],
            {"wide": at.ahead(slot)},
        )

    chunk = 256
    for load in loads[1:4]:
        load.wait()

    @pl.loop(0, rows // chunk)
    def _(i):
        here = pl.ds(pl.multiple_of(i * chunk, chunk), chunk)
        block = nodes[pl.ds(i * (chunk // BR), chunk // BR)].reshape(chunk, D)
        pool_k[here, :] = dot(block, w_key[...]).astype(BF)
        pool_v[here, :] = dot(block, w_value[...]).astype(BF)

    store(pool_k.at[0:rows], pool_k_hbm.at[0:rows])
    store(pool_v.at[0:rows], pool_v_hbm.at[0:rows])
    loads[4].wait()
    virt = virtual[...]
    vq_bd[...] = block_diagonal(dot(virt, w_query[...])).astype(BF)
    vk_bd[...] = block_diagonal(dot(virt, w_key[...])).astype(BF)
    vv_bd[...] = block_diagonal(dot(virt, w_value[...])).astype(BF)

    expo = jnp.exp(SOFT_CAP * jnp.tanh(dot_nt(vq_bd[...], pool_k[0:rows, :]) * IN_CAP))
    den = jnp.sum(expo, axis=1, keepdims=True)
    num = dot(expo.astype(BF), pool_v[0:rows, :])
    half = lanes((VIRT, 128)) // HEAD
    for h in range(HEADS):
        mine = slice(h * VIRT, (h + 1) * VIRT)
        pair = num[mine, (h // 2) * 128 : (h // 2 + 1) * 128]
        part[h] = jnp.where(half == h % 2, pair, jnp.broadcast_to(den[mine], (VIRT, 128)))
    small = SmallSum(at, part, one, mid, two, summed, small_sems)
    small.first()
    for load in loads[5:]:
        load.wait()

    @pl.loop(0, rows // chunk)
    def _(i):
        here = pl.ds(pl.multiple_of(i * chunk, chunk), chunk)
        block = nodes[pl.ds(i * (chunk // BR), chunk // BR)].reshape(chunk, D)
        queries[here, :] = dot(block, w_query[...]).astype(BF)
        d_attended[here, :] = dot_nt(grad_out[here, :], w_out[...]).astype(BF)

    store(queries, queries_hbm)
    store(d_attended, d_attended_hbm)
    small.second()

    def project_far(first, count):
        for slot in range(max(first, 1), first + count):
            copies[slot].wait_recv()
        here = slice(first * BR, (first + count) * BR)
        there = slice(rows + first * BR, rows + (first + count) * BR)
        store(far.at[here], far_hbm.at[here])
        landed = far[here, :]
        pool_k[there, :] = dot(landed, w_key[...]).astype(BF)
        store(pool_k.at[there], pool_k_hbm.at[there])
        pool_v[there, :] = dot(landed, w_value[...]).astype(BF)
        store(pool_v.at[there], pool_v_hbm.at[there])

    groups = list(range(0, nwide, 4))
    project_far(groups[0], 4)
    small.third()
    for first in groups[1:-1]:
        project_far(first, 4)
    small.finish()

    low = half == 0
    numbers, denoms = [], []
    for pair in range(HEADS // 2):
        even, odd = summed[2 * pair], summed[2 * pair + 1]
        numbers.append(jnp.where(low, even, odd))
        denoms.append(pltpu.roll(jnp.where(low, odd, even), HEAD, 1))
    vnum = jnp.concatenate(numbers, axis=1)
    vden = jnp.concatenate(denoms, axis=1)
    summary = vnum / vden
    summary_b = summary.astype(BF)
    zeta = dot(summary_b, w_out[...])
    radius = jnp.sqrt(jnp.mean(zeta * zeta, axis=1, keepdims=True) + EPSILON)
    out_virtual[...] = zeta / radius
    gv = grad_virtual[...]
    dzeta = gv / radius - zeta * jnp.sum(gv * zeta, axis=1, keepdims=True) / (
        D * radius * radius * radius
    )
    dzeta_b = dzeta.astype(BF)
    summary_out[...] = summary_b
    dzeta_out[...] = dzeta_b
    dsummary = dot_nt(dzeta_b, w_out[...])
    dnum_bd[...] = block_diagonal((dsummary / vden).astype(BF).astype(F32)).astype(BF)
    along = dsummary * summary
    for h in range(HEADS):
        lane_tile = slice((h // 2) * 128, (h // 2 + 1) * 128)
        mine = jnp.where(half == h % 2, along[:, lane_tile], 0.0)
        down = -jnp.sum(mine, axis=1, keepdims=True)
        den_h = denoms[h // 2][:, (h % 2) * HEAD : (h % 2) * HEAD + 1]
        dden_out[h * VIRT : (h + 1) * VIRT, :] = jnp.broadcast_to(down / den_h, (VIRT, 128))

    if len(groups) > 1:
        project_far(groups[-1], 4)
    for slot in range(1, nwide):
        copies[slot].wait_send()
    for copy in stores:
        copy.wait()


def exchange(nwide, nnarrow, picks, nodes, virtual, w_query, w_key, w_value, w_out, grad_out, grad_virtual):
    rows = nodes.shape[0]
    pool = rows + nwide * BR
    shape = jax.ShapeDtypeStruct
    outs = [
        shape((rows, D), BF),
        shape((pool, D), BF),
        shape((pool, D), BF),
        shape((nwide * BR, D), BF),
        shape((rows, D), BF),
        shape((HM, D), BF),
        shape((HM, D), BF),
        shape((HM, D), BF),
        shape((HM, D), BF),
        shape((HM, 128), F32),
        shape((VIRT, D), F32),
        shape((VIRT, D), BF),
        shape((VIRT, D), BF),
    ]
    ins = [
        nodes.reshape(rows // BR, BR, D),
        virtual,
        w_query,
        w_key,
        w_value,
        w_out,
        grad_out,
        grad_virtual,
    ]
    dma = pltpu.SemaphoreType.DMA
    return pl.pallas_call(
        functools.partial(exchange_kernel, nwide, nnarrow),
        out_shape=outs,
        in_specs=[SMEM] + [ANY] * 8,
        out_specs=[ANY] * 5 + [VMEM] * 8,
        scratch_shapes=[pltpu.VMEM(x.shape, x.dtype) for x in ins]
        + [pltpu.VMEM(x.shape, x.dtype) for x in outs[:5]]
        + [pltpu.VMEM((nwide * BR, D), BF)]
        + small_sum_scratch(nwide, nnarrow, VIRT)
        + [dma((nwide,)), dma((nwide,)), dma((8,)), dma((4 + 3 * (nwide // 4),))],
        compiler_params=pltpu.CompilerParams(
            collective_id=0, has_side_effects=True, vmem_limit_bytes=62 * MIB
        ),
        name="exchange",
    )(picks, *ins)


def attend_kernel(
    nwide,
    nnarrow,
    cols,
    counts,
    slot_of,
    queries,
    d_attended,
    pool_k,
    pool_v,
    vq_bd,
    vk_bd,
    vv_bd,
    dnum_bd,
    dden,
    w_out,
    out_nodes,
    attended,
    dquery,
    part_k,
    part_v,
    vq_part,
    vk_part,
    vv_part,
    sum_k,
    sum_v,
    kcat,
    vcat,
    scores,
    dprob,
    probs,
    dscore,
    acc_vk,
    acc_vv,
):
    at = Place(nwide, nnarrow)
    rows = queries.shape[0]
    blocks = rows // BR
    kmax = kcat.shape[0] // BR
    keys = kmax * BR
    gw = GROUP * HEAD
    gr = GROUP * BR
    chunk = 256

    vq = vq_bd[...]
    dn = dnum_bd[...]
    acc_vk[...] = jnp.zeros_like(acc_vk)
    acc_vv[...] = jnp.zeros_like(acc_vv)
    vq_part[...] = jnp.zeros_like(vq_part)

    @pl.loop(0, rows // chunk)
    def _(i):
        here = pl.ds(pl.multiple_of(i * chunk, chunk), chunk)
        own_k, own_v = pool_k[here, :], pool_v[here, :]
        bend = jnp.tanh(dot_nt(vq, own_k) * IN_CAP)
        expo = jnp.exp(SOFT_CAP * bend)
        dexpo = dot_nt(dn, own_v) + dden[:, 0:1]
        ds = (expo * dexpo * (1.0 - bend * bend)).astype(BF)
        vq_part[...] += diagonal_rows(dot(ds, own_k)) * SCALE
        sum_k[here, :] = dot_tn(ds, vq)
        sum_v[here, :] = dot_tn(expo.astype(BF), dn)

    sum_k[rows:, :] = jnp.zeros((nwide * BR, D), F32)
    sum_v[rows:, :] = jnp.zeros((nwide * BR, D), F32)

    lane_head = lanes((BR, HM)) // VIRT
    group_head = lanes((BR, gw)) // HEAD
    half = lanes((BR, 128)) // HEAD

    def stacked(block):
        zero = jnp.zeros_like(block)
        return jnp.concatenate([jnp.where(group_head == h, block, zero) for h in range(GROUP)], axis=0)

    def gathered(full):
        total = full[0:BR]
        for h in range(1, GROUP):
            total = jnp.where(group_head == h, full[h * BR : (h + 1) * BR], total)
        return total

    def block(b, carry):
        here = pl.ds(pl.multiple_of(b * BR, BR), BR)
        count = counts[b]
        places = []
        for t in range(kmax):
            entry = cols[b * kmax + t]
            source = jnp.maximum(entry - blocks, 0)
            dz = (at.z + at.nz - source // at.ny) % at.nz
            dy = (at.y + at.ny - source % at.ny) % at.ny
            entry = jnp.where(entry < blocks, entry, blocks + slot_of[dz * at.ny + dy])
            place = pl.ds(pl.multiple_of(entry * BR, BR), BR)
            places.append(place)
            kcat[t * BR : (t + 1) * BR, :] = pool_k[place, :]
            vcat[t * BR : (t + 1) * BR, :] = pool_v[place, :]
        live = [None, None] + [jnp.where(t < count, 1.0, 0.0).astype(F32) for t in range(2, kmax)]
        q = queries[here, :]
        da = d_attended[here, :]
        bend_v = jnp.tanh(dot_nt(q, vk_bd[...]) * IN_CAP)
        expo_v = jnp.exp(SOFT_CAP * bend_v)
        dprob_v = dot_nt(da, vv_bd[...])
        probs_v = jnp.zeros((BR, HM), F32)
        delta_v = jnp.zeros((BR, HM), F32)
        for g in range(HEADS // GROUP):
            wide = slice(g * gw, (g + 1) * gw)
            qm = stacked(q[:, wide])
            dam = stacked(da[:, wide])
            scores[...] = dot_nt(qm, kcat[:, wide])
            dprob[...] = dot_nt(dam, vcat[:, wide])
            step = 32
            for h in range(GROUP):
                head = g * GROUP + h
                virt_sum = jnp.sum(jnp.where(lane_head == head, expo_v, 0.0), axis=1, keepdims=True)
                inverses = []
                for r in range(0, BR, step):
                    at_rows = slice(h * BR + r, h * BR + r + step)
                    bends, expos = [], []
                    total = None
                    for t in range(kmax):
                        bend = jnp.tanh(scores[at_rows, t * BR : (t + 1) * BR] * IN_CAP)
                        expo = jnp.exp(SOFT_CAP * bend)
                        if live[t] is not None:
                            expo = expo * live[t]
                        bends.append(bend)
                        expos.append(expo)
                        total = expo if total is None else total + expo
                    inverse = 1.0 / (jnp.sum(total, axis=1, keepdims=True) + virt_sum[r : r + step])
                    inverses.append(inverse)
                    for t in range(kmax):
                        at_lanes = slice(t * BR, (t + 1) * BR)
                        weight = expos[t] * inverse
                        probs[at_rows, at_lanes] = weight.astype(BF)
                        scores[at_rows, at_lanes] = weight * (1.0 - bends[t] * bends[t])
                probs_v = jnp.where(lane_head == head, expo_v * jnp.concatenate(inverses, axis=0), probs_v)
            pv = probs_v.astype(BF)
            mixed = gathered(dot(probs[...], vcat[:, wide])) + dot(pv, vv_bd[:, wide])
            mixed_b = mixed.astype(BF)
            attended[here, wide] = mixed_b
            along = da[:, wide].astype(F32) * mixed_b.astype(F32)
            for h in range(GROUP):
                head = g * GROUP + h
                lane_tile = slice((h // 2) * 128, (h // 2 + 1) * 128)
                delta = jnp.sum(jnp.where(half == h % 2, along[:, lane_tile], 0.0), axis=1, keepdims=True)
                delta_v = jnp.where(lane_head == head, delta, delta_v)
                for r in range(0, BR, step):
                    at_rows = slice(h * BR + r, h * BR + r + step)
                    dscore[at_rows, :] = (
                        scores[at_rows, :] * (dprob[at_rows, :] - delta[r : r + step])
                    ).astype(BF)
            dk = dot_tn(dscore[...], qm)
            dv = dot_tn(probs[...], dam)
            for t in range(kmax):
                sum_k[places[t], wide] += dk[t * BR : (t + 1) * BR]
                sum_v[places[t], wide] += dv[t * BR : (t + 1) * BR]
            ds_v = (probs_v * (dprob_v - delta_v) * (1.0 - bend_v * bend_v)).astype(BF)
            dq = gathered(dot(dscore[...], kcat[:, wide])) + dot(ds_v, vk_bd[:, wide])
            dquery[here, wide] = (dq * SCALE).astype(BF)
        acc_vk[...] += dot_tn(ds_v, q)
        acc_vv[...] += dot_tn(pv, da)
        out_nodes[here, :] = dot(attended[here, :], w_out[...]).astype(BF)
        return carry

    lax.fori_loop(0, blocks, block, 0)

    @pl.loop(0, sum_k.shape[0] // chunk)
    def _(i):
        here = pl.ds(pl.multiple_of(i * chunk, chunk), chunk)
        part_k[here, :] = (sum_k[here, :] * SCALE).astype(BF)
        part_v[here, :] = sum_v[here, :].astype(BF)

    vk_part[...] = diagonal_rows(acc_vk[...]) * SCALE
    vv_part[...] = diagonal_rows(acc_vv[...])


def attend(nwide, nnarrow, cols, counts, queries, d_attended, pool_k, pool_v, vq_bd, vk_bd, vv_bd, dnum_bd, dden, w_out):
    rows = queries.shape[0]
    pool = pool_k.shape[0]
    nz, ny = ring_sizes(nwide)
    order = shifts(nwide)
    slot_of = jnp.asarray([order.index((i // ny, i % ny)) for i in range(nwide)], jnp.int32)
    keys = cols.shape[0] // counts.shape[0] * BR
    gr = GROUP * BR
    shape = jax.ShapeDtypeStruct
    outs = [
        shape((rows, D), BF),
        shape((rows, D), BF),
        shape((rows, D), BF),
        shape((pool, D), BF),
        shape((pool, D), BF),
        shape((VIRT, D), F32),
        shape((VIRT, D), F32),
        shape((VIRT, D), F32),
    ]
    return pl.pallas_call(
        functools.partial(attend_kernel, nwide, nnarrow),
        out_shape=outs,
        in_specs=[SMEM] * 3 + [VMEM] * 10,
        out_specs=[VMEM] * len(outs),
        scratch_shapes=[
            pltpu.VMEM((pool, D), F32),
            pltpu.VMEM((pool, D), F32),
            pltpu.VMEM((keys, D), BF),
            pltpu.VMEM((keys, D), BF),
            pltpu.VMEM((gr, keys), F32),
            pltpu.VMEM((gr, keys), F32),
            pltpu.VMEM((gr, keys), BF),
            pltpu.VMEM((gr, keys), BF),
            pltpu.VMEM((HM, D), F32),
            pltpu.VMEM((HM, D), F32),
        ],
        compiler_params=pltpu.CompilerParams(vmem_limit_bytes=62 * MIB),
        name="attend",
    )(cols, counts, slot_of, queries, d_attended, pool_k, pool_v, vq_bd, vk_bd, vv_bd, dnum_bd, dden, w_out)


def reduce_kernel(
    nwide,
    nnarrow,
    nodes_hbm,
    far_hbm,
    part_k_hbm,
    part_v_hbm,
    dquery_hbm,
    attended_hbm,
    grad_out_hbm,
    w_query_hbm,
    w_key_hbm,
    w_value_hbm,
    vq_part,
    vk_part,
    vv_part,
    local_hbm,
    back_hbm,
    lower_hbm,
    upper_hbm,
    virt_sums,
    nodes,
    far,
    part_k,
    part_v,
    dquery,
    attended,
    grad_out,
    w_query,
    w_key,
    w_value,
    local,
    back,
    lower,
    upper,
    contrib,
    sib_send,
    sib_recv,
    keep,
    x_send,
    x_recv,
    w_send,
    w_recv,
    w_own,
    part,
    one,
    mid,
    two,
    summed,
    small_sems,
    back_send,
    back_recv,
    sib_sems,
    x_sems,
    w_sems,
    low_sems,
    up_sems,
    sib_low_sems,
    sib_up_sems,
    load_sems,
    store_sems,
):
    at = Place(nwide, nnarrow)
    rows = nodes.shape[0]
    halfd = D // 2
    band = halfd // at.nx
    chunk = 4 * band // nwide
    at.greet()

    loads = {}

    def load(name, src, dst):
        loads[name] = pltpu.make_async_copy(src, dst, load_sems.at[len(loads)])
        loads[name].start()

    pooled = slice(rows, rows + nwide * BR)
    owned = slice(0, rows)
    load("w_key", w_key_hbm, w_key)
    load("far_k", part_k_hbm.at[pooled], part_k.at[pooled])
    load("w_value", w_value_hbm, w_value)
    load("far_v", part_v_hbm.at[pooled], part_v.at[pooled])
    load("attended", attended_hbm, attended)
    load("grad_out", grad_out_hbm, grad_out)
    load("nodes", nodes_hbm, nodes)
    load("dquery", dquery_hbm, dquery)
    load("far", far_hbm, far)
    load("own_k", part_k_hbm.at[owned], part_k.at[owned])
    load("own_v", part_v_hbm.at[owned], part_v.at[owned])
    load("w_query", w_query_hbm, w_query)
    stores = []

    def store(src, dst):
        stores.append(pltpu.make_async_copy(src, dst, store_sems.at[len(stores)]))
        stores[-1].start()

    for j, ref in enumerate((vq_part, vk_part, vv_part)):
        for lt in range(D // 128):
            tile = ref[:, lt * 128 : (lt + 1) * 128]
            if j == 0:
                part[2 * lt, 0:16] = tile
            elif j == 1:
                part[2 * lt, 16:24] = tile[0:8]
                part[2 * lt + 1, 0:8] = tile[8:16]
            else:
                part[2 * lt + 1, 8:24] = tile
    small = SmallSum(at, part, one, mid, two, summed, small_sems)
    for name in ("w_key", "far_k", "w_value", "far_v"):
        loads[name].wait()
    at.meet()

    returns = [None]
    for first in range(0, nwide, 4):
        there = slice(first * BR, (first + 4) * BR)
        pooled = slice(rows + first * BR, rows + (first + 4) * BR)
        contrib[there, :] = (
            dot_nt(part_k[pooled, :], w_key[...]) + dot_nt(part_v[pooled, :], w_value[...])
        ).astype(BF)
        for slot in range(max(first, 1), first + 4):
            returns.append(
                push(
                    contrib.at[slot * BR : (slot + 1) * BR],
                    back.at[slot * BR : (slot + 1) * BR],
                    back_send.at[slot],
                    back_recv.at[slot],
                    {"wide": at.behind(slot)},
                )
            )
        if first == 0:
            small.first()
    back[0:BR, :] = contrib[0:BR, :]
    store(back.at[0:BR], back_hbm.at[0:BR])

    own_rows = pl.ds(pl.multiple_of(at.c * halfd, halfd), halfd)
    sib_rows = pl.ds(pl.multiple_of((1 - at.c) * halfd, halfd), halfd)
    sibling = {"narrow": at.x * 2 + 1 - at.c}
    needs = (("attended", "grad_out"), ("nodes", "dquery"), ("far", "own_k"), ("own_v",))
    x_steps = sorted(range(1, at.nx), key=lambda step: -min(step, at.nx - step))

    def grad_half(g, which):
        if g == 0:
            return dot_tn(attended[:, which], grad_out[...])
        if g == 1:
            return dot_tn(nodes[:, which], dquery[...])
        parts = part_k if g == 2 else part_v
        total = dot_tn(nodes[:, which], parts[0:rows, :])
        for first in range(0, nwide * BR, 1024):
            size = min(1024, nwide * BR - first)
            total = total + dot_tn(
                far[first : first + size, which], parts[rows + first : rows + first + size, :]
            )
        return total

    sib_copies, x_copies = [], {}

    def x_stage(g):
        sib_copies[g].wait_recv()
        total = keep[g] + sib_recv[g].astype(F32)
        keep[g] = total
        x_send[g] = total.astype(BF)
        for step in x_steps:
            peer = (at.x + step) % at.nx
            x_copies[g, step] = push(
                x_send.at[g, pl.ds(pl.multiple_of(peer * band, band), band)],
                x_recv.at[g, step],
                x_sems.at[g, 0, step],
                x_sems.at[g, 1, step],
                {"narrow": peer * 2 + at.c},
            )

    for g in range(4):
        for name in needs[g]:
            loads[name].wait()
        sib_send[g] = grad_half(g, sib_rows).astype(BF)
        sib_copies.append(
            push(sib_send.at[g], sib_recv.at[g], sib_sems.at[0, g], sib_sems.at[1, g], sibling)
        )
        keep[g] = grad_half(g, own_rows)
        if g > 0:
            x_stage(g - 1)
        if g == 1:
            small.second()
    x_stage(3)

    tile = 256
    loads["w_query"].wait()

    @pl.loop(0, rows // tile)
    def _(i):
        here = pl.ds(pl.multiple_of(i * tile, tile), tile)
        local[here, :] = (
            dot_nt(dquery[here, :], w_query[...])
            + dot_nt(part_k[here, :], w_key[...])
            + dot_nt(part_v[here, :], w_value[...])
        )

    store(local, local_hbm)
    small.third()

    mine = pl.ds(pl.multiple_of(at.x * band, band), band)
    for g in range(4):
        total = keep[g, mine]
        for step in x_steps:
            x_copies[g, step].wait()
            total = total + x_recv[g, step].astype(F32)
        w_own[g * band : (g + 1) * band, :] = total
        w_send[g * band : (g + 1) * band, :] = total.astype(BF)

    w_copies = []
    for slot in range(1, nwide):
        peer = at.ahead(slot)
        w_copies.append(
            push(
                w_send.at[pl.ds(pl.multiple_of(peer * chunk, chunk), chunk)],
                w_recv.at[slot],
                w_sems.at[0, slot],
                w_sems.at[1, slot],
                {"wide": peer},
            )
        )
    total = w_own[pl.ds(pl.multiple_of(at.w * chunk, chunk), chunk), :]
    for slot in range(1, nwide):
        w_copies[slot - 1].wait_recv()
        total = total + w_recv[slot].astype(F32)
    done = total.astype(BF)
    lower[at.n, at.w] = done[:, 0:halfd]
    upper[at.c, at.w, at.x] = done[:, halfd:]
    up_first, low_first = [], []
    for step in x_steps:
        up_first.append(
            push(
                upper.at[at.c, at.w, at.x],
                upper.at[at.c, at.w, at.x],
                up_sems.at[0, 0, step],
                up_sems.at[0, 1, step],
                {"narrow": (at.x + step) % at.nx * 2 + at.c},
            )
        )
    for slot in range(1, nwide):
        low_first.append(
            push(
                lower.at[at.n, at.w],
                lower.at[at.n, at.w],
                low_sems.at[0, 0, slot],
                low_sems.at[0, 1, slot],
                {"wide": at.ahead(slot)},
            )
        )
    small.finish()
    virt_sums[...] = summed[...]
    for copy in up_first:
        copy.wait_recv()
    up_second, low_second, across = [], {}, []
    for slot in range(1, nwide):
        up_second.append(
            push(
                upper.at[at.c, at.w],
                upper.at[at.c, at.w],
                up_sems.at[1, 0, slot],
                up_sems.at[1, 1, slot],
                {"wide": at.ahead(slot)},
            )
        )
    for copy in low_first:
        copy.wait_recv()
    for step in x_steps:
        low_second[step] = push(
            lower.at[at.n],
            lower.at[at.n],
            low_sems.at[1, 0, step],
            low_sems.at[1, 1, step],
            {"narrow": (at.x + step) % at.nx * 2 + at.c},
        )

    def low_across(landed, step):
        across.append(
            push(lower.at[landed], lower.at[landed], sib_low_sems.at[0, step], sib_low_sems.at[1, step], sibling)
        )

    def up_across(slot):
        landed = at.behind(slot)
        across.append(
            push(
                upper.at[at.c, landed],
                upper.at[at.c, landed],
                sib_up_sems.at[0, slot],
                sib_up_sems.at[1, slot],
                sibling,
            )
        )

    low_across(at.n, 0)
    up_across(0)
    for slot in range(1, nwide):
        returns[slot].wait_recv()
        store(back.at[slot * BR : (slot + 1) * BR], back_hbm.at[slot * BR : (slot + 1) * BR])
    for slot in range(1, nwide):
        up_second[slot - 1].wait_recv()
        up_across(slot)
    for step in x_steps:
        low_second[step].wait_recv()
        low_across((at.x + at.nx - step) % at.nx * 2 + at.c, step)
    for copy in across:
        copy.wait()
    store(lower, lower_hbm)
    store(upper, upper_hbm)
    for copy in returns[1:] + w_copies + sib_copies + up_first + low_first:
        copy.wait_send()
    for copy in up_second + list(low_second.values()):
        copy.wait_send()
    for copy in stores:
        copy.wait()


def reduce(nwide, nnarrow, *args):
    rows = args[0].shape[0]
    nx = nnarrow // 2
    band = D // 2 // nx
    chunk = 4 * band // nwide
    shape = jax.ShapeDtypeStruct
    outs = [
        shape((rows, D), F32),
        shape((nwide * BR, D), BF),
        shape((nnarrow, nwide, chunk, D // 2), BF),
        shape((2, nwide, nx, chunk, D // 2), BF),
        shape((8, 24, 128), F32),
    ]
    sems = pltpu.SemaphoreType.DMA
    return pl.pallas_call(
        functools.partial(reduce_kernel, nwide, nnarrow),
        out_shape=outs,
        in_specs=[ANY] * 10 + [VMEM] * 3,
        out_specs=[ANY] * 4 + [VMEM],
        scratch_shapes=[pltpu.VMEM(x.shape, x.dtype) for x in args[:10]]
        + [pltpu.VMEM(x.shape, x.dtype) for x in outs[:4]]
        + [
            pltpu.VMEM((nwide * BR, D), BF),
            pltpu.VMEM((4, D // 2, D), BF),
            pltpu.VMEM((4, D // 2, D), BF),
            pltpu.VMEM((4, D // 2, D), F32),
            pltpu.VMEM((4, D // 2, D), BF),
            pltpu.VMEM((4, nx, band, D), BF),
            pltpu.VMEM((4 * band, D), BF),
            pltpu.VMEM((nwide, chunk, D), BF),
            pltpu.VMEM((4 * band, D), F32),
        ]
        + small_sum_scratch(nwide, nnarrow, 24)
        + [
            sems((nwide,)),
            sems((nwide,)),
            sems((2, 4)),
            sems((4, 2, nx)),
            sems((2, nwide)),
            sems((2, 2, nwide)),
            sems((2, 2, nwide)),
            sems((2, nx)),
            sems((2, nwide)),
            sems((12,)),
            sems((nwide + 3,)),
        ],
        compiler_params=pltpu.CompilerParams(
            collective_id=1, has_side_effects=True, vmem_limit_bytes=62 * MIB
        ),
        name="reduce",
    )(*args)


def finish_kernel(
    nwide,
    nnarrow,
    picks,
    local,
    back,
    lower,
    upper,
    virt_sums,
    virtual,
    summary_b,
    dzeta_b,
    w_query,
    w_key,
    w_value,
    grad_nodes,
    virtual_grad,
    grad_query,
    grad_key,
    grad_value,
    grad_wout,
):
    at = Place(nwide, nnarrow)
    grad_nodes[...] = local[...]
    for slot in range(nwide):
        place = pl.ds(pl.multiple_of(picks[at.ahead(slot)] * BR, BR), BR)
        grad_nodes[place, :] += back[slot * BR : (slot + 1) * BR, :].astype(F32)
    top = jnp.concatenate([virt_sums[2 * lt] for lt in range(D // 128)], axis=1)
    bottom = jnp.concatenate([virt_sums[2 * lt + 1] for lt in range(D // 128)], axis=1)
    vq_grad = top[0:16].astype(BF)
    vk_grad = jnp.concatenate([top[16:24], bottom[0:8]], axis=0).astype(BF)
    vv_grad = bottom[8:24].astype(BF)
    virtual_grad[...] = (
        dot_nt(vq_grad, w_query[...]) + dot_nt(vk_grad, w_key[...]) + dot_nt(vv_grad, w_value[...])
    )
    halfd = D // 2
    band = halfd // at.nx
    chunk = 4 * band // nwide
    pairs = (
        (grad_wout, summary_b[...], dzeta_b[...]),
        (grad_query, virtual[...], vq_grad),
        (grad_key, virtual[...], vk_grad),
        (grad_value, virtual[...], vv_grad),
    )
    per = nwide // 4
    for g, (out, left, right) in enumerate(pairs):
        out[...] = dot_tn(left, right)
        for n in range(nnarrow):
            first = (n % 2) * halfd + (n // 2) * band
            for j in range(per):
                here = slice(first + j * chunk, first + (j + 1) * chunk)
                out[here, 0:halfd] += lower[n, g * per + j].astype(F32)
                out[here, halfd:] += upper[n % 2, g * per + j, n // 2].astype(F32)


def finish(nwide, nnarrow, *args):
    shape = jax.ShapeDtypeStruct
    outs = [shape(args[1].shape, F32), shape((VIRT, D), F32)] + [shape((D, D), F32)] * 4
    return pl.pallas_call(
        functools.partial(finish_kernel, nwide, nnarrow),
        out_shape=outs,
        in_specs=[SMEM] + [VMEM] * (len(args) - 1),
        out_specs=[VMEM] * len(outs),
        compiler_params=pltpu.CompilerParams(vmem_limit_bytes=62 * MIB),
        name="finish",
    )(*args)


def shards(
    nwide,
    nnarrow,
    nodes,
    virtual,
    w_query,
    w_key,
    w_value,
    w_out,
    col_blocks,
    col_count,
    send_sel,
    grad_out,
    grad_virtual,
):
    picks = send_sel.reshape(nwide)
    (
        queries,
        pool_k,
        pool_v,
        far,
        d_attended,
        vq_bd,
        vk_bd,
        vv_bd,
        dnum_bd,
        dden,
        out_virtual,
        summary_b,
        dzeta_b,
    ) = exchange(
        nwide, nnarrow, picks, nodes, virtual, w_query, w_key, w_value, w_out, grad_out, grad_virtual
    )
    out_nodes, attended, dquery, part_k, part_v, vq_part, vk_part, vv_part = attend(
        nwide,
        nnarrow,
        col_blocks.reshape(-1),
        col_count,
        queries,
        d_attended,
        pool_k,
        pool_v,
        vq_bd,
        vk_bd,
        vv_bd,
        dnum_bd,
        dden,
        w_out,
    )
    local, back, lower, upper, virt_sums = reduce(
        nwide,
        nnarrow,
        nodes,
        far,
        part_k,
        part_v,
        dquery,
        attended,
        grad_out,
        w_query,
        w_key,
        w_value,
        vq_part,
        vk_part,
        vv_part,
    )
    grad_nodes, virtual_grad, grad_query, grad_key, grad_value, grad_wout = finish(
        nwide,
        nnarrow,
        picks,
        local,
        back,
        lower,
        upper,
        virt_sums,
        virtual,
        summary_b,
        dzeta_b,
        w_query,
        w_key,
        w_value,
    )
    return (
        out_nodes,
        out_virtual,
        grad_nodes,
        virtual_grad,
        grad_query,
        grad_key,
        grad_value,
        grad_wout,
    )


def solution(mesh):
    spread = P(("wide", "narrow"), None)
    in_specs = (
        spread,
        P(),
        P(),
        P(),
        P(),
        P(),
        spread,
        P(("wide", "narrow")),
        P("wide", "narrow", None),
        spread,
        P(),
    )
    out_specs = (spread, P(), spread, P(), P(), P(), P(), P())
    return jax.shard_map(
        functools.partial(shards, mesh.shape["wide"], mesh.shape["narrow"]),
        mesh=mesh,
        in_specs=in_specs,
        out_specs=out_specs,
        check_vma=False,
    )
```

```python
import functools
import types

import jax
import jax.numpy as jnp
from jax import lax
from jax.experimental import pallas as pl
from jax.experimental.pallas import tpu as pltpu
from jax.sharding import PartitionSpec as P

D = 512
HEADS = 8
VIRT = 16
BR = 128
HEAD = D // HEADS
HM = HEADS * VIRT
SCALE = HEAD ** (-0.5)
SOFT_CAP = 5.0
EPSILON = 1e-06
IN_CAP = SCALE / SOFT_CAP
BF = jnp.bfloat16
F32 = jnp.float32
MESH = pl.DeviceIdType.MESH
VMEM = pl.BlockSpec(memory_space=pltpu.VMEM)
SMEM = pl.BlockSpec(memory_space=pltpu.SMEM)
ANY = pl.BlockSpec(memory_space=pl.ANY)
VMEM_LIMIT = 62 * 1024 * 1024
GROUP = 4


def ring_sizes(nwide):
    ny = 4 if nwide == 16 else 2
    return nwide // ny, ny


def shifts(nwide):
    nz, ny = ring_sizes(nwide)
    every = [(dz, dy) for dz in range(nz) for dy in range(ny)]
    hops = lambda s: min(s[0], nz - s[0]) + min(s[1], ny - s[1])
    return sorted(every[1:], key=lambda s: -hops(s)) + every[:1]


def dot(a, b):
    return lax.dot_general(a, b, (((1,), (0,)), ((), ())), preferred_element_type=F32)


def dot_nt(a, b):
    return lax.dot_general(a, b, (((1,), (1,)), ((), ())), preferred_element_type=F32)


def dot_tn(a, b):
    return lax.dot_general(a, b, (((0,), (0,)), ((), ())), preferred_element_type=F32)


def lanes(shape, axis=1):
    return lax.broadcasted_iota(jnp.int32, shape, axis)


class Place:
    def __init__(self, nwide, nnarrow):
        self.nwide, self.nnarrow = nwide, nnarrow
        self.nz, self.ny = ring_sizes(nwide)
        self.shifts = shifts(nwide)
        self.nx = nnarrow // 2
        self.w = lax.axis_index("wide")
        self.n = lax.axis_index("narrow")
        self.z, self.y = self.w // self.ny, self.w % self.ny
        self.x, self.c = self.n // 2, self.n % 2

    def ahead(self, slot):
        dz, dy = self.shifts[slot]
        return ((self.z + dz) % self.nz) * self.ny + (self.y + dy) % self.ny

    def behind(self, slot):
        dz, dy = self.shifts[slot]
        return ((self.z + self.nz - dz) % self.nz) * self.ny + (self.y + self.ny - dy) % self.ny

    def narrow_at(self, step):
        return (self.n + step) % self.nnarrow

    def greet(self):
        barrier = pltpu.get_barrier_semaphore()
        for slot in range(self.nwide - 1):
            pl.semaphore_signal(
                barrier, inc=1, device_id={"wide": self.ahead(slot)}, device_id_type=MESH
            )
        for step in range(1, self.nnarrow):
            pl.semaphore_signal(
                barrier, inc=1, device_id={"narrow": self.narrow_at(step)}, device_id_type=MESH
            )

    def meet(self):
        pl.semaphore_wait(pltpu.get_barrier_semaphore(), self.nwide + self.nnarrow - 2)


def push(src, dst, send, recv, device):
    copy = pltpu.make_async_remote_copy(
        src_ref=src, dst_ref=dst, send_sem=send, recv_sem=recv, device_id=device, device_id_type=MESH
    )
    copy.start()
    return copy


KMAX = 4
PAIRS = 32
ORDER, JOINS, PLACE, LIVE, END, HAS, PICK, TABLE = 0, 32, 64, 96, 128, 160, 192, 256


def tables_kernel(nwide, nnarrow, cols, counts, send_sel, slot_of, table, tally, following):
    at = Place(nwide, nnarrow)
    blocks, kmax = cols.shape
    dead = nwide + blocks

    def clear(i, carry):
        tally[i] = 0
        return carry

    lax.fori_loop(0, dead + 1, clear, 0)

    def enter(i, carry):
        b, t = i // kmax, i % kmax
        entry = cols[b, t]
        source = jnp.maximum(entry - blocks, 0)
        dz = (at.z + at.nz - source // at.ny) % at.nz
        dy = (at.y + at.ny - source % at.ny) % at.ny
        place = jnp.where(entry < blocks, nwide + entry, slot_of[dz * at.ny + dy])
        live = t < counts[b]
        table[PLACE + i] = place
        table[LIVE + i] = jnp.where(live, 1, 0)
        key = jnp.where(live, place, dead)
        tally[key] = tally[key] + 1
        return carry

    lax.fori_loop(0, blocks * kmax, enter, 0)

    def begin(p, start):
        number = tally[p]
        following[p] = start
        table[END + p] = jnp.maximum(start + number - 1, 0)
        table[HAS + p] = jnp.where(number > 0, 1, 0)
        tally[p] = start
        return start + number

    lax.fori_loop(0, dead + 1, begin, 0)

    def sort(i, carry):
        key = jnp.where(table[LIVE + i] > 0, table[PLACE + i], dead)
        position = following[key]
        following[key] = position + 1
        table[ORDER + position] = i
        table[JOINS + position] = jnp.where(position > tally[key], 1, 0)
        return carry

    lax.fori_loop(0, blocks * kmax, sort, 0)
    for slot in range(nwide):
        table[PICK + slot] = send_sel[0, 0, at.ahead(slot)]


def tables(nwide, nnarrow, cols, counts, send_sel):
    order = shifts(nwide)
    nz, ny = ring_sizes(nwide)
    slot_of = jnp.asarray([order.index((i // ny, i % ny)) for i in range(nwide)], jnp.int32)
    return pl.pallas_call(
        functools.partial(tables_kernel, nwide, nnarrow),
        out_shape=jax.ShapeDtypeStruct((TABLE,), jnp.int32),
        in_specs=[SMEM] * 4,
        out_specs=SMEM,
        scratch_shapes=[pltpu.SMEM((32,), jnp.int32), pltpu.SMEM((32,), jnp.int32)],
        name="tables",
    )(cols, counts, send_sel, slot_of)


class SmallSum:
    def __init__(self, place, part, one, mid, two, out, sems):
        self.place, self.part, self.one, self.mid, self.two, self.out = place, part, one, mid, two, out
        self.sems = sems
        self.per = part.shape[0] // place.nnarrow

    def first(self):
        at, per = self.place, self.per
        self.copies = []
        for step in range(1, at.nnarrow):
            peer = at.narrow_at(step)
            self.copies.append(
                push(
                    self.part.at[pl.ds(peer * per, per)],
                    self.one.at[at.n],
                    self.sems.at[0, 0, step],
                    self.sems.at[0, 1, step],
                    {"narrow": peer},
                )
            )
        self.one[at.n] = self.part[pl.ds(at.n * per, per)]

    def second(self):
        at = self.place
        for copy in self.copies:
            copy.wait()
        total = self.one[0]
        for j in range(1, at.nnarrow):
            total = total + self.one[j]
        self.mid[...] = total
        self.copies = []
        for slot in range(at.nwide - 1):
            self.copies.append(
                push(
                    self.mid,
                    self.two.at[at.w],
                    self.sems.at[1, 0, slot],
                    self.sems.at[1, 1, slot],
                    {"wide": at.ahead(slot)},
                )
            )
        self.two[at.w] = total

    def third(self):
        at, per = self.place, self.per
        for copy in self.copies:
            copy.wait()
        total = self.two[0]
        for j in range(1, at.nwide):
            total = total + self.two[j]
        self.out[pl.ds(at.n * per, per)] = total
        self.copies = []
        for step in range(1, at.nnarrow):
            self.copies.append(
                push(
                    self.out.at[pl.ds(at.n * per, per)],
                    self.out.at[pl.ds(at.n * per, per)],
                    self.sems.at[2, 0, step],
                    self.sems.at[2, 1, step],
                    {"narrow": at.narrow_at(step)},
                )
            )

    def finish(self):
        for copy in self.copies:
            copy.wait()


def block_diagonal(rows16):
    tiled = jnp.concatenate([rows16] * HEADS, axis=0)
    head_row = lanes((HM, D), 0) // VIRT
    head_col = lanes((HM, D), 1) // HEAD
    return jnp.where(head_row == head_col, tiled, jnp.zeros_like(tiled))


def diagonal_rows(full):
    head_col = lanes((VIRT, D), 1) // HEAD
    total = jnp.zeros((VIRT, D), F32)
    for h in range(HEADS):
        total = jnp.where(head_col == h, full[h * VIRT : (h + 1) * VIRT], total)
    return total


class Copies:
    def __init__(self, sems):
        self.sems, self.started = sems, []

    def start(self, src, dst):
        copy = pltpu.make_async_copy(src, dst, self.sems.at[len(self.started)])
        copy.start()
        self.started.append(copy)
        return copy


def sum_refs(at, r, name):
    return SmallSum(at, *[getattr(r, name + key) for key in ("part", "one", "mid", "two", "summed", "sems")])


def stacked(block):
    group_head = lanes(block.shape) // HEAD
    zero = jnp.zeros_like(block)
    return jnp.concatenate([jnp.where(group_head == h, block, zero) for h in range(GROUP)], axis=0)


def unstacked(full):
    rows = full.shape[0] // GROUP
    group_head = lanes((rows, full.shape[1])) // HEAD
    total = full[0:rows]
    for h in range(1, GROUP):
        total = jnp.where(group_head == h, full[h * rows : (h + 1) * rows], total)
    return total


def flat(value):
    return value.reshape(value.shape[0] * value.shape[1], value.shape[2])


def exchange_phase(at, r, loads):
    nwide = at.nwide
    blocks = r.nodes.shape[0]
    rows = blocks * BR
    loads["nodes"].wait()
    copies = []
    for slot in range(nwide):
        block = r.nodes[r.table[PICK + slot]]
        if slot == nwide - 1:
            r.far[slot] = block
            continue
        r.stage[slot] = block
        if slot == 0:
            at.meet()
        copies.append(
            push(
                r.stage.at[slot],
                r.far.at[slot],
                r.send_sems.at[slot],
                r.recv_sems.at[slot],
                {"wide": at.ahead(slot)},
            )
        )
    for name in ("w_key", "w_value"):
        loads[name].wait()
    pair = 2

    @pl.loop(0, blocks // pair)
    def _(i):
        here = pl.ds(i * pair, pair)
        there = pl.ds(nwide + i * pair, pair)
        block = flat(r.nodes[here])
        r.pool_k[there] = dot(block, r.w_key[...]).astype(BF).reshape(pair, BR, D)
        r.pool_v[there] = dot(block, r.w_value[...]).astype(BF).reshape(pair, BR, D)

    for name in ("virtual", "w_query"):
        loads[name].wait()
    virt = r.virtual[...]
    r.vq_bd[...] = block_diagonal(dot(virt, r.w_query[...])).astype(BF)
    r.vk_bd[...] = block_diagonal(dot(virt, r.w_key[...])).astype(BF)
    r.vv_bd[...] = block_diagonal(dot(virt, r.w_value[...])).astype(BF)

    expo = jnp.exp(SOFT_CAP * jnp.tanh(dot_nt(r.vq_bd[...], flat(r.pool_k[nwide:])) * IN_CAP))
    den = jnp.sum(expo, axis=1, keepdims=True)
    num = dot(expo.astype(BF), flat(r.pool_v[nwide:]))
    half = lanes((VIRT, 128)) // HEAD
    for h in range(HEADS):
        mine = slice(h * VIRT, (h + 1) * VIRT)
        two = num[mine, (h // 2) * 128 : (h // 2 + 1) * 128]
        r.f_part[h] = jnp.where(half == h % 2, two, jnp.broadcast_to(den[mine], (VIRT, 128)))
    small = sum_refs(at, r, "f_")
    small.first()
    for name in ("grad_out", "w_out", "grad_virtual"):
        loads[name].wait()

    @pl.loop(0, blocks // pair)
    def _(i):
        here = pl.ds(i * pair, pair)
        out_rows = pl.ds(pl.multiple_of(i * pair * BR, pair * BR), pair * BR)
        r.queries[here] = dot(flat(r.nodes[here]), r.w_query[...]).astype(BF).reshape(pair, BR, D)
        da = dot_nt(r.grad_out[out_rows, :], r.w_out[...])
        r.d_attended[here] = da.astype(BF).reshape(pair, BR, D)

    small.second()

    def project_far(first):
        here = slice(first, first + 4)
        for slot in range(first, min(first + 4, nwide - 1)):
            copies[slot].wait_recv()
        landed = flat(r.far[here])
        r.pool_k[here] = dot(landed, r.w_key[...]).astype(BF).reshape(4, BR, D)
        r.pool_v[here] = dot(landed, r.w_value[...]).astype(BF).reshape(4, BR, D)

    groups = list(range(0, nwide, 4))
    project_far(groups[0])
    small.third()
    for first in groups[1:-1]:
        project_far(first)
    small.finish()

    low = half == 0
    numbers, denoms = [], []
    for j in range(HEADS // 2):
        even, odd = r.f_summed[2 * j], r.f_summed[2 * j + 1]
        numbers.append(jnp.where(low, even, odd))
        denoms.append(pltpu.roll(jnp.where(low, odd, even), HEAD, 1))
    vnum = jnp.concatenate(numbers, axis=1)
    vden = jnp.concatenate(denoms, axis=1)
    summary = vnum / vden
    summary_b = summary.astype(BF)
    zeta = dot(summary_b, r.w_out[...])
    radius = jnp.sqrt(jnp.mean(zeta * zeta, axis=1, keepdims=True) + EPSILON)
    r.out_virtual[...] = zeta / radius
    gv = r.grad_virtual[...]
    dzeta = gv / radius - zeta * jnp.sum(gv * zeta, axis=1, keepdims=True) / (
        D * radius * radius * radius
    )
    dzeta_b = dzeta.astype(BF)
    r.summary_out[...] = summary_b
    r.dzeta_out[...] = dzeta_b
    dsummary = dot_nt(dzeta_b, r.w_out[...])
    r.dnum_bd[...] = block_diagonal((dsummary / vden).astype(BF).astype(F32)).astype(BF)
    along = dsummary * summary
    for h in range(HEADS):
        lane_tile = slice((h // 2) * 128, (h // 2 + 1) * 128)
        mine = jnp.where(half == h % 2, along[:, lane_tile], 0.0)
        down = -jnp.sum(mine, axis=1, keepdims=True)
        den_h = denoms[h // 2][:, (h % 2) * HEAD : (h % 2) * HEAD + 1]
        r.dden[h * VIRT : (h + 1) * VIRT, :] = jnp.broadcast_to(down / den_h, (VIRT, 128))

    r.vq_part[...] = jnp.zeros_like(r.vq_part)
    vq, dn = r.vq_bd[...], r.dnum_bd[...]

    @pl.loop(0, blocks // pair)
    def _(i):
        here = pl.ds(i * pair, pair)
        there = pl.ds(nwide + i * pair, pair)
        own_k, own_v = flat(r.pool_k[there]), flat(r.pool_v[there])
        bend = jnp.tanh(dot_nt(vq, own_k) * IN_CAP)
        expo = jnp.exp(SOFT_CAP * bend)
        dexpo = dot_nt(dn, own_v) + r.dden[:, 0:1]
        ds = (expo * dexpo * (1.0 - bend * bend)).astype(BF)
        r.vq_part[...] += diagonal_rows(dot(ds, own_k)) * SCALE
        r.base_k[here] = dot_tn(ds, vq).reshape(pair, BR, D)
        r.base_v[here] = dot_tn(expo.astype(BF), dn).reshape(pair, BR, D)

    r.base_k[blocks] = jnp.zeros((BR, D), F32)
    r.base_v[blocks] = jnp.zeros((BR, D), F32)
    if len(groups) > 1:
        project_far(groups[-1])
    for copy in copies:
        copy.wait_send()


def attend_phase(at, r):
    blocks = r.nodes.shape[0]
    gw = GROUP * HEAD
    step = 32
    r.acc_vk[...] = jnp.zeros_like(r.acc_vk)
    r.acc_vv[...] = jnp.zeros_like(r.acc_vv)
    lane_head = lanes((BR, HM)) // VIRT
    half = lanes((BR, 128)) // HEAD

    def block(b, carry):
        live = [None, None]
        for t in range(KMAX):
            place = r.table[PLACE + b * KMAX + t]
            r.kcat[t * BR : (t + 1) * BR, :] = r.pool_k[place]
            r.vcat[t * BR : (t + 1) * BR, :] = r.pool_v[place]
            if t >= 2:
                live.append(r.table[LIVE + b * KMAX + t].astype(F32))
        q = r.queries[b]
        da = r.d_attended[b]
        bend_v = jnp.tanh(dot_nt(q, r.vk_bd[...]) * IN_CAP)
        expo_v = jnp.exp(SOFT_CAP * bend_v)
        dprob_v = dot_nt(da, r.vv_bd[...])
        probs_v = jnp.zeros((BR, HM), F32)
        delta_v = jnp.zeros((BR, HM), F32)
        for g in range(HEADS // GROUP):
            wide = slice(g * gw, (g + 1) * gw)
            at_tile = [(b * KMAX + t) * 2 + g for t in range(KMAX)]
            r.scores[...] = dot_nt(stacked(q[:, wide]), r.kcat[:, wide])
            r.dprob[...] = dot_nt(stacked(da[:, wide]), r.vcat[:, wide])
            for h in range(GROUP):
                head = g * GROUP + h
                virt_sum = jnp.sum(jnp.where(lane_head == head, expo_v, 0.0), axis=1, keepdims=True)
                inverses = []
                for first in range(0, BR, step):
                    here = slice(h * BR + first, h * BR + first + step)
                    bends, expos = [], []
                    total = None
                    for t in range(KMAX):
                        bend = jnp.tanh(r.scores[here, t * BR : (t + 1) * BR] * IN_CAP)
                        expo = jnp.exp(SOFT_CAP * bend)
                        if live[t] is not None:
                            expo = expo * live[t]
                        bends.append(bend)
                        expos.append(expo)
                        total = expo if total is None else total + expo
                    total = jnp.sum(total, axis=1, keepdims=True) + virt_sum[first : first + step]
                    inverse = 1.0 / total
                    inverses.append(inverse)
                    for t in range(KMAX):
                        weight = expos[t] * inverse
                        r.probs[at_tile[t], here, :] = weight.astype(BF)
                        r.scores[here, t * BR : (t + 1) * BR] = weight * (1.0 - bends[t] * bends[t])
                probs_v = jnp.where(lane_head == head, expo_v * jnp.concatenate(inverses, axis=0), probs_v)
            pv = probs_v.astype(BF)
            probs = jnp.concatenate([r.probs[i] for i in at_tile], axis=1)
            mixed = unstacked(dot(probs, r.vcat[:, wide])) + dot(pv, r.vv_bd[:, wide])
            mixed_b = mixed.astype(BF)
            r.attended[b, :, wide] = mixed_b
            along = da[:, wide].astype(F32) * mixed_b.astype(F32)
            for h in range(GROUP):
                head = g * GROUP + h
                lane_tile = slice((h // 2) * 128, (h // 2 + 1) * 128)
                delta = jnp.sum(jnp.where(half == h % 2, along[:, lane_tile], 0.0), axis=1, keepdims=True)
                delta_v = jnp.where(lane_head == head, delta, delta_v)
                for first in range(0, BR, step):
                    here = slice(h * BR + first, h * BR + first + step)
                    for t in range(KMAX):
                        at_lanes = slice(t * BR, (t + 1) * BR)
                        r.dscore[at_tile[t], here, :] = (
                            r.scores[here, at_lanes] * (r.dprob[here, at_lanes] - delta[first : first + step])
                        ).astype(BF)
            ds_v = (probs_v * (dprob_v - delta_v) * (1.0 - bend_v * bend_v)).astype(BF)
            dscore = jnp.concatenate([r.dscore[i] for i in at_tile], axis=1)
            dq = unstacked(dot(dscore, r.kcat[:, wide])) + dot(ds_v, r.vk_bd[:, wide])
            r.dquery[b, :, wide] = (dq * SCALE).astype(BF)
        r.acc_vk[...] += dot_tn(ds_v, q)
        r.acc_vv[...] += dot_tn(pv, da)
        return carry

    lax.fori_loop(0, blocks, block, 0)
    r.vk_part[...] = diagonal_rows(r.acc_vk[...]) * SCALE
    r.vv_part[...] = diagonal_rows(r.acc_vv[...])
    r.sum_k[...] = jnp.zeros_like(r.sum_k)
    r.sum_v[...] = jnp.zeros_like(r.sum_v)


def reduce_phase(at, r, loads, stores):
    nwide = at.nwide
    blocks = r.nodes.shape[0]
    rows = blocks * BR
    halfd = D // 2
    band = halfd // at.nx
    chunk = 4 * band // nwide
    gw = GROUP * HEAD

    for j, ref in enumerate((r.vq_part, r.vk_part, r.vv_part)):
        for lt in range(D // 128):
            tile = ref[:, lt * 128 : (lt + 1) * 128]
            if j == 0:
                r.b_part[2 * lt, 0:16] = tile
            elif j == 1:
                r.b_part[2 * lt, 16:24] = tile[0:8]
                r.b_part[2 * lt + 1, 0:8] = tile[8:16]
            else:
                r.b_part[2 * lt + 1, 8:24] = tile
    small = sum_refs(at, r, "b_")
    small.first()

    def entry(position, carry):
        i = r.table[ORDER + position]
        joins = r.table[JOINS + position].astype(F32)
        base = jnp.where(r.table[PLACE + i] >= nwide, r.table[PLACE + i] - nwide, blocks)
        q, da = r.queries[i // KMAX], r.d_attended[i // KMAX]
        base_k, base_v = r.base_k[base], r.base_v[base]
        for g in range(HEADS // GROUP):
            wide = slice(g * gw, (g + 1) * gw)
            dk = dot_tn(r.dscore[i * 2 + g], stacked(q[:, wide]))
            dv = dot_tn(r.probs[i * 2 + g], stacked(da[:, wide]))
            total_k = joins * r.sum_k[:, wide] + (1.0 - joins) * base_k[:, wide] + dk
            total_v = joins * r.sum_v[:, wide] + (1.0 - joins) * base_v[:, wide] + dv
            r.sum_k[:, wide] = total_k
            r.sum_v[:, wide] = total_v
            r.run_k[position, :, wide] = (total_k * SCALE).astype(BF)
            r.run_v[position, :, wide] = total_v.astype(BF)
        return carry

    slack = blocks * KMAX - blocks - nwide
    returns = []
    reached = 0
    for first in range(0, nwide, 4):
        until = slack + first + 4
        lax.fori_loop(reached, until, entry, 0)
        reached = until
        for place in range(first, first + 4):
            end = r.table[END + place]
            r.pool_k[place] = r.run_k[end]
            r.pool_v[place] = r.run_v[end]
        here = slice(first, first + 4)
        part = dot_nt(flat(r.pool_k[here]), r.w_key[...]) + dot_nt(flat(r.pool_v[here]), r.w_value[...])
        r.stage[here] = part.astype(BF).reshape(4, BR, D)
        for slot in range(first, min(first + 4, nwide - 1)):
            returns.append(
                push(
                    r.stage.at[slot],
                    r.back.at[slot],
                    r.back_sems.at[0, slot],
                    r.back_sems.at[1, slot],
                    {"wide": at.behind(slot)},
                )
            )
        if first == 0:
            small.second()
    stores.start(r.stage.at[nwide - 1], r.back_hbm.at[nwide - 1])
    lax.fori_loop(reached, blocks * KMAX, entry, 0)
    for own in range(blocks):
        end = r.table[END + nwide + own]
        has = r.table[HAS + nwide + own] > 0
        r.pool_k[nwide + own] = jnp.where(has, r.run_k[end], (r.base_k[own] * SCALE).astype(BF))
        r.pool_v[nwide + own] = jnp.where(has, r.run_v[end], r.base_v[own].astype(BF))

    own_rows = pl.ds(pl.multiple_of(at.c * halfd, halfd), halfd)
    sib_rows = pl.ds(pl.multiple_of((1 - at.c) * halfd, halfd), halfd)
    sibling = {"narrow": at.x * 2 + 1 - at.c}
    x_steps = sorted(range(1, at.nx), key=lambda step: -min(step, at.nx - step))
    per = halfd // BR

    def grad_half(g, which):
        if g == 0:
            return dot_tn(flat(r.attended[:, :, which]), r.grad_out[...])
        if g == 1:
            return dot_tn(flat(r.nodes[:, :, which]), flat(r.dquery[...]))
        parts = r.pool_k if g == 2 else r.pool_v
        total = dot_tn(flat(r.nodes[:, :, which]), flat(parts[nwide:]))
        for first in range(0, nwide, 8):
            here = slice(first, min(first + 8, nwide))
            total = total + dot_tn(flat(r.far[here, :, which]), flat(parts[here]))
        return total

    sib_copies, x_copies = [], {}

    def x_stage(g):
        sib_copies[g].wait_recv()
        mine = slice(per * g, per * g + per)
        total = r.base_k[mine] + r.sib_recv[mine].astype(F32)
        r.base_k[mine] = total
        r.run_v[mine] = total.astype(BF)
        for step in x_steps:
            peer = (at.x + step) % at.nx
            spot = peer * band
            x_copies[g, step] = push(
                r.run_v.at[per * g + spot // BR, pl.ds(pl.multiple_of(spot % BR, band), band)],
                r.x_recv.at[g, step],
                r.x_sems.at[g, 0, step],
                r.x_sems.at[g, 1, step],
                {"narrow": peer * 2 + at.c},
            )

    for g in range(4):
        mine = slice(per * g, per * g + per)
        r.run_k[mine] = grad_half(g, sib_rows).astype(BF).reshape(per, BR, D)
        sib_copies.append(
            push(
                r.run_k.at[mine],
                r.sib_recv.at[mine],
                r.sib_sems.at[0, g],
                r.sib_sems.at[1, g],
                sibling,
            )
        )
        r.base_k[mine] = grad_half(g, own_rows).reshape(per, BR, D)
        if g > 0:
            x_stage(g - 1)
    x_stage(3)
    small.third()
    pair = 2

    @pl.loop(0, blocks // pair)
    def _(i):
        here = pl.ds(i * pair, pair)
        there = pl.ds(nwide + i * pair, pair)
        total = (
            dot_nt(flat(r.dquery[here]), r.w_query[...])
            + dot_nt(flat(r.pool_k[there]), r.w_key[...])
            + dot_nt(flat(r.pool_v[there]), r.w_value[...])
        )
        r.base_v[here] = total.reshape(pair, BR, D)

    stores.start(r.base_v.at[0:blocks], r.local_hbm)

    spot = at.x * band
    for g in range(4):
        total = r.base_k[per * g + spot // BR, pl.ds(pl.multiple_of(spot % BR, band), band)]
        for step in x_steps:
            x_copies[g, step].wait()
            total = total + r.x_recv[g, step].astype(F32)
        r.w_own[g * band : (g + 1) * band, :] = total
        r.w_send[g * band : (g + 1) * band, :] = total.astype(BF)

    w_copies = []
    for slot in range(nwide - 1):
        peer = at.ahead(slot)
        w_copies.append(
            push(
                r.w_send.at[pl.ds(pl.multiple_of(peer * chunk, chunk), chunk)],
                r.w_recv.at[slot],
                r.w_sems.at[0, slot],
                r.w_sems.at[1, slot],
                {"wide": peer},
            )
        )

    @pl.loop(0, blocks // pair)
    def _(i):
        here = pl.ds(i * pair, pair)
        out = dot(flat(r.attended[here]), r.w_out[...])
        r.attended[here] = out.astype(BF).reshape(pair, BR, D)

    stores.start(r.attended, r.out_nodes_hbm)

    total = r.w_own[pl.ds(pl.multiple_of(at.w * chunk, chunk), chunk), :]
    for slot in range(nwide - 1):
        w_copies[slot].wait_recv()
        total = total + r.w_recv[slot].astype(F32)
    done = total.astype(BF)
    r.lower[at.n, at.w] = done[:, 0:halfd]
    r.upper[at.c, at.w, at.x] = done[:, halfd:]
    up_first, low_first = [], []
    for step in x_steps:
        up_first.append(
            push(
                r.upper.at[at.c, at.w, at.x],
                r.upper.at[at.c, at.w, at.x],
                r.up_sems.at[0, 0, step],
                r.up_sems.at[0, 1, step],
                {"narrow": (at.x + step) % at.nx * 2 + at.c},
            )
        )
    for slot in range(nwide - 1):
        low_first.append(
            push(
                r.lower.at[at.n, at.w],
                r.lower.at[at.n, at.w],
                r.low_sems.at[0, 0, slot],
                r.low_sems.at[0, 1, slot],
                {"wide": at.ahead(slot)},
            )
        )
    small.finish()
    r.virt_sums[...] = r.b_summed[...]
    for copy in up_first:
        copy.wait_recv()
    up_second, low_second, across = [], {}, []
    for slot in range(nwide - 1):
        up_second.append(
            push(
                r.upper.at[at.c, at.w],
                r.upper.at[at.c, at.w],
                r.up_sems.at[1, 0, slot],
                r.up_sems.at[1, 1, slot],
                {"wide": at.ahead(slot)},
            )
        )
    for copy in low_first:
        copy.wait_recv()
    for step in x_steps:
        low_second[step] = push(
            r.lower.at[at.n],
            r.lower.at[at.n],
            r.low_sems.at[1, 0, step],
            r.low_sems.at[1, 1, step],
            {"narrow": (at.x + step) % at.nx * 2 + at.c},
        )

    def low_across(landed, step):
        across.append(
            push(
                r.lower.at[landed],
                r.lower.at[landed],
                r.across_sems.at[0, 0, step],
                r.across_sems.at[0, 1, step],
                sibling,
            )
        )

    def up_across(slot):
        landed = at.behind(slot)
        across.append(
            push(
                r.upper.at[at.c, landed],
                r.upper.at[at.c, landed],
                r.across_sems.at[1, 0, slot],
                r.across_sems.at[1, 1, slot],
                sibling,
            )
        )

    low_across(at.n, 0)
    up_across(nwide - 1)
    for slot in range(nwide - 1):
        returns[slot].wait_recv()
        stores.start(r.back.at[slot], r.back_hbm.at[slot])
    for slot in range(nwide - 1):
        up_second[slot].wait_recv()
        up_across(slot)
    for step in x_steps:
        low_second[step].wait_recv()
        low_across((at.x + at.nx - step) % at.nx * 2 + at.c, step)
    for copy in across:
        copy.wait()
    stores.start(r.lower, r.lower_hbm)
    stores.start(r.upper, r.upper_hbm)
    for copy in returns + w_copies + sib_copies + up_first + low_first + up_second:
        copy.wait_send()
    for copy in low_second.values():
        copy.wait_send()


LOADED = ("nodes", "w_key", "w_value", "virtual", "w_query", "grad_out", "w_out", "grad_virtual")


def layer_kernel(nwide, nnarrow, names, *refs):
    r = types.SimpleNamespace(**dict(zip(names, refs, strict=True)))
    at = Place(nwide, nnarrow)
    at.greet()
    started = Copies(r.load_sems)
    loads = {name: started.start(getattr(r, name + "_hbm"), getattr(r, name)) for name in LOADED}
    stores = Copies(r.store_sems)
    exchange_phase(at, r, loads)
    attend_phase(at, r)
    reduce_phase(at, r, loads, stores)
    for copy in stores.started:
        copy.wait()


def layer(nwide, nnarrow, table, arrays):
    blocks = arrays["nodes"].shape[0]
    rows = blocks * BR
    pool = blocks + nwide
    entries = blocks * KMAX
    nx = nnarrow // 2
    band = D // 2 // nx
    chunk = 4 * band // nwide
    per = 8 // nnarrow
    sems = pltpu.SemaphoreType.DMA
    most = max(nwide, nnarrow)
    shape = jax.ShapeDtypeStruct
    outs = {
        "out_nodes_hbm": shape((blocks, BR, D), BF),
        "local_hbm": shape((blocks, BR, D), F32),
        "back_hbm": shape((nwide, BR, D), BF),
        "lower_hbm": shape((nnarrow, nwide, chunk, D // 2), BF),
        "upper_hbm": shape((2, nwide, nx, chunk, D // 2), BF),
        "virt_sums": shape((8, 24, 128), F32),
        "out_virtual": shape((VIRT, D), F32),
        "summary_out": shape((VIRT, D), BF),
        "dzeta_out": shape((VIRT, D), BF),
    }
    vmem = {name: (arrays[name].shape, arrays[name].dtype) for name in LOADED}
    vmem |= {
        "stage": ((nwide, BR, D), BF),
        "far": ((nwide, BR, D), BF),
        "queries": ((blocks, BR, D), BF),
        "d_attended": ((blocks, BR, D), BF),
        "attended": ((blocks, BR, D), BF),
        "dquery": ((blocks, BR, D), BF),
        "pool_k": ((pool, BR, D), BF),
        "pool_v": ((pool, BR, D), BF),
        "vq_bd": ((HM, D), BF),
        "vk_bd": ((HM, D), BF),
        "vv_bd": ((HM, D), BF),
        "dnum_bd": ((HM, D), BF),
        "dden": ((HM, 128), F32),
        "vq_part": ((VIRT, D), F32),
        "vk_part": ((VIRT, D), F32),
        "vv_part": ((VIRT, D), F32),
        "acc_vk": ((HM, D), F32),
        "acc_vv": ((HM, D), F32),
        "base_k": ((max(blocks, 8) + 1, BR, D), F32),
        "base_v": ((max(blocks, 8) + 1, BR, D), F32),
        "kcat": ((KMAX * BR, D), BF),
        "vcat": ((KMAX * BR, D), BF),
        "scores": ((GROUP * BR, KMAX * BR), F32),
        "dprob": ((GROUP * BR, KMAX * BR), F32),
        "probs": ((entries * 2, GROUP * BR, BR), BF),
        "dscore": ((entries * 2, GROUP * BR, BR), BF),
        "sum_k": ((BR, D), F32),
        "sum_v": ((BR, D), F32),
        "run_k": ((entries, BR, D), BF),
        "run_v": ((entries, BR, D), BF),
        "back": ((nwide, BR, D), BF),
        "sib_recv": ((4 * (D // 2 // BR), BR, D), BF),
        "x_recv": ((4, nx, band, D), BF),
        "w_send": ((4 * band, D), BF),
        "w_recv": ((nwide, chunk, D), BF),
        "w_own": ((4 * band, D), F32),
        "lower": (outs["lower_hbm"].shape, BF),
        "upper": (outs["upper_hbm"].shape, BF),
    }
    for name, height in (("f_", VIRT), ("b_", 24)):
        vmem |= {
            name + "part": ((8, height, 128), F32),
            name + "one": ((nnarrow, per, height, 128), F32),
            name + "mid": ((per, height, 128), F32),
            name + "two": ((nwide, per, height, 128), F32),
            name + "summed": ((8, height, 128), F32),
        }
    sem_shapes = {
        "f_sems": (3, 2, most),
        "b_sems": (3, 2, most),
        "send_sems": (nwide,),
        "recv_sems": (nwide,),
        "back_sems": (2, nwide),
        "sib_sems": (2, 4),
        "x_sems": (4, 2, nx),
        "w_sems": (2, nwide),
        "low_sems": (2, 2, nwide),
        "up_sems": (2, 2, nwide),
        "across_sems": (2, 2, nwide),
        "load_sems": (len(LOADED),),
        "store_sems": (nwide + 4,),
    }
    names = (
        ["table"] + [name + "_hbm" for name in LOADED] + list(outs) + list(vmem) + list(sem_shapes)
    )
    results = pl.pallas_call(
        functools.partial(layer_kernel, nwide, nnarrow, names),
        out_shape=list(outs.values()),
        in_specs=[SMEM] + [ANY] * len(LOADED),
        out_specs=[ANY] * 5 + [VMEM] * 4,
        scratch_shapes=[pltpu.VMEM(*kind) for kind in vmem.values()]
        + [sems(kind) for kind in sem_shapes.values()],
        compiler_params=pltpu.CompilerParams(
            collective_id=0, has_side_effects=True, vmem_limit_bytes=VMEM_LIMIT
        ),
        name="layer",
    )(table, *[arrays[name] for name in LOADED])
    return dict(zip(outs, results))


def finish_kernel(
    nwide,
    nnarrow,
    table,
    local_hbm,
    back_hbm,
    lower_hbm,
    upper_hbm,
    out_nodes_in,
    virt_sums,
    virtual,
    summary_b,
    dzeta_b,
    out_virtual_in,
    w_query_hbm,
    w_key_hbm,
    w_value_hbm,
    out_nodes,
    grad_nodes_hbm,
    grad_query_hbm,
    grad_key_hbm,
    grad_value_hbm,
    grad_wout_hbm,
    out_virtual,
    virtual_grad,
    lower,
    upper,
    back,
    grad_nodes,
    grads,
    w_query,
    w_key,
    w_value,
    out_rows,
    load_sems,
    store_sems,
):
    at = Place(nwide, nnarrow)
    started, stores = Copies(load_sems), Copies(store_sems)
    load_low = started.start(lower_hbm, lower)
    load_up = started.start(upper_hbm, upper)
    load_back = started.start(back_hbm, back)
    load_local = started.start(local_hbm, grad_nodes)
    load_w = [
        started.start(src, dst)
        for src, dst in ((w_query_hbm, w_query), (w_key_hbm, w_key), (w_value_hbm, w_value))
    ]
    load_out = started.start(out_nodes_in, out_rows)
    out_virtual[...] = out_virtual_in[...]
    top = jnp.concatenate([virt_sums[2 * lt] for lt in range(D // 128)], axis=1)
    bottom = jnp.concatenate([virt_sums[2 * lt + 1] for lt in range(D // 128)], axis=1)
    vq_grad = top[0:16].astype(BF)
    vk_grad = jnp.concatenate([top[16:24], bottom[0:8]], axis=0).astype(BF)
    vv_grad = bottom[8:24].astype(BF)
    halfd = D // 2
    band = halfd // at.nx
    chunk = 4 * band // nwide
    pairs = (
        (grad_wout_hbm, summary_b[...], dzeta_b[...]),
        (grad_query_hbm, virtual[...], vq_grad),
        (grad_key_hbm, virtual[...], vk_grad),
        (grad_value_hbm, virtual[...], vv_grad),
    )
    per = nwide // 4
    load_low.wait()
    load_up.wait()
    for g, (out, left, right) in enumerate(pairs):
        grads[g] = dot_tn(left, right)
        for n in range(nnarrow):
            first = (n % 2) * halfd + (n // 2) * band
            for j in range(per):
                here = slice(first + j * chunk, first + (j + 1) * chunk)
                grads[g, here, 0:halfd] += lower[n, g * per + j].astype(F32)
                grads[g, here, halfd:] += upper[n % 2, g * per + j, n // 2].astype(F32)
        stores.start(grads.at[g], out)
    load_out.wait()
    stores.start(out_rows, out_nodes)
    load_back.wait()
    load_local.wait()
    for slot in range(nwide):
        grad_nodes[table[PICK + slot]] += back[slot].astype(F32)
    stores.start(grad_nodes, grad_nodes_hbm)
    for copy in load_w:
        copy.wait()
    virtual_grad[...] = (
        dot_nt(vq_grad, w_query[...]) + dot_nt(vk_grad, w_key[...]) + dot_nt(vv_grad, w_value[...])
    )
    for copy in stores.started:
        copy.wait()


def finish(nwide, nnarrow, table, got, arrays):
    shape = jax.ShapeDtypeStruct
    outs = (
        [shape(got["out_nodes_hbm"].shape, BF), shape(got["local_hbm"].shape, F32)]
        + [shape((D, D), F32)] * 4
        + [shape((VIRT, D), F32)] * 2
    )
    scratch = [(got[name].shape, got[name].dtype) for name in ("lower_hbm", "upper_hbm", "back_hbm", "local_hbm")]
    scratch += [((4, D, D), F32)] + [((D, D), BF)] * 3
    scratch += [(got["out_nodes_hbm"].shape, BF)]
    return pl.pallas_call(
        functools.partial(finish_kernel, nwide, nnarrow),
        out_shape=outs,
        in_specs=[SMEM] + [ANY] * 5 + [VMEM] * 5 + [ANY] * 3,
        out_specs=[ANY] * 6 + [VMEM] * 2,
        scratch_shapes=[pltpu.VMEM(*kind) for kind in scratch]
        + [pltpu.SemaphoreType.DMA((8,)), pltpu.SemaphoreType.DMA((6,))],
        compiler_params=pltpu.CompilerParams(vmem_limit_bytes=VMEM_LIMIT),
        name="finish",
    )(
        table,
        *[got[name] for name in ("local_hbm", "back_hbm", "lower_hbm", "upper_hbm", "out_nodes_hbm", "virt_sums")],
        arrays["virtual"],
        *[got[name] for name in ("summary_out", "dzeta_out", "out_virtual")],
        arrays["w_query"],
        arrays["w_key"],
        arrays["w_value"],
    )


def shards(
    nwide,
    nnarrow,
    nodes,
    virtual,
    w_query,
    w_key,
    w_value,
    w_out,
    col_blocks,
    col_count,
    send_sel,
    grad_out,
    grad_virtual,
):
    rows = nodes.shape[0]
    arrays = {
        "nodes": nodes.reshape(rows // BR, BR, D),
        "w_key": w_key,
        "w_value": w_value,
        "virtual": virtual,
        "w_query": w_query,
        "grad_out": grad_out,
        "w_out": w_out,
        "grad_virtual": grad_virtual,
    }
    table = tables(nwide, nnarrow, col_blocks, col_count, send_sel)
    got = layer(nwide, nnarrow, table, arrays)
    out_nodes, grad_nodes, grad_query, grad_key, grad_value, grad_wout, out_virtual, virtual_grad = finish(
        nwide, nnarrow, table, got, arrays
    )
    return (
        out_nodes.reshape(rows, D),
        out_virtual,
        grad_nodes.reshape(rows, D),
        virtual_grad,
        grad_query,
        grad_key,
        grad_value,
        grad_wout,
    )


def solution(mesh):
    spread = P(("wide", "narrow"), None)
    in_specs = (
        spread,
        P(),
        P(),
        P(),
        P(),
        P(),
        spread,
        P(("wide", "narrow")),
        P("wide", "narrow", None),
        spread,
        P(),
    )
    out_specs = (spread, P(), spread, P(), P(), P(), P(), P())
    return jax.shard_map(
        functools.partial(shards, mesh.shape["wide"], mesh.shape["narrow"]),
        mesh=mesh,
        in_specs=in_specs,
        out_specs=out_specs,
        check_vma=False,
    )
```

```python
import functools
import math
import types

import jax
import jax.numpy as jnp
from jax import lax
from jax.experimental import pallas as pl
from jax.experimental.pallas import tpu as pltpu
from jax.sharding import PartitionSpec as P

D = 512
HEADS = 8
VIRT = 16
BR = 128
HEAD = D // HEADS
HM = HEADS * VIRT
SCALE = HEAD ** (-0.5)
SOFT_CAP = 5.0
EPSILON = 1e-06
IN_CAP = SCALE / SOFT_CAP
EXP_CAP = SOFT_CAP * math.log2(math.e)
BF = jnp.bfloat16
F32 = jnp.float32
MESH = pl.DeviceIdType.MESH
VMEM = pl.BlockSpec(memory_space=pltpu.VMEM)
SMEM = pl.BlockSpec(memory_space=pltpu.SMEM)
ANY = pl.BlockSpec(memory_space=pl.ANY)
VMEM_LIMIT = 63 * 1024 * 1024
GROUP = 4


def ring_sizes(nwide):
    ny = 4 if nwide == 16 else 2
    return nwide // ny, ny


def shifts(nwide):
    nz, ny = ring_sizes(nwide)
    every = [(dz, dy) for dz in range(nz) for dy in range(ny)]
    hops = lambda s: min(s[0], nz - s[0]) + min(s[1], ny - s[1])
    return sorted(every[1:], key=lambda s: -hops(s)) + every[:1]


def dot(a, b):
    return lax.dot_general(a, b, (((1,), (0,)), ((), ())), preferred_element_type=F32)


def dot_nt(a, b):
    return lax.dot_general(a, b, (((1,), (1,)), ((), ())), preferred_element_type=F32)


def dot_tn(a, b):
    return lax.dot_general(a, b, (((0,), (0,)), ((), ())), preferred_element_type=F32)


def lanes(shape, axis=1):
    return lax.broadcasted_iota(jnp.int32, shape, axis)


class Place:
    def __init__(self, nwide, nnarrow):
        self.nwide, self.nnarrow = nwide, nnarrow
        self.nz, self.ny = ring_sizes(nwide)
        self.shifts = shifts(nwide)
        self.nx = nnarrow // 2
        self.w = lax.axis_index("wide")
        self.n = lax.axis_index("narrow")
        self.z, self.y = self.w // self.ny, self.w % self.ny
        self.x, self.c = self.n // 2, self.n % 2

    def ahead(self, slot):
        dz, dy = self.shifts[slot]
        return ((self.z + dz) % self.nz) * self.ny + (self.y + dy) % self.ny

    def behind(self, slot):
        dz, dy = self.shifts[slot]
        return ((self.z + self.nz - dz) % self.nz) * self.ny + (self.y + self.ny - dy) % self.ny

    def narrow_at(self, step):
        return (self.n + step) % self.nnarrow

    def greet(self):
        barrier = pltpu.get_barrier_semaphore()
        for slot in range(self.nwide - 1):
            pl.semaphore_signal(
                barrier, inc=1, device_id={"wide": self.ahead(slot)}, device_id_type=MESH
            )
        for step in range(1, self.nnarrow):
            pl.semaphore_signal(
                barrier, inc=1, device_id={"narrow": self.narrow_at(step)}, device_id_type=MESH
            )

    def meet(self):
        pl.semaphore_wait(pltpu.get_barrier_semaphore(), self.nwide + self.nnarrow - 2)


def push(src, dst, send, recv, device):
    copy = pltpu.make_async_remote_copy(
        src_ref=src, dst_ref=dst, send_sem=send, recv_sem=recv, device_id=device, device_id_type=MESH
    )
    copy.start()
    return copy


KMAX = 4
PAIRS = 32
ORDER, JOINS, PLACE, LIVE, END, HAS, PICK, TABLE = 0, 32, 64, 96, 128, 160, 192, 256


def tables_kernel(nwide, nnarrow, cols, counts, send_sel, slot_of, table, tally, following):
    at = Place(nwide, nnarrow)
    blocks, kmax = cols.shape
    dead = nwide + blocks

    def clear(i, carry):
        tally[i] = 0
        return carry

    lax.fori_loop(0, dead + 1, clear, 0)

    def enter(i, carry):
        b, t = i // kmax, i % kmax
        entry = cols[b, t]
        source = jnp.maximum(entry - blocks, 0)
        dz = (at.z + at.nz - source // at.ny) % at.nz
        dy = (at.y + at.ny - source % at.ny) % at.ny
        place = jnp.where(entry < blocks, nwide + entry, slot_of[dz * at.ny + dy])
        live = t < counts[b]
        table[PLACE + i] = place
        table[LIVE + i] = jnp.where(live, 1, 0)
        key = jnp.where(live, place, dead)
        tally[key] = tally[key] + 1
        return carry

    lax.fori_loop(0, blocks * kmax, enter, 0)

    def begin(p, start):
        number = tally[p]
        following[p] = start
        table[END + p] = jnp.maximum(start + number - 1, 0)
        table[HAS + p] = jnp.where(number > 0, 1, 0)
        tally[p] = start
        return start + number

    lax.fori_loop(0, dead + 1, begin, 0)

    def sort(i, carry):
        key = jnp.where(table[LIVE + i] > 0, table[PLACE + i], dead)
        position = following[key]
        following[key] = position + 1
        table[ORDER + position] = i
        table[JOINS + position] = jnp.where(position > tally[key], 1, 0)
        return carry

    lax.fori_loop(0, blocks * kmax, sort, 0)
    for slot in range(nwide):
        table[PICK + slot] = send_sel[0, 0, at.ahead(slot)]


def tables(nwide, nnarrow, cols, counts, send_sel):
    order = shifts(nwide)
    nz, ny = ring_sizes(nwide)
    slot_of = jnp.asarray([order.index((i // ny, i % ny)) for i in range(nwide)], jnp.int32)
    return pl.pallas_call(
        functools.partial(tables_kernel, nwide, nnarrow),
        out_shape=jax.ShapeDtypeStruct((TABLE,), jnp.int32),
        in_specs=[SMEM] * 4,
        out_specs=SMEM,
        scratch_shapes=[pltpu.SMEM((32,), jnp.int32), pltpu.SMEM((32,), jnp.int32)],
        name="tables",
    )(cols, counts, send_sel, slot_of)


class SmallSum:
    def __init__(self, place, part, one, mid, two, out, sems):
        self.place, self.part, self.one, self.mid, self.two, self.out = place, part, one, mid, two, out
        self.sems = sems
        self.per = part.shape[0] // place.nnarrow

    def first(self):
        at, per = self.place, self.per
        self.copies = []
        for step in range(1, at.nnarrow):
            peer = at.narrow_at(step)
            self.copies.append(
                push(
                    self.part.at[pl.ds(peer * per, per)],
                    self.one.at[at.n],
                    self.sems.at[0, 0, step],
                    self.sems.at[0, 1, step],
                    {"narrow": peer},
                )
            )
        self.one[at.n] = self.part[pl.ds(at.n * per, per)]

    def second(self):
        at = self.place
        for copy in self.copies:
            copy.wait()
        total = self.one[0]
        for j in range(1, at.nnarrow):
            total = total + self.one[j]
        self.mid[...] = total
        self.copies = []
        for slot in range(at.nwide - 1):
            self.copies.append(
                push(
                    self.mid,
                    self.two.at[at.w],
                    self.sems.at[1, 0, slot],
                    self.sems.at[1, 1, slot],
                    {"wide": at.ahead(slot)},
                )
            )
        self.two[at.w] = total

    def third(self):
        at, per = self.place, self.per
        for copy in self.copies:
            copy.wait()
        total = self.two[0]
        for j in range(1, at.nwide):
            total = total + self.two[j]
        self.out[pl.ds(at.n * per, per)] = total
        self.copies = []
        for step in range(1, at.nnarrow):
            self.copies.append(
                push(
                    self.out.at[pl.ds(at.n * per, per)],
                    self.out.at[pl.ds(at.n * per, per)],
                    self.sems.at[2, 0, step],
                    self.sems.at[2, 1, step],
                    {"narrow": at.narrow_at(step)},
                )
            )

    def finish(self):
        for copy in self.copies:
            copy.wait()


def block_diagonal(rows16):
    tiled = jnp.concatenate([rows16] * HEADS, axis=0)
    head_row = lanes((HM, D), 0) // VIRT
    head_col = lanes((HM, D), 1) // HEAD
    return jnp.where(head_row == head_col, tiled, jnp.zeros_like(tiled))


def diagonal_rows(full):
    head_col = lanes((VIRT, D), 1) // HEAD
    total = jnp.zeros((VIRT, D), F32)
    for h in range(HEADS):
        total = jnp.where(head_col == h, full[h * VIRT : (h + 1) * VIRT], total)
    return total


class Copies:
    def __init__(self, sems):
        self.sems, self.started = sems, []

    def start(self, src, dst):
        copy = pltpu.make_async_copy(src, dst, self.sems.at[len(self.started)])
        copy.start()
        self.started.append(copy)
        return copy


def sum_refs(at, r, name):
    return SmallSum(at, *[getattr(r, name + key) for key in ("part", "one", "mid", "two", "summed", "sems")])


def stacked(block):
    group_head = lanes(block.shape) // HEAD
    zero = jnp.zeros_like(block)
    return jnp.concatenate([jnp.where(group_head == h, block, zero) for h in range(GROUP)], axis=0)


def unstacked(full):
    rows = full.shape[0] // GROUP
    group_head = lanes((rows, full.shape[1])) // HEAD
    total = full[0:rows]
    for h in range(1, GROUP):
        total = jnp.where(group_head == h, full[h * rows : (h + 1) * rows], total)
    return total


def flat(value):
    return value.reshape(value.shape[0] * value.shape[1], value.shape[2])


def exchange_phase(at, r, loads):
    nwide = at.nwide
    blocks = r.nodes.shape[0]
    rows = blocks * BR
    loads["nodes"].wait()
    copies = []

    def send(first, last):
        for slot in range(first, last):
            copies.append(
                push(
                    r.stage.at[slot],
                    r.far.at[slot],
                    r.send_sems.at[slot],
                    r.recv_sems.at[slot],
                    {"wide": at.ahead(slot)},
                )
            )

    remote = nwide - 1
    early = min(4, remote)
    for slot in range(remote):
        r.stage[slot] = r.nodes[r.table[PICK + slot]]
    at.meet()
    send(0, early)
    r.far[remote] = r.nodes[r.table[PICK + remote]]
    for name in ("w_key", "w_value"):
        loads[name].wait()
    pair = 2

    @pl.loop(0, blocks // pair)
    def _(i):
        here = pl.ds(i * pair, pair)
        there = pl.ds(nwide + i * pair, pair)
        block = flat(r.nodes[here])
        r.pool_k[there] = dot(block, r.w_key[...]).astype(BF).reshape(pair, BR, D)
        r.pool_v[there] = dot(block, r.w_value[...]).astype(BF).reshape(pair, BR, D)

    for name in ("virtual", "w_query"):
        loads[name].wait()
    virt = r.virtual[...]
    r.vq_bd[...] = block_diagonal(dot(virt, r.w_query[...])).astype(BF)
    r.vk_bd[...] = block_diagonal(dot(virt, r.w_key[...])).astype(BF)
    r.vv_bd[...] = block_diagonal(dot(virt, r.w_value[...])).astype(BF)

    expo = jnp.exp(SOFT_CAP * jnp.tanh(dot_nt(r.vq_bd[...], flat(r.pool_k[nwide:])) * IN_CAP))
    den = jnp.sum(expo, axis=1, keepdims=True)
    num = dot(expo.astype(BF), flat(r.pool_v[nwide:]))
    half = lanes((VIRT, 128)) // HEAD
    for h in range(HEADS):
        mine = slice(h * VIRT, (h + 1) * VIRT)
        two = num[mine, (h // 2) * 128 : (h // 2 + 1) * 128]
        r.f_part[h] = jnp.where(half == h % 2, two, jnp.broadcast_to(den[mine], (VIRT, 128)))
    small = sum_refs(at, r, "f_")
    small.first()
    for name in ("grad_out", "w_out", "grad_virtual"):
        loads[name].wait()

    @pl.loop(0, blocks // pair)
    def _(i):
        here = pl.ds(i * pair, pair)
        out_rows = pl.ds(pl.multiple_of(i * pair * BR, pair * BR), pair * BR)
        r.queries[here] = dot(flat(r.nodes[here]), r.w_query[...]).astype(BF).reshape(pair, BR, D)
        da = dot_nt(r.grad_out[out_rows, :], r.w_out[...])
        r.d_attended[here] = da.astype(BF).reshape(pair, BR, D)

    small.second()

    def project_far(first):
        here = slice(first, first + 4)
        for slot in range(first, min(first + 4, nwide - 1)):
            copies[slot].wait_recv()
        landed = flat(r.far[here])
        r.pool_k[here] = dot(landed, r.w_key[...]).astype(BF).reshape(4, BR, D)
        r.pool_v[here] = dot(landed, r.w_value[...]).astype(BF).reshape(4, BR, D)

    send(early, remote)
    groups = list(range(0, nwide, 4))
    project_far(groups[0])
    small.third()
    for first in groups[1:2]:
        project_far(first)
    small.finish()
    virtual_phase(at, r)
    for first in groups[2:]:
        project_far(first)
    for copy in copies:
        copy.wait_send()


def virtual_phase(at, r):
    nwide = at.nwide
    blocks = r.nodes.shape[0]
    pair = 2
    half = lanes((VIRT, 128)) // HEAD
    low = half == 0
    numbers, denoms = [], []
    for j in range(HEADS // 2):
        even, odd = r.f_summed[2 * j], r.f_summed[2 * j + 1]
        numbers.append(jnp.where(low, even, odd))
        denoms.append(pltpu.roll(jnp.where(low, odd, even), HEAD, 1))
    vnum = jnp.concatenate(numbers, axis=1)
    vden = jnp.concatenate(denoms, axis=1)
    summary = vnum / vden
    summary_b = summary.astype(BF)
    zeta = dot(summary_b, r.w_out[...])
    radius = jnp.sqrt(jnp.mean(zeta * zeta, axis=1, keepdims=True) + EPSILON)
    r.out_virtual[...] = zeta / radius
    gv = r.grad_virtual[...]
    dzeta = gv / radius - zeta * jnp.sum(gv * zeta, axis=1, keepdims=True) / (
        D * radius * radius * radius
    )
    dzeta_b = dzeta.astype(BF)
    r.summary_out[...] = summary_b
    r.dzeta_out[...] = dzeta_b
    dsummary = dot_nt(dzeta_b, r.w_out[...])
    r.dnum_bd[...] = block_diagonal((dsummary / vden).astype(BF).astype(F32)).astype(BF)
    along = dsummary * summary
    for h in range(HEADS):
        lane_tile = slice((h // 2) * 128, (h // 2 + 1) * 128)
        mine = jnp.where(half == h % 2, along[:, lane_tile], 0.0)
        down = -jnp.sum(mine, axis=1, keepdims=True)
        den_h = denoms[h // 2][:, (h % 2) * HEAD : (h % 2) * HEAD + 1]
        r.dden[h * VIRT : (h + 1) * VIRT, :] = jnp.broadcast_to(down / den_h, (VIRT, 128))

    r.vq_part[...] = jnp.zeros_like(r.vq_part)
    vq, dn = r.vq_bd[...], r.dnum_bd[...]

    @pl.loop(0, blocks // pair)
    def _(i):
        here = pl.ds(i * pair, pair)
        there = pl.ds(nwide + i * pair, pair)
        own_k, own_v = flat(r.pool_k[there]), flat(r.pool_v[there])
        bend = jnp.tanh(dot_nt(vq, own_k) * IN_CAP)
        expo = jnp.exp2(EXP_CAP * bend)
        dexpo = dot_nt(dn, own_v) + r.dden[:, 0:1]
        ds = (expo * dexpo * (1.0 - bend * bend)).astype(BF)
        r.vq_part[...] += diagonal_rows(dot(ds, own_k)) * SCALE
        r.base_k[here] = dot_tn(ds, vq).reshape(pair, BR, D)
        r.base_v[here] = dot_tn(expo.astype(BF), dn).reshape(pair, BR, D)


def attend_phase(at, r):
    blocks = r.nodes.shape[0]
    gw = GROUP * HEAD
    step = 32
    r.acc_vk[...] = jnp.zeros_like(r.acc_vk)
    r.acc_vv[...] = jnp.zeros_like(r.acc_vv)
    lane_head = lanes((BR, HM)) // VIRT
    half = lanes((BR, 128)) // HEAD

    def block(b, carry):
        live = [None, None]
        for t in range(KMAX):
            place = r.table[PLACE + b * KMAX + t]
            r.kcat[t * BR : (t + 1) * BR, :] = r.pool_k[place]
            r.vcat[t * BR : (t + 1) * BR, :] = r.pool_v[place]
            if t >= 2:
                live.append(r.table[LIVE + b * KMAX + t].astype(F32))
        q = r.queries[b]
        da = r.d_attended[b]
        bend_v = jnp.tanh(dot_nt(q, r.vk_bd[...]) * IN_CAP)
        expo_v = jnp.exp2(EXP_CAP * bend_v)
        dprob_v = dot_nt(da, r.vv_bd[...])
        probs_v = jnp.zeros((BR, HM), F32)
        delta_v = jnp.zeros((BR, HM), F32)
        for g in range(HEADS // GROUP):
            wide = slice(g * gw, (g + 1) * gw)
            at_tile = [(b * KMAX + t) * 2 + g for t in range(KMAX)]
            r.scores[...] = dot_nt(stacked(q[:, wide]), r.kcat[:, wide])
            r.dprob[...] = dot_nt(stacked(da[:, wide]), r.vcat[:, wide])
            for h in range(GROUP):
                head = g * GROUP + h
                virt_sum = jnp.sum(jnp.where(lane_head == head, expo_v, 0.0), axis=1, keepdims=True)
                inverses = []
                for first in range(0, BR, step):
                    here = slice(h * BR + first, h * BR + first + step)
                    bends, expos = [], []
                    total = None
                    for t in range(KMAX):
                        bend = jnp.tanh(r.scores[here, t * BR : (t + 1) * BR] * IN_CAP)
                        expo = jnp.exp2(EXP_CAP * bend)
                        if live[t] is not None:
                            expo = expo * live[t]
                        bends.append(bend)
                        expos.append(expo)
                        total = expo if total is None else total + expo
                    total = jnp.sum(total, axis=1, keepdims=True) + virt_sum[first : first + step]
                    inverse = 1.0 / total
                    inverses.append(inverse)
                    for t in range(KMAX):
                        weight = expos[t] * inverse
                        r.probs[at_tile[t], here, :] = weight.astype(BF)
                        r.scores[here, t * BR : (t + 1) * BR] = weight * (1.0 - bends[t] * bends[t])
                probs_v = jnp.where(lane_head == head, expo_v * jnp.concatenate(inverses, axis=0), probs_v)
            pv = probs_v.astype(BF)
            probs = jnp.concatenate([r.probs[i] for i in at_tile], axis=1)
            mixed = unstacked(dot(probs, r.vcat[:, wide])) + dot(pv, r.vv_bd[:, wide])
            mixed_b = mixed.astype(BF)
            r.attended[b, :, wide] = mixed_b
            along = da[:, wide].astype(F32) * mixed_b.astype(F32)
            for h in range(GROUP):
                head = g * GROUP + h
                lane_tile = slice((h // 2) * 128, (h // 2 + 1) * 128)
                delta = jnp.sum(jnp.where(half == h % 2, along[:, lane_tile], 0.0), axis=1, keepdims=True)
                delta_v = jnp.where(lane_head == head, delta, delta_v)
                for first in range(0, BR, step):
                    here = slice(h * BR + first, h * BR + first + step)
                    for t in range(KMAX):
                        at_lanes = slice(t * BR, (t + 1) * BR)
                        r.dscore[at_tile[t], here, :] = (
                            r.scores[here, at_lanes] * (r.dprob[here, at_lanes] - delta[first : first + step])
                        ).astype(BF)
            ds_v = (probs_v * (dprob_v - delta_v) * (1.0 - bend_v * bend_v)).astype(BF)
            dscore = jnp.concatenate([r.dscore[i] for i in at_tile], axis=1)
            dq = unstacked(dot(dscore, r.kcat[:, wide])) + dot(ds_v, r.vk_bd[:, wide])
            r.dquery[b, :, wide] = (dq * SCALE).astype(BF)
        r.acc_vk[...] += dot_tn(ds_v, q)
        r.acc_vv[...] += dot_tn(pv, da)
        return carry

    lax.fori_loop(0, blocks, block, 0)
    r.vk_part[...] = diagonal_rows(r.acc_vk[...]) * SCALE
    r.vv_part[...] = diagonal_rows(r.acc_vv[...])
    r.sum_k[...] = jnp.zeros_like(r.sum_k)
    r.sum_v[...] = jnp.zeros_like(r.sum_v)
    r.base_k[blocks] = jnp.zeros((BR, D), F32)
    r.base_v[blocks] = jnp.zeros((BR, D), F32)


def reduce_phase(at, r, stores):
    nwide = at.nwide
    blocks = r.nodes.shape[0]
    rows = blocks * BR
    halfd = D // 2
    band = halfd // at.nx
    chunk = 4 * band // nwide
    gw = GROUP * HEAD

    for j, ref in enumerate((r.vq_part, r.vk_part, r.vv_part)):
        for lt in range(D // 128):
            tile = ref[:, lt * 128 : (lt + 1) * 128]
            if j == 0:
                r.b_part[2 * lt, 0:16] = tile
            elif j == 1:
                r.b_part[2 * lt, 16:24] = tile[0:8]
                r.b_part[2 * lt + 1, 0:8] = tile[8:16]
            else:
                r.b_part[2 * lt + 1, 8:24] = tile
    small = sum_refs(at, r, "b_")
    small.first()

    def entry(based, position, carry):
        i = r.table[ORDER + position]
        joins = r.table[JOINS + position].astype(F32)
        q, da = r.queries[i // KMAX], r.d_attended[i // KMAX]
        if based:
            base = jnp.where(r.table[PLACE + i] >= nwide, r.table[PLACE + i] - nwide, blocks)
            base_k, base_v = r.base_k[base], r.base_v[base]
        for g in range(HEADS // GROUP):
            wide = slice(g * gw, (g + 1) * gw)
            dk = dot_tn(r.dscore[i * 2 + g], stacked(q[:, wide]))
            dv = dot_tn(r.probs[i * 2 + g], stacked(da[:, wide]))
            total_k = joins * r.sum_k[:, wide] + dk
            total_v = joins * r.sum_v[:, wide] + dv
            if based:
                total_k = total_k + (1.0 - joins) * base_k[:, wide]
                total_v = total_v + (1.0 - joins) * base_v[:, wide]
            r.sum_k[:, wide] = total_k
            r.sum_v[:, wide] = total_v
            r.run_k[position, :, wide] = (total_k * SCALE).astype(BF)
            r.run_v[position, :, wide] = total_v.astype(BF)
        return carry

    def entries(first, last):
        middle = min(max(first, nwide), last)
        if middle > first:
            lax.fori_loop(first, middle, functools.partial(entry, False), 0)
        if last > middle:
            lax.fori_loop(middle, last, functools.partial(entry, True), 0)

    own_rows = pl.ds(pl.multiple_of(at.c * halfd, halfd), halfd)
    sib_rows = pl.ds(pl.multiple_of((1 - at.c) * halfd, halfd), halfd)
    sibling = {"narrow": at.x * 2 + 1 - at.c}
    x_steps = sorted(range(1, at.nx), key=lambda step: -min(step, at.nx - step))
    per = halfd // BR

    def grad_half(g, which):
        if g == 0:
            return dot_tn(flat(r.attended[:, :, which]), r.grad_out[...])
        if g == 1:
            return dot_tn(flat(r.nodes[:, :, which]), flat(r.dquery[...]))
        parts = r.pool_k if g == 2 else r.pool_v
        total = dot_tn(flat(r.nodes[:, :, which]), flat(parts[nwide:]))
        for first in range(0, nwide, 8):
            here = slice(first, min(first + 8, nwide))
            total = total + dot_tn(flat(r.far[here, :, which]), flat(parts[here]))
        return total

    sib_copies, x_copies = [], {}

    def kept(g):
        return (r.scores, r.dprob)[g // 2].at[(g % 2) * halfd : (g % 2 + 1) * halfd]

    def leaving(g):
        return (r.kcat, r.vcat)[g // 2].at[(g % 2) * halfd : (g % 2 + 1) * halfd]

    def x_stage(g):
        sib_copies[g].wait_recv()
        mine = slice(per * g, per * g + per)
        total = kept(g)[...] + flat(r.sib_recv[mine]).astype(F32)
        kept(g)[...] = total
        leaving(g)[...] = total.astype(BF)
        for step in x_steps:
            peer = (at.x + step) % at.nx
            x_copies[g, step] = push(
                leaving(g).at[pl.ds(pl.multiple_of(peer * band, band), band)],
                r.x_recv.at[g, step - 1],
                r.x_sems.at[g, 0, step],
                r.x_sems.at[g, 1, step],
                {"narrow": peer * 2 + at.c},
            )

    def gradient(g):
        mine = slice(per * g, per * g + per)
        r.sib_send[mine] = grad_half(g, sib_rows).astype(BF).reshape(per, BR, D)
        sib_copies.append(
            push(
                r.sib_send.at[mine],
                r.sib_recv.at[mine],
                r.sib_sems.at[0, g],
                r.sib_sems.at[1, g],
                sibling,
            )
        )
        kept(g)[...] = grad_half(g, own_rows)

    slack = blocks * KMAX - blocks - nwide
    returns = []
    reached = 0
    groups = list(range(0, nwide, 4))
    for first in groups:
        until = slack + first + 4
        entries(reached, until)
        reached = until
        for place in range(first, first + 4):
            end = r.table[END + place]
            r.pool_k[place] = r.run_k[end]
            r.pool_v[place] = r.run_v[end]
        here = slice(first, first + 4)
        part = dot_nt(flat(r.pool_k[here]), r.w_key[...]) + dot_nt(flat(r.pool_v[here]), r.w_value[...])
        r.stage[here] = part.astype(BF).reshape(4, BR, D)
        for slot in range(first, min(first + 4, nwide - 1)):
            returns.append(
                push(
                    r.stage.at[slot],
                    r.back.at[slot],
                    r.back_sems.at[0, slot],
                    r.back_sems.at[1, slot],
                    {"wide": at.behind(slot)},
                )
            )
        if first == groups[0]:
            small.second()
        if first == groups[min(1, len(groups) - 1)]:
            gradient(0)
            gradient(1)
            x_stage(0)
            x_stage(1)
    stores.start(r.stage.at[nwide - 1], r.back_hbm.at[nwide - 1])
    entries(reached, blocks * KMAX)
    for own in range(blocks):
        end = r.table[END + nwide + own]
        has = r.table[HAS + nwide + own] > 0
        r.pool_k[nwide + own] = jnp.where(has, r.run_k[end], (r.base_k[own] * SCALE).astype(BF))
        r.pool_v[nwide + own] = jnp.where(has, r.run_v[end], r.base_v[own].astype(BF))

    gradient(2)
    gradient(3)
    x_stage(2)
    x_stage(3)
    small.third()
    pair = 2

    @pl.loop(0, blocks // pair)
    def _(i):
        here = pl.ds(i * pair, pair)
        there = pl.ds(nwide + i * pair, pair)
        total = (
            dot_nt(flat(r.dquery[here]), r.w_query[...])
            + dot_nt(flat(r.pool_k[there]), r.w_key[...])
            + dot_nt(flat(r.pool_v[there]), r.w_value[...])
        )
        r.base_v[here] = total.reshape(pair, BR, D)

    stores.start(r.base_v.at[0:blocks], r.local_hbm)

    spot = at.x * band
    for g in range(4):
        total = kept(g)[pl.ds(pl.multiple_of(spot, band), band), :]
        for step in x_steps:
            x_copies[g, step].wait()
            total = total + r.x_recv[g, step - 1].astype(F32)
        r.base_k[g * band // BR, g * band % BR : g * band % BR + band, :] = total
        r.w_send[g * band : (g + 1) * band, :] = total.astype(BF)

    w_copies = []
    for slot in range(nwide - 1):
        peer = at.ahead(slot)
        w_copies.append(
            push(
                r.w_send.at[pl.ds(pl.multiple_of(peer * chunk, chunk), chunk)],
                r.w_recv.at[slot],
                r.w_sems.at[0, slot],
                r.w_sems.at[1, slot],
                {"wide": peer},
            )
        )

    @pl.loop(0, blocks // pair)
    def _(i):
        here = pl.ds(i * pair, pair)
        out = dot(flat(r.attended[here]), r.w_out[...])
        r.attended[here] = out.astype(BF).reshape(pair, BR, D)

    stores.start(r.attended, r.out_nodes_hbm)

    spot = at.w * chunk
    total = r.base_k[spot // BR, pl.ds(pl.multiple_of(spot % BR, chunk), chunk), :]
    for slot in range(nwide - 1):
        w_copies[slot].wait_recv()
        total = total + r.w_recv[slot].astype(F32)
    done = total.astype(BF)
    r.lower[at.n, at.w] = done[:, 0:halfd]
    r.upper[at.c, at.w, at.x] = done[:, halfd:]
    up_first, low_first = [], []
    for step in x_steps:
        up_first.append(
            push(
                r.upper.at[at.c, at.w, at.x],
                r.upper.at[at.c, at.w, at.x],
                r.up_sems.at[0, 0, step],
                r.up_sems.at[0, 1, step],
                {"narrow": (at.x + step) % at.nx * 2 + at.c},
            )
        )
    for slot in range(nwide - 1):
        low_first.append(
            push(
                r.lower.at[at.n, at.w],
                r.lower.at[at.n, at.w],
                r.low_sems.at[0, 0, slot],
                r.low_sems.at[0, 1, slot],
                {"wide": at.ahead(slot)},
            )
        )
    small.finish()
    r.virt_sums[...] = r.b_summed[...]
    for copy in up_first:
        copy.wait_recv()
    up_second, low_second, across = [], {}, []
    for slot in range(nwide - 1):
        up_second.append(
            push(
                r.upper.at[at.c, at.w],
                r.upper.at[at.c, at.w],
                r.up_sems.at[1, 0, slot],
                r.up_sems.at[1, 1, slot],
                {"wide": at.ahead(slot)},
            )
        )
    for copy in low_first:
        copy.wait_recv()
    for step in x_steps:
        low_second[step] = push(
            r.lower.at[at.n],
            r.lower.at[at.n],
            r.low_sems.at[1, 0, step],
            r.low_sems.at[1, 1, step],
            {"narrow": (at.x + step) % at.nx * 2 + at.c},
        )

    def low_across(landed, step):
        across.append(
            push(
                r.lower.at[landed],
                r.lower.at[landed],
                r.across_sems.at[0, 0, step],
                r.across_sems.at[0, 1, step],
                sibling,
            )
        )

    def up_across(slot):
        landed = at.behind(slot)
        across.append(
            push(
                r.upper.at[at.c, landed],
                r.upper.at[at.c, landed],
                r.across_sems.at[1, 0, slot],
                r.across_sems.at[1, 1, slot],
                sibling,
            )
        )

    low_across(at.n, 0)
    up_across(nwide - 1)
    for slot in range(nwide - 1):
        returns[slot].wait_recv()
        stores.start(r.back.at[slot], r.back_hbm.at[slot])
    for slot in range(nwide - 1):
        up_second[slot].wait_recv()
        up_across(slot)
    for step in x_steps:
        low_second[step].wait_recv()
        low_across((at.x + at.nx - step) % at.nx * 2 + at.c, step)
    for copy in across:
        copy.wait()
    stores.start(r.lower, r.lower_hbm)
    stores.start(r.upper, r.upper_hbm)
    for copy in returns + w_copies + sib_copies + up_first + low_first + up_second:
        copy.wait_send()
    for copy in low_second.values():
        copy.wait_send()


LOADED = ("nodes", "w_key", "w_value", "virtual", "w_query", "grad_out", "w_out", "grad_virtual")


def layer_kernel(nwide, nnarrow, names, *refs):
    r = types.SimpleNamespace(**dict(zip(names, refs, strict=True)))
    at = Place(nwide, nnarrow)
    at.greet()
    started = Copies(r.load_sems)
    loads = {name: started.start(getattr(r, name + "_hbm"), getattr(r, name)) for name in LOADED}
    stores = Copies(r.store_sems)
    exchange_phase(at, r, loads)
    attend_phase(at, r)
    reduce_phase(at, r, stores)
    for copy in stores.started:
        copy.wait()


def layer(nwide, nnarrow, table, arrays):
    blocks = arrays["nodes"].shape[0]
    rows = blocks * BR
    pool = blocks + nwide
    entries = blocks * KMAX
    nx = nnarrow // 2
    band = D // 2 // nx
    chunk = 4 * band // nwide
    per = 8 // nnarrow
    sems = pltpu.SemaphoreType.DMA
    most = max(nwide, nnarrow)
    shape = jax.ShapeDtypeStruct
    outs = {
        "out_nodes_hbm": shape((blocks, BR, D), BF),
        "local_hbm": shape((blocks, BR, D), F32),
        "back_hbm": shape((nwide, BR, D), BF),
        "lower_hbm": shape((nnarrow, nwide, chunk, D // 2), BF),
        "upper_hbm": shape((2, nwide, nx, chunk, D // 2), BF),
        "virt_sums": shape((8, 24, 128), F32),
        "out_virtual": shape((VIRT, D), F32),
        "summary_out": shape((VIRT, D), BF),
        "dzeta_out": shape((VIRT, D), BF),
    }
    vmem = {name: (arrays[name].shape, arrays[name].dtype) for name in LOADED}
    vmem |= {
        "stage": ((nwide, BR, D), BF),
        "far": ((nwide, BR, D), BF),
        "queries": ((blocks, BR, D), BF),
        "d_attended": ((blocks, BR, D), BF),
        "attended": ((blocks, BR, D), BF),
        "dquery": ((blocks, BR, D), BF),
        "pool_k": ((pool, BR, D), BF),
        "pool_v": ((pool, BR, D), BF),
        "vq_bd": ((HM, D), BF),
        "vk_bd": ((HM, D), BF),
        "vv_bd": ((HM, D), BF),
        "dnum_bd": ((HM, D), BF),
        "dden": ((HM, 128), F32),
        "vq_part": ((VIRT, D), F32),
        "vk_part": ((VIRT, D), F32),
        "vv_part": ((VIRT, D), F32),
        "acc_vk": ((HM, D), F32),
        "acc_vv": ((HM, D), F32),
        "base_k": ((blocks + 1, BR, D), F32),
        "base_v": ((blocks + 1, BR, D), F32),
        "kcat": ((KMAX * BR, D), BF),
        "vcat": ((KMAX * BR, D), BF),
        "scores": ((GROUP * BR, KMAX * BR), F32),
        "dprob": ((GROUP * BR, KMAX * BR), F32),
        "probs": ((entries * 2, GROUP * BR, BR), BF),
        "dscore": ((entries * 2, GROUP * BR, BR), BF),
        "sum_k": ((BR, D), F32),
        "sum_v": ((BR, D), F32),
        "run_k": ((entries, BR, D), BF),
        "run_v": ((entries, BR, D), BF),
        "back": ((nwide, BR, D), BF),
        "sib_send": ((4 * (D // 2 // BR), BR, D), BF),
        "sib_recv": ((4 * (D // 2 // BR), BR, D), BF),
        "x_recv": ((4, nx - 1, band, D), BF),
        "w_send": ((4 * band, D), BF),
        "w_recv": ((nwide, chunk, D), BF),
        "lower": (outs["lower_hbm"].shape, BF),
        "upper": (outs["upper_hbm"].shape, BF),
    }
    for name, height in (("f_", VIRT), ("b_", 24)):
        vmem |= {
            name + "part": ((8, height, 128), F32),
            name + "one": ((nnarrow, per, height, 128), F32),
            name + "mid": ((per, height, 128), F32),
            name + "two": ((nwide, per, height, 128), F32),
            name + "summed": ((8, height, 128), F32),
        }
    sem_shapes = {
        "f_sems": (3, 2, most),
        "b_sems": (3, 2, most),
        "send_sems": (nwide,),
        "recv_sems": (nwide,),
        "back_sems": (2, nwide),
        "sib_sems": (2, 4),
        "x_sems": (4, 2, nx),
        "w_sems": (2, nwide),
        "low_sems": (2, 2, nwide),
        "up_sems": (2, 2, nwide),
        "across_sems": (2, 2, nwide),
        "load_sems": (len(LOADED),),
        "store_sems": (nwide + 4,),
    }
    names = (
        ["table"] + [name + "_hbm" for name in LOADED] + list(outs) + list(vmem) + list(sem_shapes)
    )
    results = pl.pallas_call(
        functools.partial(layer_kernel, nwide, nnarrow, names),
        out_shape=list(outs.values()),
        in_specs=[SMEM] + [ANY] * len(LOADED),
        out_specs=[ANY] * 5 + [VMEM] * 4,
        scratch_shapes=[pltpu.VMEM(*kind) for kind in vmem.values()]
        + [sems(kind) for kind in sem_shapes.values()],
        compiler_params=pltpu.CompilerParams(
            collective_id=0, has_side_effects=True, vmem_limit_bytes=VMEM_LIMIT
        ),
        name="layer",
    )(table, *[arrays[name] for name in LOADED])
    return dict(zip(outs, results))


def finish_kernel(
    nwide,
    nnarrow,
    table,
    local_hbm,
    back_hbm,
    lower_hbm,
    upper_hbm,
    out_nodes_in,
    virt_sums,
    virtual,
    summary_b,
    dzeta_b,
    out_virtual_in,
    w_query_hbm,
    w_key_hbm,
    w_value_hbm,
    out_nodes,
    grad_nodes_hbm,
    grad_query_hbm,
    grad_key_hbm,
    grad_value_hbm,
    grad_wout_hbm,
    out_virtual,
    virtual_grad,
    lower,
    upper,
    back,
    grad_nodes,
    grads,
    w_query,
    w_key,
    w_value,
    out_rows,
    load_sems,
    store_sems,
):
    at = Place(nwide, nnarrow)
    started, stores = Copies(load_sems), Copies(store_sems)
    load_low = started.start(lower_hbm, lower)
    load_up = started.start(upper_hbm, upper)
    load_back = started.start(back_hbm, back)
    load_local = started.start(local_hbm, grad_nodes)
    load_w = [
        started.start(src, dst)
        for src, dst in ((w_query_hbm, w_query), (w_key_hbm, w_key), (w_value_hbm, w_value))
    ]
    load_out = started.start(out_nodes_in, out_rows)
    out_virtual[...] = out_virtual_in[...]
    top = jnp.concatenate([virt_sums[2 * lt] for lt in range(D // 128)], axis=1)
    bottom = jnp.concatenate([virt_sums[2 * lt + 1] for lt in range(D // 128)], axis=1)
    vq_grad = top[0:16].astype(BF)
    vk_grad = jnp.concatenate([top[16:24], bottom[0:8]], axis=0).astype(BF)
    vv_grad = bottom[8:24].astype(BF)
    halfd = D // 2
    band = halfd // at.nx
    chunk = 4 * band // nwide
    pairs = (
        (grad_wout_hbm, summary_b[...], dzeta_b[...]),
        (grad_query_hbm, virtual[...], vq_grad),
        (grad_key_hbm, virtual[...], vk_grad),
        (grad_value_hbm, virtual[...], vv_grad),
    )
    per = nwide // 4
    load_low.wait()
    load_up.wait()
    for g, (out, left, right) in enumerate(pairs):
        grads[g] = dot_tn(left, right)
        for n in range(nnarrow):
            first = (n % 2) * halfd + (n // 2) * band
            for j in range(per):
                here = slice(first + j * chunk, first + (j + 1) * chunk)
                grads[g, here, 0:halfd] += lower[n, g * per + j].astype(F32)
                grads[g, here, halfd:] += upper[n % 2, g * per + j, n // 2].astype(F32)
        stores.start(grads.at[g], out)
    load_out.wait()
    stores.start(out_rows, out_nodes)
    load_back.wait()
    load_local.wait()
    for slot in range(nwide):
        grad_nodes[table[PICK + slot]] += back[slot].astype(F32)
    stores.start(grad_nodes, grad_nodes_hbm)
    for copy in load_w:
        copy.wait()
    virtual_grad[...] = (
        dot_nt(vq_grad, w_query[...]) + dot_nt(vk_grad, w_key[...]) + dot_nt(vv_grad, w_value[...])
    )
    for copy in stores.started:
        copy.wait()


def finish(nwide, nnarrow, table, got, arrays):
    shape = jax.ShapeDtypeStruct
    outs = (
        [shape(got["out_nodes_hbm"].shape, BF), shape(got["local_hbm"].shape, F32)]
        + [shape((D, D), F32)] * 4
        + [shape((VIRT, D), F32)] * 2
    )
    scratch = [(got[name].shape, got[name].dtype) for name in ("lower_hbm", "upper_hbm", "back_hbm", "local_hbm")]
    scratch += [((4, D, D), F32)] + [((D, D), BF)] * 3
    scratch += [(got["out_nodes_hbm"].shape, BF)]
    return pl.pallas_call(
        functools.partial(finish_kernel, nwide, nnarrow),
        out_shape=outs,
        in_specs=[SMEM] + [ANY] * 5 + [VMEM] * 5 + [ANY] * 3,
        out_specs=[ANY] * 6 + [VMEM] * 2,
        scratch_shapes=[pltpu.VMEM(*kind) for kind in scratch]
        + [pltpu.SemaphoreType.DMA((8,)), pltpu.SemaphoreType.DMA((6,))],
        compiler_params=pltpu.CompilerParams(vmem_limit_bytes=VMEM_LIMIT),
        name="finish",
    )(
        table,
        *[got[name] for name in ("local_hbm", "back_hbm", "lower_hbm", "upper_hbm", "out_nodes_hbm", "virt_sums")],
        arrays["virtual"],
        *[got[name] for name in ("summary_out", "dzeta_out", "out_virtual")],
        arrays["w_query"],
        arrays["w_key"],
        arrays["w_value"],
    )


def shards(
    nwide,
    nnarrow,
    nodes,
    virtual,
    w_query,
    w_key,
    w_value,
    w_out,
    col_blocks,
    col_count,
    send_sel,
    grad_out,
    grad_virtual,
):
    rows = nodes.shape[0]
    arrays = {
        "nodes": nodes.reshape(rows // BR, BR, D),
        "w_key": w_key,
        "w_value": w_value,
        "virtual": virtual,
        "w_query": w_query,
        "grad_out": grad_out,
        "w_out": w_out,
        "grad_virtual": grad_virtual,
    }
    table = tables(nwide, nnarrow, col_blocks, col_count, send_sel)
    got = layer(nwide, nnarrow, table, arrays)
    out_nodes, grad_nodes, grad_query, grad_key, grad_value, grad_wout, out_virtual, virtual_grad = finish(
        nwide, nnarrow, table, got, arrays
    )
    return (
        out_nodes.reshape(rows, D),
        out_virtual,
        grad_nodes.reshape(rows, D),
        virtual_grad,
        grad_query,
        grad_key,
        grad_value,
        grad_wout,
    )


def solution(mesh):
    spread = P(("wide", "narrow"), None)
    in_specs = (
        spread,
        P(),
        P(),
        P(),
        P(),
        P(),
        spread,
        P(("wide", "narrow")),
        P("wide", "narrow", None),
        spread,
        P(),
    )
    out_specs = (spread, P(), spread, P(), P(), P(), P(), P())
    return jax.shard_map(
        functools.partial(shards, mesh.shape["wide"], mesh.shape["narrow"]),
        mesh=mesh,
        in_specs=in_specs,
        out_specs=out_specs,
        check_vma=False,
    )
```

```python
import functools
import math
import types

import jax
import jax.numpy as jnp
from jax import lax
from jax.experimental import pallas as pl
from jax.experimental.pallas import tpu as pltpu
from jax.sharding import PartitionSpec as P

D = 512
HEADS = 8
VIRT = 16
BR = 128
HEAD = D // HEADS
HM = HEADS * VIRT
SCALE = HEAD ** (-0.5)
SOFT_CAP = 5.0
EPSILON = 1e-06
IN_CAP = SCALE / SOFT_CAP
EXP_CAP = SOFT_CAP * math.log2(math.e)
BF = jnp.bfloat16
F32 = jnp.float32
MESH = pl.DeviceIdType.MESH
VMEM = pl.BlockSpec(memory_space=pltpu.VMEM)
SMEM = pl.BlockSpec(memory_space=pltpu.SMEM)
ANY = pl.BlockSpec(memory_space=pl.ANY)
VMEM_LIMIT = 63 * 1024 * 1024
GROUP = 4


def ring_sizes(nwide):
    ny = 4 if nwide == 16 else 2
    return nwide // ny, ny


def shifts(nwide):
    nz, ny = ring_sizes(nwide)
    every = [(dz, dy) for dz in range(nz) for dy in range(ny)]
    hops = lambda s: min(s[0], nz - s[0]) + min(s[1], ny - s[1])
    return sorted(every[1:], key=lambda s: -hops(s)) + every[:1]


def dot(a, b):
    return lax.dot_general(a, b, (((1,), (0,)), ((), ())), preferred_element_type=F32)


def dot_nt(a, b):
    return lax.dot_general(a, b, (((1,), (1,)), ((), ())), preferred_element_type=F32)


def dot_tn(a, b):
    return lax.dot_general(a, b, (((0,), (0,)), ((), ())), preferred_element_type=F32)


def lanes(shape, axis=1):
    return lax.broadcasted_iota(jnp.int32, shape, axis)


class Place:
    def __init__(self, nwide, nnarrow):
        self.nwide, self.nnarrow = nwide, nnarrow
        self.nz, self.ny = ring_sizes(nwide)
        self.shifts = shifts(nwide)
        self.nx = nnarrow // 2
        self.w = lax.axis_index("wide")
        self.n = lax.axis_index("narrow")
        self.z, self.y = self.w // self.ny, self.w % self.ny
        self.x, self.c = self.n // 2, self.n % 2

    def ahead(self, slot):
        dz, dy = self.shifts[slot]
        return ((self.z + dz) % self.nz) * self.ny + (self.y + dy) % self.ny

    def behind(self, slot):
        dz, dy = self.shifts[slot]
        return ((self.z + self.nz - dz) % self.nz) * self.ny + (self.y + self.ny - dy) % self.ny

    def narrow_at(self, step):
        return (self.n + step) % self.nnarrow

    def greet(self):
        barrier = pltpu.get_barrier_semaphore()
        for slot in range(self.nwide - 1):
            pl.semaphore_signal(
                barrier, inc=1, device_id={"wide": self.ahead(slot)}, device_id_type=MESH
            )
        for step in range(1, self.nnarrow):
            pl.semaphore_signal(
                barrier, inc=1, device_id={"narrow": self.narrow_at(step)}, device_id_type=MESH
            )

    def meet(self):
        pl.semaphore_wait(pltpu.get_barrier_semaphore(), self.nwide + self.nnarrow - 2)


def push(src, dst, send, recv, device):
    copy = pltpu.make_async_remote_copy(
        src_ref=src, dst_ref=dst, send_sem=send, recv_sem=recv, device_id=device, device_id_type=MESH
    )
    copy.start()
    return copy


KMAX = 4
PAIRS = 32
ORDER, JOINS, PLACE, LIVE, END, HAS, PICK, TABLE = 0, 32, 64, 96, 128, 160, 192, 256


def tables_kernel(nwide, nnarrow, cols, counts, send_sel, slot_of, table, tally, following):
    at = Place(nwide, nnarrow)
    kmax, blocks = cols.shape
    dead = nwide + blocks

    def clear(i, carry):
        tally[i] = 0
        return carry

    lax.fori_loop(0, dead + 1, clear, 0, unroll=True)

    def enter(i, carry):
        b, t = i // kmax, i % kmax
        entry = cols[t, b]
        source = jnp.maximum(entry - blocks, 0)
        dz = (at.z + at.nz - source // at.ny) % at.nz
        dy = (at.y + at.ny - source % at.ny) % at.ny
        place = jnp.where(entry < blocks, nwide + entry, slot_of[dz * at.ny + dy])
        live = t < counts[b]
        table[PLACE + i] = place
        table[LIVE + i] = jnp.where(live, 1, 0)
        key = jnp.where(live, place, dead)
        tally[key] = tally[key] + 1
        return carry

    lax.fori_loop(0, blocks * kmax, enter, 0, unroll=True)

    def begin(p, start):
        number = tally[p]
        following[p] = start
        table[END + p] = jnp.maximum(start + number - 1, 0)
        table[HAS + p] = jnp.where(number > 0, 1, 0)
        tally[p] = start
        return start + number

    lax.fori_loop(0, dead + 1, begin, 0, unroll=True)

    def sort(i, carry):
        key = jnp.where(table[LIVE + i] > 0, table[PLACE + i], dead)
        position = following[key]
        following[key] = position + 1
        table[ORDER + position] = i
        table[JOINS + position] = jnp.where(position > tally[key], 1, 0)
        return carry

    lax.fori_loop(0, blocks * kmax, sort, 0, unroll=True)
    for slot in range(nwide):
        table[PICK + slot] = send_sel[0, 0, at.ahead(slot)]


def tables(nwide, nnarrow, cols, counts, send_sel):
    order = shifts(nwide)
    nz, ny = ring_sizes(nwide)
    slot_of = jnp.asarray([order.index((i // ny, i % ny)) for i in range(nwide)], jnp.int32)
    return pl.pallas_call(
        functools.partial(tables_kernel, nwide, nnarrow),
        out_shape=jax.ShapeDtypeStruct((TABLE,), jnp.int32),
        in_specs=[SMEM] * 4,
        out_specs=SMEM,
        scratch_shapes=[pltpu.SMEM((32,), jnp.int32), pltpu.SMEM((32,), jnp.int32)],
        name="tables",
    )(cols, counts, send_sel, slot_of)


class SmallSum:
    def __init__(self, place, part, one, mid, two, out, sems):
        self.place, self.part, self.one, self.mid, self.two, self.out = place, part, one, mid, two, out
        self.sems = sems
        self.per = part.shape[0] // place.nnarrow

    def first(self):
        at, per = self.place, self.per
        self.copies = []
        for step in range(1, at.nnarrow):
            peer = at.narrow_at(step)
            self.copies.append(
                push(
                    self.part.at[pl.ds(peer * per, per)],
                    self.one.at[at.n],
                    self.sems.at[0, 0, step],
                    self.sems.at[0, 1, step],
                    {"narrow": peer},
                )
            )
        self.one[at.n] = self.part[pl.ds(at.n * per, per)]

    def second(self):
        at = self.place
        for copy in self.copies:
            copy.wait()
        total = self.one[0]
        for j in range(1, at.nnarrow):
            total = total + self.one[j]
        self.mid[...] = total
        self.copies = []
        for slot in range(at.nwide - 1):
            self.copies.append(
                push(
                    self.mid,
                    self.two.at[at.w],
                    self.sems.at[1, 0, slot],
                    self.sems.at[1, 1, slot],
                    {"wide": at.ahead(slot)},
                )
            )
        self.two[at.w] = total

    def third(self):
        at, per = self.place, self.per
        for copy in self.copies:
            copy.wait()
        total = self.two[0]
        for j in range(1, at.nwide):
            total = total + self.two[j]
        self.out[pl.ds(at.n * per, per)] = total
        self.copies = []
        for step in range(1, at.nnarrow):
            self.copies.append(
                push(
                    self.out.at[pl.ds(at.n * per, per)],
                    self.out.at[pl.ds(at.n * per, per)],
                    self.sems.at[2, 0, step],
                    self.sems.at[2, 1, step],
                    {"narrow": at.narrow_at(step)},
                )
            )

    def finish(self):
        for copy in self.copies:
            copy.wait()


def block_diagonal(rows16):
    tiled = jnp.concatenate([rows16] * HEADS, axis=0)
    head_row = lanes((HM, D), 0) // VIRT
    head_col = lanes((HM, D), 1) // HEAD
    return jnp.where(head_row == head_col, tiled, jnp.zeros_like(tiled))


def diagonal_rows(full):
    head_col = lanes((VIRT, D), 1) // HEAD
    total = jnp.zeros((VIRT, D), F32)
    for h in range(HEADS):
        total = jnp.where(head_col == h, full[h * VIRT : (h + 1) * VIRT], total)
    return total


class Copies:
    def __init__(self, sems):
        self.sems, self.started = sems, []

    def start(self, src, dst):
        copy = pltpu.make_async_copy(src, dst, self.sems.at[len(self.started)])
        copy.start()
        self.started.append(copy)
        return copy


def sum_refs(at, r, name):
    return SmallSum(at, *[getattr(r, name + key) for key in ("part", "one", "mid", "two", "summed", "sems")])


def stacked(block):
    group_head = lanes(block.shape) // HEAD
    zero = jnp.zeros_like(block)
    return jnp.concatenate([jnp.where(group_head == h, block, zero) for h in range(GROUP)], axis=0)


def unstacked(full):
    rows = full.shape[0] // GROUP
    group_head = lanes((rows, full.shape[1])) // HEAD
    total = full[0:rows]
    for h in range(1, GROUP):
        total = jnp.where(group_head == h, full[h * rows : (h + 1) * rows], total)
    return total


def flat(value):
    return value.reshape(value.shape[0] * value.shape[1], value.shape[2])


def exchange_phase(at, r, loads):
    nwide = at.nwide
    blocks = r.nodes.shape[0]
    rows = blocks * BR
    loads["nodes"].wait()
    copies = []

    def send(first, last):
        for slot in range(first, last):
            copies.append(
                push(
                    r.stage.at[slot],
                    r.far.at[slot],
                    r.send_sems.at[slot],
                    r.recv_sems.at[slot],
                    {"wide": at.ahead(slot)},
                )
            )

    remote = nwide - 1
    early = min(4, remote)
    for slot in range(remote):
        r.stage[slot] = r.nodes[r.table[PICK + slot]]
    at.meet()
    send(0, early)
    r.far[remote] = r.nodes[r.table[PICK + remote]]
    for name in ("w_key", "w_value"):
        loads[name].wait()
    pair = 2

    @pl.loop(0, blocks // pair)
    def _(i):
        here = pl.ds(i * pair, pair)
        there = pl.ds(nwide + i * pair, pair)
        block = flat(r.nodes[here])
        r.pool_k[there] = dot(block, r.w_key[...]).astype(BF).reshape(pair, BR, D)
        r.pool_v[there] = dot(block, r.w_value[...]).astype(BF).reshape(pair, BR, D)

    for name in ("virtual", "w_query"):
        loads[name].wait()
    virt = r.virtual[...]
    r.vq_bd[...] = block_diagonal(dot(virt, r.w_query[...])).astype(BF)
    r.vk_bd[...] = block_diagonal(dot(virt, r.w_key[...])).astype(BF)
    r.vv_bd[...] = block_diagonal(dot(virt, r.w_value[...])).astype(BF)

    expo = jnp.exp(SOFT_CAP * jnp.tanh(dot_nt(r.vq_bd[...], flat(r.pool_k[nwide:])) * IN_CAP))
    den = jnp.sum(expo, axis=1, keepdims=True)
    num = dot(expo.astype(BF), flat(r.pool_v[nwide:]))
    half = lanes((VIRT, 128)) // HEAD
    for h in range(HEADS):
        mine = slice(h * VIRT, (h + 1) * VIRT)
        two = num[mine, (h // 2) * 128 : (h // 2 + 1) * 128]
        r.f_part[h] = jnp.where(half == h % 2, two, jnp.broadcast_to(den[mine], (VIRT, 128)))
    small = sum_refs(at, r, "f_")
    small.first()
    for name in ("grad_out", "w_out", "grad_virtual"):
        loads[name].wait()

    @pl.loop(0, blocks // pair)
    def _(i):
        here = pl.ds(i * pair, pair)
        out_rows = pl.ds(pl.multiple_of(i * pair * BR, pair * BR), pair * BR)
        r.queries[here] = dot(flat(r.nodes[here]), r.w_query[...]).astype(BF).reshape(pair, BR, D)
        da = dot_nt(r.grad_out[out_rows, :], r.w_out[...])
        r.d_attended[here] = da.astype(BF).reshape(pair, BR, D)

    small.second()

    def project_far(first):
        here = slice(first, first + 4)
        for slot in range(first, min(first + 4, nwide - 1)):
            copies[slot].wait_recv()
        landed = flat(r.far[here])
        r.pool_k[here] = dot(landed, r.w_key[...]).astype(BF).reshape(4, BR, D)
        r.pool_v[here] = dot(landed, r.w_value[...]).astype(BF).reshape(4, BR, D)

    send(early, remote)
    groups = list(range(0, nwide, 4))
    project_far(groups[0])
    small.third()
    for first in groups[1:2]:
        project_far(first)
    small.finish()
    virtual_phase(at, r)
    for first in groups[2:]:
        project_far(first)
    for copy in copies:
        copy.wait_send()


def virtual_phase(at, r):
    nwide = at.nwide
    blocks = r.nodes.shape[0]
    pair = 2
    half = lanes((VIRT, 128)) // HEAD
    low = half == 0
    numbers, denoms = [], []
    for j in range(HEADS // 2):
        even, odd = r.f_summed[2 * j], r.f_summed[2 * j + 1]
        numbers.append(jnp.where(low, even, odd))
        denoms.append(pltpu.roll(jnp.where(low, odd, even), HEAD, 1))
    vnum = jnp.concatenate(numbers, axis=1)
    vden = jnp.concatenate(denoms, axis=1)
    summary = vnum / vden
    summary_b = summary.astype(BF)
    zeta = dot(summary_b, r.w_out[...])
    radius = jnp.sqrt(jnp.mean(zeta * zeta, axis=1, keepdims=True) + EPSILON)
    r.out_virtual[...] = zeta / radius
    gv = r.grad_virtual[...]
    dzeta = gv / radius - zeta * jnp.sum(gv * zeta, axis=1, keepdims=True) / (
        D * radius * radius * radius
    )
    dzeta_b = dzeta.astype(BF)
    r.summary_out[...] = summary_b
    r.dzeta_out[...] = dzeta_b
    dsummary = dot_nt(dzeta_b, r.w_out[...])
    r.dnum_bd[...] = block_diagonal((dsummary / vden).astype(BF).astype(F32)).astype(BF)
    along = dsummary * summary
    for h in range(HEADS):
        lane_tile = slice((h // 2) * 128, (h // 2 + 1) * 128)
        mine = jnp.where(half == h % 2, along[:, lane_tile], 0.0)
        down = -jnp.sum(mine, axis=1, keepdims=True)
        den_h = denoms[h // 2][:, (h % 2) * HEAD : (h % 2) * HEAD + 1]
        r.dden[h * VIRT : (h + 1) * VIRT, :] = jnp.broadcast_to(down / den_h, (VIRT, 128))

    r.vq_part[...] = jnp.zeros_like(r.vq_part)
    vq, dn = r.vq_bd[...], r.dnum_bd[...]

    @pl.loop(0, blocks // pair)
    def _(i):
        here = pl.ds(i * pair, pair)
        there = pl.ds(nwide + i * pair, pair)
        own_k, own_v = flat(r.pool_k[there]), flat(r.pool_v[there])
        bend = jnp.tanh(dot_nt(vq, own_k) * IN_CAP)
        expo = jnp.exp2(EXP_CAP * bend)
        dexpo = dot_nt(dn, own_v) + r.dden[:, 0:1]
        ds = (expo * dexpo * (1.0 - bend * bend)).astype(BF)
        r.vq_part[...] += diagonal_rows(dot(ds, own_k)) * SCALE
        r.base_k[here] = dot_tn(ds, vq).reshape(pair, BR, D)
        r.base_v[here] = dot_tn(expo.astype(BF), dn).reshape(pair, BR, D)


def attend_phase(at, r):
    blocks = r.nodes.shape[0]
    gw = GROUP * HEAD
    step = 32
    r.acc_vk[...] = jnp.zeros_like(r.acc_vk)
    r.acc_vv[...] = jnp.zeros_like(r.acc_vv)
    lane_head = lanes((BR, HM)) // VIRT
    half = lanes((BR, 128)) // HEAD

    def block(b, carry):
        live = [None, None]
        for t in range(KMAX):
            place = r.table[PLACE + b * KMAX + t]
            r.kcat[t * BR : (t + 1) * BR, :] = r.pool_k[place]
            r.vcat[t * BR : (t + 1) * BR, :] = r.pool_v[place]
            if t >= 2:
                live.append(r.table[LIVE + b * KMAX + t].astype(F32))
        q = r.queries[b]
        da = r.d_attended[b]
        bend_v = jnp.tanh(dot_nt(q, r.vk_bd[...]) * IN_CAP)
        expo_v = jnp.exp2(EXP_CAP * bend_v)
        dprob_v = dot_nt(da, r.vv_bd[...])
        probs_v = jnp.zeros((BR, HM), F32)
        delta_v = jnp.zeros((BR, HM), F32)
        for g in range(HEADS // GROUP):
            wide = slice(g * gw, (g + 1) * gw)
            at_tile = [(b * KMAX + t) * 2 + g for t in range(KMAX)]
            r.scores[...] = dot_nt(stacked(q[:, wide]), r.kcat[:, wide])
            r.dprob[...] = dot_nt(stacked(da[:, wide]), r.vcat[:, wide])
            for h in range(GROUP):
                head = g * GROUP + h
                virt_sum = jnp.sum(jnp.where(lane_head == head, expo_v, 0.0), axis=1, keepdims=True)
                inverses = []
                for first in range(0, BR, step):
                    here = slice(h * BR + first, h * BR + first + step)
                    bends, expos = [], []
                    total = None
                    for t in range(KMAX):
                        bend = jnp.tanh(r.scores[here, t * BR : (t + 1) * BR] * IN_CAP)
                        expo = jnp.exp2(EXP_CAP * bend)
                        if live[t] is not None:
                            expo = expo * live[t]
                        bends.append(bend)
                        expos.append(expo)
                        total = expo if total is None else total + expo
                    total = jnp.sum(total, axis=1, keepdims=True) + virt_sum[first : first + step]
                    inverse = 1.0 / total
                    inverses.append(inverse)
                    for t in range(KMAX):
                        weight = expos[t] * inverse
                        r.probs[at_tile[t], here, :] = weight.astype(BF)
                        r.scores[here, t * BR : (t + 1) * BR] = weight * (1.0 - bends[t] * bends[t])
                probs_v = jnp.where(lane_head == head, expo_v * jnp.concatenate(inverses, axis=0), probs_v)
            pv = probs_v.astype(BF)
            probs = jnp.concatenate([r.probs[i] for i in at_tile], axis=1)
            mixed = unstacked(dot(probs, r.vcat[:, wide])) + dot(pv, r.vv_bd[:, wide])
            mixed_b = mixed.astype(BF)
            r.attended[b, :, wide] = mixed_b
            along = da[:, wide].astype(F32) * mixed_b.astype(F32)
            for h in range(GROUP):
                head = g * GROUP + h
                lane_tile = slice((h // 2) * 128, (h // 2 + 1) * 128)
                delta = jnp.sum(jnp.where(half == h % 2, along[:, lane_tile], 0.0), axis=1, keepdims=True)
                delta_v = jnp.where(lane_head == head, delta, delta_v)
                for first in range(0, BR, step):
                    here = slice(h * BR + first, h * BR + first + step)
                    for t in range(KMAX):
                        at_lanes = slice(t * BR, (t + 1) * BR)
                        r.dscore[at_tile[t], here, :] = (
                            r.scores[here, at_lanes] * (r.dprob[here, at_lanes] - delta[first : first + step])
                        ).astype(BF)
            ds_v = (probs_v * (dprob_v - delta_v) * (1.0 - bend_v * bend_v)).astype(BF)
            dscore = jnp.concatenate([r.dscore[i] for i in at_tile], axis=1)
            dq = unstacked(dot(dscore, r.kcat[:, wide])) + dot(ds_v, r.vk_bd[:, wide])
            r.dquery[b, :, wide] = (dq * SCALE).astype(BF)
        r.acc_vk[...] += dot_tn(ds_v, q)
        r.acc_vv[...] += dot_tn(pv, da)
        return carry

    lax.fori_loop(0, blocks, block, 0)
    r.vk_part[...] = diagonal_rows(r.acc_vk[...]) * SCALE
    r.vv_part[...] = diagonal_rows(r.acc_vv[...])
    r.sum_k[...] = jnp.zeros_like(r.sum_k)
    r.sum_v[...] = jnp.zeros_like(r.sum_v)
    r.base_k[blocks] = jnp.zeros((BR, D), F32)
    r.base_v[blocks] = jnp.zeros((BR, D), F32)


def reduce_phase(at, r, stores):
    nwide = at.nwide
    blocks = r.nodes.shape[0]
    rows = blocks * BR
    halfd = D // 2
    band = halfd // at.nx
    chunk = 4 * band // nwide
    gw = GROUP * HEAD

    for j, ref in enumerate((r.vq_part, r.vk_part, r.vv_part)):
        for lt in range(D // 128):
            tile = ref[:, lt * 128 : (lt + 1) * 128]
            if j == 0:
                r.b_part[2 * lt, 0:16] = tile
            elif j == 1:
                r.b_part[2 * lt, 16:24] = tile[0:8]
                r.b_part[2 * lt + 1, 0:8] = tile[8:16]
            else:
                r.b_part[2 * lt + 1, 8:24] = tile
    small = sum_refs(at, r, "b_")
    small.first()

    def entry(based, position, carry):
        i = r.table[ORDER + position]
        joins = r.table[JOINS + position].astype(F32)
        q, da = r.queries[i // KMAX], r.d_attended[i // KMAX]
        if based:
            base = jnp.where(r.table[PLACE + i] >= nwide, r.table[PLACE + i] - nwide, blocks)
            base_k, base_v = r.base_k[base], r.base_v[base]
        for g in range(HEADS // GROUP):
            wide = slice(g * gw, (g + 1) * gw)
            dk = dot_tn(r.dscore[i * 2 + g], stacked(q[:, wide]))
            dv = dot_tn(r.probs[i * 2 + g], stacked(da[:, wide]))
            total_k = joins * r.sum_k[:, wide] + dk
            total_v = joins * r.sum_v[:, wide] + dv
            if based:
                total_k = total_k + (1.0 - joins) * base_k[:, wide]
                total_v = total_v + (1.0 - joins) * base_v[:, wide]
            r.sum_k[:, wide] = total_k
            r.sum_v[:, wide] = total_v
            r.run_k[position, :, wide] = (total_k * SCALE).astype(BF)
            r.run_v[position, :, wide] = total_v.astype(BF)
        return carry

    def entries(first, last):
        middle = min(max(first, nwide), last)
        if middle > first:
            lax.fori_loop(first, middle, functools.partial(entry, False), 0)
        if last > middle:
            lax.fori_loop(middle, last, functools.partial(entry, True), 0)

    own_rows = pl.ds(pl.multiple_of(at.c * halfd, halfd), halfd)
    sib_rows = pl.ds(pl.multiple_of((1 - at.c) * halfd, halfd), halfd)
    sibling = {"narrow": at.x * 2 + 1 - at.c}
    x_steps = sorted(range(1, at.nx), key=lambda step: -min(step, at.nx - step))
    per = halfd // BR

    def grad_half(g, which):
        if g == 0:
            return dot_tn(flat(r.attended[:, :, which]), r.grad_out[...])
        if g == 1:
            return dot_tn(flat(r.nodes[:, :, which]), flat(r.dquery[...]))
        parts = r.pool_k if g == 2 else r.pool_v
        total = dot_tn(flat(r.nodes[:, :, which]), flat(parts[nwide:]))
        for first in range(0, nwide, 8):
            here = slice(first, min(first + 8, nwide))
            total = total + dot_tn(flat(r.far[here, :, which]), flat(parts[here]))
        return total

    sib_copies, x_copies = [], {}

    def kept(g):
        return (r.scores, r.dprob)[g // 2].at[(g % 2) * halfd : (g % 2 + 1) * halfd]

    def leaving(g):
        return (r.kcat, r.vcat)[g // 2].at[(g % 2) * halfd : (g % 2 + 1) * halfd]

    def x_stage(g):
        sib_copies[g].wait_recv()
        mine = slice(per * g, per * g + per)
        total = kept(g)[...] + flat(r.sib_recv[mine]).astype(F32)
        kept(g)[...] = total
        leaving(g)[...] = total.astype(BF)
        for step in x_steps:
            peer = (at.x + step) % at.nx
            x_copies[g, step] = push(
                leaving(g).at[pl.ds(pl.multiple_of(peer * band, band), band)],
                r.x_recv.at[g, step - 1],
                r.x_sems.at[g, 0, step],
                r.x_sems.at[g, 1, step],
                {"narrow": peer * 2 + at.c},
            )

    def gradient_across(g):
        mine = slice(per * g, per * g + per)
        r.sib_send[mine] = grad_half(g, sib_rows).astype(BF).reshape(per, BR, D)
        sib_copies.append(
            push(
                r.sib_send.at[mine],
                r.sib_recv.at[mine],
                r.sib_sems.at[0, g],
                r.sib_sems.at[1, g],
                sibling,
            )
        )

    def gradient_here(g):
        kept(g)[...] = grad_half(g, own_rows)

    slack = blocks * KMAX - blocks - nwide
    returns = []
    reached = 0
    groups = list(range(0, nwide, 4))
    for first in groups:
        until = slack + first + 4
        entries(reached, until)
        reached = until
        for place in range(first, first + 4):
            end = r.table[END + place]
            r.pool_k[place] = r.run_k[end]
            r.pool_v[place] = r.run_v[end]
        here = slice(first, first + 4)
        part = dot_nt(flat(r.pool_k[here]), r.w_key[...]) + dot_nt(flat(r.pool_v[here]), r.w_value[...])
        r.stage[here] = part.astype(BF).reshape(4, BR, D)
        for slot in range(first, min(first + 4, nwide - 1)):
            returns.append(
                push(
                    r.stage.at[slot],
                    r.back.at[slot],
                    r.back_sems.at[0, slot],
                    r.back_sems.at[1, slot],
                    {"wide": at.behind(slot)},
                )
            )
        if first == groups[0]:
            small.second()
        if first == groups[min(1, len(groups) - 1)]:
            gradient_across(0)
            gradient_across(1)
            gradient_here(0)
            x_stage(0)
            gradient_here(1)
            x_stage(1)
    stores.start(r.stage.at[nwide - 1], r.back_hbm.at[nwide - 1])
    entries(reached, blocks * KMAX)
    for own in range(blocks):
        end = r.table[END + nwide + own]
        has = r.table[HAS + nwide + own] > 0
        r.pool_k[nwide + own] = jnp.where(has, r.run_k[end], (r.base_k[own] * SCALE).astype(BF))
        r.pool_v[nwide + own] = jnp.where(has, r.run_v[end], r.base_v[own].astype(BF))

    gradient_across(2)
    gradient_here(2)
    gradient_across(3)
    x_stage(2)
    gradient_here(3)
    x_stage(3)
    small.third()
    pair = 2

    @pl.loop(0, blocks // pair)
    def _(i):
        here = pl.ds(i * pair, pair)
        there = pl.ds(nwide + i * pair, pair)
        total = (
            dot_nt(flat(r.dquery[here]), r.w_query[...])
            + dot_nt(flat(r.pool_k[there]), r.w_key[...])
            + dot_nt(flat(r.pool_v[there]), r.w_value[...])
        )
        r.base_v[here] = total.reshape(pair, BR, D)

    stores.start(r.base_v.at[0:blocks], r.local_hbm)

    spot = at.x * band
    for g in range(4):
        total = kept(g)[pl.ds(pl.multiple_of(spot, band), band), :]
        for step in x_steps:
            x_copies[g, step].wait()
            total = total + r.x_recv[g, step - 1].astype(F32)
        r.base_k[g * band // BR, g * band % BR : g * band % BR + band, :] = total
        r.w_send[g * band : (g + 1) * band, :] = total.astype(BF)

    w_copies = []
    for slot in range(nwide - 1):
        peer = at.ahead(slot)
        w_copies.append(
            push(
                r.w_send.at[pl.ds(pl.multiple_of(peer * chunk, chunk), chunk)],
                r.w_recv.at[slot],
                r.w_sems.at[0, slot],
                r.w_sems.at[1, slot],
                {"wide": peer},
            )
        )

    @pl.loop(0, blocks // pair)
    def _(i):
        here = pl.ds(i * pair, pair)
        out = dot(flat(r.attended[here]), r.w_out[...])
        r.attended[here] = out.astype(BF).reshape(pair, BR, D)

    stores.start(r.attended, r.out_nodes_hbm)

    spot = at.w * chunk
    total = r.base_k[spot // BR, pl.ds(pl.multiple_of(spot % BR, chunk), chunk), :]
    for slot in range(nwide - 1):
        w_copies[slot].wait_recv()
        total = total + r.w_recv[slot].astype(F32)
    done = total.astype(BF)
    r.lower[at.n, at.w] = done[:, 0:halfd]
    r.upper[at.c, at.w, at.x] = done[:, halfd:]
    up_first, low_first = [], []
    for step in x_steps:
        up_first.append(
            push(
                r.upper.at[at.c, at.w, at.x],
                r.upper.at[at.c, at.w, at.x],
                r.up_sems.at[0, 0, step],
                r.up_sems.at[0, 1, step],
                {"narrow": (at.x + step) % at.nx * 2 + at.c},
            )
        )
    for slot in range(nwide - 1):
        low_first.append(
            push(
                r.lower.at[at.n, at.w],
                r.lower.at[at.n, at.w],
                r.low_sems.at[0, 0, slot],
                r.low_sems.at[0, 1, slot],
                {"wide": at.ahead(slot)},
            )
        )
    small.finish()
    r.virt_sums[...] = r.b_summed[...]
    for copy in up_first:
        copy.wait_recv()
    up_second, low_second, across = [], {}, []
    for slot in range(nwide - 1):
        up_second.append(
            push(
                r.upper.at[at.c, at.w],
                r.upper.at[at.c, at.w],
                r.up_sems.at[1, 0, slot],
                r.up_sems.at[1, 1, slot],
                {"wide": at.ahead(slot)},
            )
        )
    for copy in low_first:
        copy.wait_recv()
    for step in x_steps:
        low_second[step] = push(
            r.lower.at[at.n],
            r.lower.at[at.n],
            r.low_sems.at[1, 0, step],
            r.low_sems.at[1, 1, step],
            {"narrow": (at.x + step) % at.nx * 2 + at.c},
        )

    def low_across(landed, step):
        across.append(
            push(
                r.lower.at[landed],
                r.lower.at[landed],
                r.across_sems.at[0, 0, step],
                r.across_sems.at[0, 1, step],
                sibling,
            )
        )

    def up_across(slot):
        landed = at.behind(slot)
        across.append(
            push(
                r.upper.at[at.c, landed],
                r.upper.at[at.c, landed],
                r.across_sems.at[1, 0, slot],
                r.across_sems.at[1, 1, slot],
                sibling,
            )
        )

    low_across(at.n, 0)
    up_across(nwide - 1)
    for slot in range(nwide - 1):
        returns[slot].wait_recv()
        stores.start(r.back.at[slot], r.back_hbm.at[slot])
    for slot in range(nwide - 1):
        up_second[slot].wait_recv()
        up_across(slot)
    for step in x_steps:
        low_second[step].wait_recv()
        low_across((at.x + at.nx - step) % at.nx * 2 + at.c, step)
    for copy in across:
        copy.wait()
    stores.start(r.lower, r.lower_hbm)
    stores.start(r.upper, r.upper_hbm)
    for copy in returns + w_copies + sib_copies + up_first + low_first + up_second:
        copy.wait_send()
    for copy in low_second.values():
        copy.wait_send()


LOADED = ("nodes", "w_key", "w_value", "virtual", "w_query", "grad_out", "w_out", "grad_virtual")


def layer_kernel(nwide, nnarrow, names, *refs):
    r = types.SimpleNamespace(**dict(zip(names, refs, strict=True)))
    at = Place(nwide, nnarrow)
    at.greet()
    started = Copies(r.load_sems)
    loads = {name: started.start(getattr(r, name + "_hbm"), getattr(r, name)) for name in LOADED}
    stores = Copies(r.store_sems)
    exchange_phase(at, r, loads)
    attend_phase(at, r)
    reduce_phase(at, r, stores)
    for copy in stores.started:
        copy.wait()


def layer(nwide, nnarrow, table, arrays):
    blocks = arrays["nodes"].shape[0]
    rows = blocks * BR
    pool = blocks + nwide
    entries = blocks * KMAX
    nx = nnarrow // 2
    band = D // 2 // nx
    chunk = 4 * band // nwide
    per = 8 // nnarrow
    sems = pltpu.SemaphoreType.DMA
    most = max(nwide, nnarrow)
    shape = jax.ShapeDtypeStruct
    outs = {
        "out_nodes_hbm": shape((blocks, BR, D), BF),
        "local_hbm": shape((blocks, BR, D), F32),
        "back_hbm": shape((nwide, BR, D), BF),
        "lower_hbm": shape((nnarrow, nwide, chunk, D // 2), BF),
        "upper_hbm": shape((2, nwide, nx, chunk, D // 2), BF),
        "virt_sums": shape((8, 24, 128), F32),
        "out_virtual": shape((VIRT, D), F32),
        "summary_out": shape((VIRT, D), BF),
        "dzeta_out": shape((VIRT, D), BF),
    }
    vmem = {name: (arrays[name].shape, arrays[name].dtype) for name in LOADED}
    vmem |= {
        "stage": ((nwide, BR, D), BF),
        "far": ((nwide, BR, D), BF),
        "queries": ((blocks, BR, D), BF),
        "d_attended": ((blocks, BR, D), BF),
        "attended": ((blocks, BR, D), BF),
        "dquery": ((blocks, BR, D), BF),
        "pool_k": ((pool, BR, D), BF),
        "pool_v": ((pool, BR, D), BF),
        "vq_bd": ((HM, D), BF),
        "vk_bd": ((HM, D), BF),
        "vv_bd": ((HM, D), BF),
        "dnum_bd": ((HM, D), BF),
        "dden": ((HM, 128), F32),
        "vq_part": ((VIRT, D), F32),
        "vk_part": ((VIRT, D), F32),
        "vv_part": ((VIRT, D), F32),
        "acc_vk": ((HM, D), F32),
        "acc_vv": ((HM, D), F32),
        "base_k": ((blocks + 1, BR, D), F32),
        "base_v": ((blocks + 1, BR, D), F32),
        "kcat": ((KMAX * BR, D), BF),
        "vcat": ((KMAX * BR, D), BF),
        "scores": ((GROUP * BR, KMAX * BR), F32),
        "dprob": ((GROUP * BR, KMAX * BR), F32),
        "probs": ((entries * 2, GROUP * BR, BR), BF),
        "dscore": ((entries * 2, GROUP * BR, BR), BF),
        "sum_k": ((BR, D), F32),
        "sum_v": ((BR, D), F32),
        "run_k": ((entries, BR, D), BF),
        "run_v": ((entries, BR, D), BF),
        "back": ((nwide, BR, D), BF),
        "sib_send": ((4 * (D // 2 // BR), BR, D), BF),
        "sib_recv": ((4 * (D // 2 // BR), BR, D), BF),
        "x_recv": ((4, nx - 1, band, D), BF),
        "w_send": ((4 * band, D), BF),
        "w_recv": ((nwide, chunk, D), BF),
        "lower": (outs["lower_hbm"].shape, BF),
        "upper": (outs["upper_hbm"].shape, BF),
    }
    for name, height in (("f_", VIRT), ("b_", 24)):
        vmem |= {
            name + "part": ((8, height, 128), F32),
            name + "one": ((nnarrow, per, height, 128), F32),
            name + "mid": ((per, height, 128), F32),
            name + "two": ((nwide, per, height, 128), F32),
            name + "summed": ((8, height, 128), F32),
        }
    sem_shapes = {
        "f_sems": (3, 2, most),
        "b_sems": (3, 2, most),
        "send_sems": (nwide,),
        "recv_sems": (nwide,),
        "back_sems": (2, nwide),
        "sib_sems": (2, 4),
        "x_sems": (4, 2, nx),
        "w_sems": (2, nwide),
        "low_sems": (2, 2, nwide),
        "up_sems": (2, 2, nwide),
        "across_sems": (2, 2, nwide),
        "load_sems": (len(LOADED),),
        "store_sems": (nwide + 4,),
    }
    names = (
        ["table"] + [name + "_hbm" for name in LOADED] + list(outs) + list(vmem) + list(sem_shapes)
    )
    results = pl.pallas_call(
        functools.partial(layer_kernel, nwide, nnarrow, names),
        out_shape=list(outs.values()),
        in_specs=[SMEM] + [ANY] * len(LOADED),
        out_specs=[ANY] * 5 + [VMEM] * 4,
        scratch_shapes=[pltpu.VMEM(*kind) for kind in vmem.values()]
        + [sems(kind) for kind in sem_shapes.values()],
        compiler_params=pltpu.CompilerParams(
            collective_id=0, has_side_effects=True, vmem_limit_bytes=VMEM_LIMIT
        ),
        name="layer",
    )(table, *[arrays[name] for name in LOADED])
    return dict(zip(outs, results))


def finish_kernel(
    nwide,
    nnarrow,
    table,
    local_hbm,
    back_hbm,
    lower_hbm,
    upper_hbm,
    out_nodes_in,
    virt_sums,
    virtual,
    summary_b,
    dzeta_b,
    out_virtual_in,
    w_query_hbm,
    w_key_hbm,
    w_value_hbm,
    out_nodes,
    grad_nodes_hbm,
    grad_query_hbm,
    grad_key_hbm,
    grad_value_hbm,
    grad_wout_hbm,
    out_virtual,
    virtual_grad,
    lower,
    upper,
    back,
    grad_nodes,
    grads,
    w_query,
    w_key,
    w_value,
    out_rows,
    load_sems,
    store_sems,
):
    at = Place(nwide, nnarrow)
    started, stores = Copies(load_sems), Copies(store_sems)
    load_local = started.start(local_hbm, grad_nodes)
    load_back = started.start(back_hbm, back)
    load_out = started.start(out_nodes_in, out_rows)
    load_low = started.start(lower_hbm, lower)
    load_up = started.start(upper_hbm, upper)
    load_w = [
        started.start(src, dst)
        for src, dst in ((w_query_hbm, w_query), (w_key_hbm, w_key), (w_value_hbm, w_value))
    ]
    out_virtual[...] = out_virtual_in[...]
    load_local.wait()
    load_back.wait()
    for slot in range(nwide):
        grad_nodes[table[PICK + slot]] += back[slot].astype(F32)
    stores.start(grad_nodes, grad_nodes_hbm)
    load_out.wait()
    stores.start(out_rows, out_nodes)
    top = jnp.concatenate([virt_sums[2 * lt] for lt in range(D // 128)], axis=1)
    bottom = jnp.concatenate([virt_sums[2 * lt + 1] for lt in range(D // 128)], axis=1)
    vq_grad = top[0:16].astype(BF)
    vk_grad = jnp.concatenate([top[16:24], bottom[0:8]], axis=0).astype(BF)
    vv_grad = bottom[8:24].astype(BF)
    halfd = D // 2
    band = halfd // at.nx
    chunk = 4 * band // nwide
    pairs = (
        (grad_wout_hbm, summary_b[...], dzeta_b[...]),
        (grad_query_hbm, virtual[...], vq_grad),
        (grad_key_hbm, virtual[...], vk_grad),
        (grad_value_hbm, virtual[...], vv_grad),
    )
    per = nwide // 4
    load_low.wait()
    load_up.wait()
    for g, (out, left, right) in enumerate(pairs):
        grads[g] = dot_tn(left, right)
        for n in range(nnarrow):
            first = (n % 2) * halfd + (n // 2) * band
            for j in range(per):
                here = slice(first + j * chunk, first + (j + 1) * chunk)
                grads[g, here, 0:halfd] += lower[n, g * per + j].astype(F32)
                grads[g, here, halfd:] += upper[n % 2, g * per + j, n // 2].astype(F32)
        stores.start(grads.at[g], out)
    for copy in load_w:
        copy.wait()
    virtual_grad[...] = (
        dot_nt(vq_grad, w_query[...]) + dot_nt(vk_grad, w_key[...]) + dot_nt(vv_grad, w_value[...])
    )
    for copy in stores.started:
        copy.wait()


def finish(nwide, nnarrow, table, got, arrays):
    shape = jax.ShapeDtypeStruct
    outs = (
        [shape(got["out_nodes_hbm"].shape, BF), shape(got["local_hbm"].shape, F32)]
        + [shape((D, D), F32)] * 4
        + [shape((VIRT, D), F32)] * 2
    )
    scratch = [(got[name].shape, got[name].dtype) for name in ("lower_hbm", "upper_hbm", "back_hbm", "local_hbm")]
    scratch += [((4, D, D), F32)] + [((D, D), BF)] * 3
    scratch += [(got["out_nodes_hbm"].shape, BF)]
    return pl.pallas_call(
        functools.partial(finish_kernel, nwide, nnarrow),
        out_shape=outs,
        in_specs=[SMEM] + [ANY] * 5 + [VMEM] * 5 + [ANY] * 3,
        out_specs=[ANY] * 6 + [VMEM] * 2,
        scratch_shapes=[pltpu.VMEM(*kind) for kind in scratch]
        + [pltpu.SemaphoreType.DMA((8,)), pltpu.SemaphoreType.DMA((6,))],
        compiler_params=pltpu.CompilerParams(vmem_limit_bytes=VMEM_LIMIT),
        name="finish",
    )(
        table,
        *[got[name] for name in ("local_hbm", "back_hbm", "lower_hbm", "upper_hbm", "out_nodes_hbm", "virt_sums")],
        arrays["virtual"],
        *[got[name] for name in ("summary_out", "dzeta_out", "out_virtual")],
        arrays["w_query"],
        arrays["w_key"],
        arrays["w_value"],
    )


def shards(
    nwide,
    nnarrow,
    nodes,
    virtual,
    w_query,
    w_key,
    w_value,
    w_out,
    col_blocks,
    col_count,
    send_sel,
    grad_out,
    grad_virtual,
):
    rows = nodes.shape[0]
    arrays = {
        "nodes": nodes.reshape(rows // BR, BR, D),
        "w_key": w_key,
        "w_value": w_value,
        "virtual": virtual,
        "w_query": w_query,
        "grad_out": grad_out,
        "w_out": w_out,
        "grad_virtual": grad_virtual,
    }
    table = tables(nwide, nnarrow, col_blocks.T, col_count, send_sel)
    got = layer(nwide, nnarrow, table, arrays)
    out_nodes, grad_nodes, grad_query, grad_key, grad_value, grad_wout, out_virtual, virtual_grad = finish(
        nwide, nnarrow, table, got, arrays
    )
    return (
        out_nodes.reshape(rows, D),
        out_virtual,
        grad_nodes.reshape(rows, D),
        virtual_grad,
        grad_query,
        grad_key,
        grad_value,
        grad_wout,
    )


def solution(mesh):
    spread = P(("wide", "narrow"), None)
    in_specs = (
        spread,
        P(),
        P(),
        P(),
        P(),
        P(),
        spread,
        P(("wide", "narrow")),
        P("wide", "narrow", None),
        spread,
        P(),
    )
    out_specs = (spread, P(), spread, P(), P(), P(), P(), P())
    return jax.shard_map(
        functools.partial(shards, mesh.shape["wide"], mesh.shape["narrow"]),
        mesh=mesh,
        in_specs=in_specs,
        out_specs=out_specs,
        check_vma=False,
    )
```

```python
import functools
import math
import types

import jax
import jax.numpy as jnp
from jax import lax
from jax.experimental import pallas as pl
from jax.experimental.pallas import tpu as pltpu
from jax.sharding import PartitionSpec as P

D = 512
HEADS = 8
VIRT = 16
BR = 128
HEAD = D // HEADS
HM = HEADS * VIRT
SCALE = HEAD ** (-0.5)
SOFT_CAP = 5.0
EPSILON = 1e-06
IN_CAP = SCALE / SOFT_CAP
EXP_CAP = SOFT_CAP * math.log2(math.e)
BF = jnp.bfloat16
F32 = jnp.float32
MESH = pl.DeviceIdType.MESH
VMEM = pl.BlockSpec(memory_space=pltpu.VMEM)
SMEM = pl.BlockSpec(memory_space=pltpu.SMEM)
ANY = pl.BlockSpec(memory_space=pl.ANY)
VMEM_LIMIT = 63 * 1024 * 1024
GROUP = 4


def ring_sizes(nwide):
    ny = 4 if nwide == 16 else 2
    return nwide // ny, ny


def shifts(nwide):
    nz, ny = ring_sizes(nwide)
    every = [(dz, dy) for dz in range(nz) for dy in range(ny)]
    hops = lambda s: min(s[0], nz - s[0]) + min(s[1], ny - s[1])
    return sorted(every[1:], key=lambda s: -hops(s)) + every[:1]


def dot(a, b):
    return lax.dot_general(a, b, (((1,), (0,)), ((), ())), preferred_element_type=F32)


def dot_nt(a, b):
    return lax.dot_general(a, b, (((1,), (1,)), ((), ())), preferred_element_type=F32)


def dot_tn(a, b):
    return lax.dot_general(a, b, (((0,), (0,)), ((), ())), preferred_element_type=F32)


def lanes(shape, axis=1):
    return lax.broadcasted_iota(jnp.int32, shape, axis)


class Place:
    def __init__(self, nwide, nnarrow):
        self.nwide, self.nnarrow = nwide, nnarrow
        self.nz, self.ny = ring_sizes(nwide)
        self.shifts = shifts(nwide)
        self.nx = nnarrow // 2
        self.w = lax.axis_index("wide")
        self.n = lax.axis_index("narrow")
        self.z, self.y = self.w // self.ny, self.w % self.ny
        self.x, self.c = self.n // 2, self.n % 2

    def ahead(self, slot):
        dz, dy = self.shifts[slot]
        return ((self.z + dz) % self.nz) * self.ny + (self.y + dy) % self.ny

    def behind(self, slot):
        dz, dy = self.shifts[slot]
        return ((self.z + self.nz - dz) % self.nz) * self.ny + (self.y + self.ny - dy) % self.ny

    def narrow_at(self, step):
        return (self.n + step) % self.nnarrow

    def greet(self):
        barrier = pltpu.get_barrier_semaphore()
        for slot in range(self.nwide - 1):
            pl.semaphore_signal(
                barrier, inc=1, device_id={"wide": self.ahead(slot)}, device_id_type=MESH
            )
        for step in range(1, self.nnarrow):
            pl.semaphore_signal(
                barrier, inc=1, device_id={"narrow": self.narrow_at(step)}, device_id_type=MESH
            )

    def meet(self):
        pl.semaphore_wait(pltpu.get_barrier_semaphore(), self.nwide + self.nnarrow - 2)


def push(src, dst, send, recv, device):
    copy = pltpu.make_async_remote_copy(
        src_ref=src, dst_ref=dst, send_sem=send, recv_sem=recv, device_id=device, device_id_type=MESH
    )
    copy.start()
    return copy


KMAX = 4
PAIRS = 32
ORDER, JOINS, PLACE, LIVE, END, HAS, PICK, TABLE = 0, 32, 64, 96, 128, 160, 192, 256


def tables_kernel(nwide, nnarrow, cols, counts, send_sel, slot_of, table, tally, following):
    at = Place(nwide, nnarrow)
    kmax, blocks = cols.shape
    dead = nwide + blocks

    def clear(i, carry):
        tally[i] = 0
        return carry

    lax.fori_loop(0, dead + 1, clear, 0, unroll=True)

    def enter(i, carry):
        b, t = i // kmax, i % kmax
        entry = cols[t, b]
        source = jnp.maximum(entry - blocks, 0)
        dz = (at.z + at.nz - source // at.ny) % at.nz
        dy = (at.y + at.ny - source % at.ny) % at.ny
        place = jnp.where(entry < blocks, nwide + entry, slot_of[dz * at.ny + dy])
        live = t < counts[b]
        table[PLACE + i] = place
        table[LIVE + i] = jnp.where(live, 1, 0)
        key = jnp.where(live, place, dead)
        tally[key] = tally[key] + 1
        return carry

    lax.fori_loop(0, blocks * kmax, enter, 0, unroll=True)

    def begin(p, start):
        number = tally[p]
        following[p] = start
        table[END + p] = jnp.maximum(start + number - 1, 0)
        table[HAS + p] = jnp.where(number > 0, 1, 0)
        tally[p] = start
        return start + number

    lax.fori_loop(0, dead + 1, begin, 0, unroll=True)

    def sort(i, carry):
        key = jnp.where(table[LIVE + i] > 0, table[PLACE + i], dead)
        position = following[key]
        following[key] = position + 1
        table[ORDER + position] = i
        table[JOINS + position] = jnp.where(position > tally[key], 1, 0)
        return carry

    lax.fori_loop(0, blocks * kmax, sort, 0, unroll=True)
    for slot in range(nwide):
        table[PICK + slot] = send_sel[0, 0, at.ahead(slot)]


def tables(nwide, nnarrow, cols, counts, send_sel):
    order = shifts(nwide)
    nz, ny = ring_sizes(nwide)
    slot_of = jnp.asarray([order.index((i // ny, i % ny)) for i in range(nwide)], jnp.int32)
    return pl.pallas_call(
        functools.partial(tables_kernel, nwide, nnarrow),
        out_shape=jax.ShapeDtypeStruct((TABLE,), jnp.int32),
        in_specs=[SMEM] * 4,
        out_specs=SMEM,
        scratch_shapes=[pltpu.SMEM((32,), jnp.int32), pltpu.SMEM((32,), jnp.int32)],
        name="tables",
    )(cols, counts, send_sel, slot_of)


class SmallSum:
    def __init__(self, place, part, one, mid, two, out, sems):
        self.place, self.part, self.one, self.mid, self.two, self.out = place, part, one, mid, two, out
        self.sems = sems
        self.per = part.shape[0] // place.nnarrow

    def first(self):
        at, per = self.place, self.per
        self.copies = []
        for step in range(1, at.nnarrow):
            peer = at.narrow_at(step)
            self.copies.append(
                push(
                    self.part.at[pl.ds(peer * per, per)],
                    self.one.at[at.n],
                    self.sems.at[0, 0, step],
                    self.sems.at[0, 1, step],
                    {"narrow": peer},
                )
            )
        self.one[at.n] = self.part[pl.ds(at.n * per, per)]

    def second(self):
        at = self.place
        for copy in self.copies:
            copy.wait()
        total = self.one[0]
        for j in range(1, at.nnarrow):
            total = total + self.one[j]
        self.mid[...] = total
        self.copies = []
        for slot in range(at.nwide - 1):
            self.copies.append(
                push(
                    self.mid,
                    self.two.at[at.w],
                    self.sems.at[1, 0, slot],
                    self.sems.at[1, 1, slot],
                    {"wide": at.ahead(slot)},
                )
            )
        self.two[at.w] = total

    def third(self):
        at, per = self.place, self.per
        for copy in self.copies:
            copy.wait()
        total = self.two[0]
        for j in range(1, at.nwide):
            total = total + self.two[j]
        self.out[pl.ds(at.n * per, per)] = total
        self.copies = []
        for step in range(1, at.nnarrow):
            self.copies.append(
                push(
                    self.out.at[pl.ds(at.n * per, per)],
                    self.out.at[pl.ds(at.n * per, per)],
                    self.sems.at[2, 0, step],
                    self.sems.at[2, 1, step],
                    {"narrow": at.narrow_at(step)},
                )
            )

    def finish(self):
        for copy in self.copies:
            copy.wait()


def block_diagonal(rows16):
    tiled = jnp.concatenate([rows16] * HEADS, axis=0)
    head_row = lanes((HM, D), 0) // VIRT
    head_col = lanes((HM, D), 1) // HEAD
    return jnp.where(head_row == head_col, tiled, jnp.zeros_like(tiled))


def diagonal_rows(full):
    head_col = lanes((VIRT, D), 1) // HEAD
    total = jnp.zeros((VIRT, D), F32)
    for h in range(HEADS):
        total = jnp.where(head_col == h, full[h * VIRT : (h + 1) * VIRT], total)
    return total


class Copies:
    def __init__(self, sems):
        self.sems, self.started = sems, []

    def start(self, src, dst):
        copy = pltpu.make_async_copy(src, dst, self.sems.at[len(self.started)])
        copy.start()
        self.started.append(copy)
        return copy


def sum_refs(at, r, name):
    return SmallSum(at, *[getattr(r, name + key) for key in ("part", "one", "mid", "two", "summed", "sems")])


def stacked(block):
    group_head = lanes(block.shape) // HEAD
    zero = jnp.zeros_like(block)
    return jnp.concatenate([jnp.where(group_head == h, block, zero) for h in range(GROUP)], axis=0)


def unstacked(full):
    rows = full.shape[0] // GROUP
    group_head = lanes((rows, full.shape[1])) // HEAD
    total = full[0:rows]
    for h in range(1, GROUP):
        total = jnp.where(group_head == h, full[h * rows : (h + 1) * rows], total)
    return total


def flat(value):
    return value.reshape(value.shape[0] * value.shape[1], value.shape[2])


def exchange_phase(at, r, loads):
    nwide = at.nwide
    blocks = r.nodes.shape[0]
    rows = blocks * BR
    loads["nodes"].wait()
    copies = []

    def send(first, last):
        for slot in range(first, last):
            copies.append(
                push(
                    r.stage.at[slot],
                    r.far.at[slot],
                    r.send_sems.at[slot],
                    r.recv_sems.at[slot],
                    {"wide": at.ahead(slot)},
                )
            )

    remote = nwide - 1
    early = min(4, remote)
    for slot in range(remote):
        r.stage[slot] = r.nodes[r.table[PICK + slot]]
    at.meet()
    send(0, early)
    r.far[remote] = r.nodes[r.table[PICK + remote]]
    for name in ("w_key", "w_value"):
        loads[name].wait()
    pair = 2

    @pl.loop(0, blocks // pair)
    def _(i):
        here = pl.ds(i * pair, pair)
        there = pl.ds(nwide + i * pair, pair)
        block = flat(r.nodes[here])
        r.pool_k[there] = dot(block, r.w_key[...]).astype(BF).reshape(pair, BR, D)
        r.pool_v[there] = dot(block, r.w_value[...]).astype(BF).reshape(pair, BR, D)

    for name in ("virtual", "w_query"):
        loads[name].wait()
    virt = r.virtual[...]
    r.vq_bd[...] = block_diagonal(dot(virt, r.w_query[...])).astype(BF)
    r.vk_bd[...] = block_diagonal(dot(virt, r.w_key[...])).astype(BF)
    r.vv_bd[...] = block_diagonal(dot(virt, r.w_value[...])).astype(BF)

    expo = jnp.exp(SOFT_CAP * jnp.tanh(dot_nt(r.vq_bd[...], flat(r.pool_k[nwide:])) * IN_CAP))
    den = jnp.sum(expo, axis=1, keepdims=True)
    num = dot(expo.astype(BF), flat(r.pool_v[nwide:]))
    half = lanes((VIRT, 128)) // HEAD
    for h in range(HEADS):
        mine = slice(h * VIRT, (h + 1) * VIRT)
        two = num[mine, (h // 2) * 128 : (h // 2 + 1) * 128]
        r.f_part[h] = jnp.where(half == h % 2, two, jnp.broadcast_to(den[mine], (VIRT, 128)))
    small = sum_refs(at, r, "f_")
    small.first()
    for name in ("grad_out", "w_out", "grad_virtual"):
        loads[name].wait()

    @pl.loop(0, blocks // pair)
    def _(i):
        here = pl.ds(i * pair, pair)
        out_rows = pl.ds(pl.multiple_of(i * pair * BR, pair * BR), pair * BR)
        r.queries[here] = dot(flat(r.nodes[here]), r.w_query[...]).astype(BF).reshape(pair, BR, D)
        da = dot_nt(r.grad_out[out_rows, :], r.w_out[...])
        r.d_attended[here] = da.astype(BF).reshape(pair, BR, D)

    small.second()

    def project_far(first):
        here = slice(first, first + 4)
        for slot in range(first, min(first + 4, nwide - 1)):
            copies[slot].wait_recv()
        landed = flat(r.far[here])
        r.pool_k[here] = dot(landed, r.w_key[...]).astype(BF).reshape(4, BR, D)
        r.pool_v[here] = dot(landed, r.w_value[...]).astype(BF).reshape(4, BR, D)

    send(early, remote)
    groups = list(range(0, nwide, 4))
    project_far(groups[0])
    small.third()
    for first in groups[1:2]:
        project_far(first)
    small.finish()
    virtual_phase(at, r)
    for first in groups[2:]:
        project_far(first)
    for copy in copies:
        copy.wait_send()


def virtual_phase(at, r):
    nwide = at.nwide
    blocks = r.nodes.shape[0]
    pair = 2
    half = lanes((VIRT, 128)) // HEAD
    low = half == 0
    numbers, denoms = [], []
    for j in range(HEADS // 2):
        even, odd = r.f_summed[2 * j], r.f_summed[2 * j + 1]
        numbers.append(jnp.where(low, even, odd))
        denoms.append(pltpu.roll(jnp.where(low, odd, even), HEAD, 1))
    vnum = jnp.concatenate(numbers, axis=1)
    vden = jnp.concatenate(denoms, axis=1)
    summary = vnum / vden
    summary_b = summary.astype(BF)
    zeta = dot(summary_b, r.w_out[...])
    radius = jnp.sqrt(jnp.mean(zeta * zeta, axis=1, keepdims=True) + EPSILON)
    r.out_virtual[...] = zeta / radius
    gv = r.grad_virtual[...]
    dzeta = gv / radius - zeta * jnp.sum(gv * zeta, axis=1, keepdims=True) / (
        D * radius * radius * radius
    )
    dzeta_b = dzeta.astype(BF)
    r.summary_out[...] = summary_b
    r.dzeta_out[...] = dzeta_b
    dsummary = dot_nt(dzeta_b, r.w_out[...])
    r.dnum_bd[...] = block_diagonal((dsummary / vden).astype(BF).astype(F32)).astype(BF)
    along = dsummary * summary
    for h in range(HEADS):
        lane_tile = slice((h // 2) * 128, (h // 2 + 1) * 128)
        mine = jnp.where(half == h % 2, along[:, lane_tile], 0.0)
        down = -jnp.sum(mine, axis=1, keepdims=True)
        den_h = denoms[h // 2][:, (h % 2) * HEAD : (h % 2) * HEAD + 1]
        r.dden[h * VIRT : (h + 1) * VIRT, :] = jnp.broadcast_to(down / den_h, (VIRT, 128))

    r.vq_part[...] = jnp.zeros_like(r.vq_part)
    vq, dn = r.vq_bd[...], r.dnum_bd[...]

    @pl.loop(0, blocks // pair)
    def _(i):
        here = pl.ds(i * pair, pair)
        there = pl.ds(nwide + i * pair, pair)
        own_k, own_v = flat(r.pool_k[there]), flat(r.pool_v[there])
        bend = jnp.tanh(dot_nt(vq, own_k) * IN_CAP)
        expo = jnp.exp2(EXP_CAP * bend)
        dexpo = dot_nt(dn, own_v) + r.dden[:, 0:1]
        ds = (expo * dexpo * (1.0 - bend * bend)).astype(BF)
        r.vq_part[...] += diagonal_rows(dot(ds, own_k)) * SCALE
        r.base_k[here] = dot_tn(ds, vq).reshape(pair, BR, D)
        r.base_v[here] = dot_tn(expo.astype(BF), dn).reshape(pair, BR, D)


def attend_phase(at, r):
    blocks = r.nodes.shape[0]
    gw = GROUP * HEAD
    step = 32
    r.acc_vk[...] = jnp.zeros_like(r.acc_vk)
    r.acc_vv[...] = jnp.zeros_like(r.acc_vv)
    lane_head = lanes((BR, HM)) // VIRT
    half = lanes((BR, 128)) // HEAD

    def block(b, carry):
        live = [None, None]
        for t in range(KMAX):
            place = r.table[PLACE + b * KMAX + t]
            r.kcat[t * BR : (t + 1) * BR, :] = r.pool_k[place]
            r.vcat[t * BR : (t + 1) * BR, :] = r.pool_v[place]
            if t >= 2:
                live.append(r.table[LIVE + b * KMAX + t].astype(F32))
        q = r.queries[b]
        da = r.d_attended[b]
        bend_v = jnp.tanh(dot_nt(q, r.vk_bd[...]) * IN_CAP)
        expo_v = jnp.exp2(EXP_CAP * bend_v)
        dprob_v = dot_nt(da, r.vv_bd[...])
        probs_v = jnp.zeros((BR, HM), F32)
        delta_v = jnp.zeros((BR, HM), F32)
        for g in range(HEADS // GROUP):
            wide = slice(g * gw, (g + 1) * gw)
            at_tile = [(b * KMAX + t) * 2 + g for t in range(KMAX)]
            r.scores[...] = dot_nt(stacked(q[:, wide]), r.kcat[:, wide])
            r.dprob[...] = dot_nt(stacked(da[:, wide]), r.vcat[:, wide])
            for h in range(GROUP):
                head = g * GROUP + h
                virt_sum = jnp.sum(jnp.where(lane_head == head, expo_v, 0.0), axis=1, keepdims=True)
                inverses = []
                for first in range(0, BR, step):
                    here = slice(h * BR + first, h * BR + first + step)
                    bends, expos = [], []
                    total = None
                    for t in range(KMAX):
                        bend = jnp.tanh(r.scores[here, t * BR : (t + 1) * BR] * IN_CAP)
                        expo = jnp.exp2(EXP_CAP * bend)
                        if live[t] is not None:
                            expo = expo * live[t]
                        bends.append(bend)
                        expos.append(expo)
                        total = expo if total is None else total + expo
                    total = jnp.sum(total, axis=1, keepdims=True) + virt_sum[first : first + step]
                    inverse = 1.0 / total
                    inverses.append(inverse)
                    for t in range(KMAX):
                        weight = expos[t] * inverse
                        r.probs[at_tile[t], here, :] = weight.astype(BF)
                        r.scores[here, t * BR : (t + 1) * BR] = weight * (1.0 - bends[t] * bends[t])
                probs_v = jnp.where(lane_head == head, expo_v * jnp.concatenate(inverses, axis=0), probs_v)
            pv = probs_v.astype(BF)
            probs = jnp.concatenate([r.probs[i] for i in at_tile], axis=1)
            mixed = unstacked(dot(probs, r.vcat[:, wide])) + dot(pv, r.vv_bd[:, wide])
            mixed_b = mixed.astype(BF)
            r.attended[b, :, wide] = mixed_b
            along = da[:, wide].astype(F32) * mixed_b.astype(F32)
            for h in range(GROUP):
                head = g * GROUP + h
                lane_tile = slice((h // 2) * 128, (h // 2 + 1) * 128)
                delta = jnp.sum(jnp.where(half == h % 2, along[:, lane_tile], 0.0), axis=1, keepdims=True)
                delta_v = jnp.where(lane_head == head, delta, delta_v)
                for first in range(0, BR, step):
                    here = slice(h * BR + first, h * BR + first + step)
                    for t in range(KMAX):
                        at_lanes = slice(t * BR, (t + 1) * BR)
                        r.dscore[at_tile[t], here, :] = (
                            r.scores[here, at_lanes] * (r.dprob[here, at_lanes] - delta[first : first + step])
                        ).astype(BF)
            ds_v = (probs_v * (dprob_v - delta_v) * (1.0 - bend_v * bend_v)).astype(BF)
            dscore = jnp.concatenate([r.dscore[i] for i in at_tile], axis=1)
            dq = unstacked(dot(dscore, r.kcat[:, wide])) + dot(ds_v, r.vk_bd[:, wide])
            r.dquery[b, :, wide] = (dq * SCALE).astype(BF)
        r.acc_vk[...] += dot_tn(ds_v, q)
        r.acc_vv[...] += dot_tn(pv, da)
        return carry

    lax.fori_loop(0, blocks, block, 0)
    r.vk_part[...] = diagonal_rows(r.acc_vk[...]) * SCALE
    r.vv_part[...] = diagonal_rows(r.acc_vv[...])
    r.sum_k[...] = jnp.zeros_like(r.sum_k)
    r.sum_v[...] = jnp.zeros_like(r.sum_v)
    r.base_k[blocks] = jnp.zeros((BR, D), F32)
    r.base_v[blocks] = jnp.zeros((BR, D), F32)


def reduce_phase(at, r, stores):
    nwide = at.nwide
    blocks = r.nodes.shape[0]
    rows = blocks * BR
    halfd = D // 2
    band = halfd // at.nx
    chunk = 4 * band // nwide
    gw = GROUP * HEAD

    for j, ref in enumerate((r.vq_part, r.vk_part, r.vv_part)):
        for lt in range(D // 128):
            tile = ref[:, lt * 128 : (lt + 1) * 128]
            if j == 0:
                r.b_part[2 * lt, 0:16] = tile
            elif j == 1:
                r.b_part[2 * lt, 16:24] = tile[0:8]
                r.b_part[2 * lt + 1, 0:8] = tile[8:16]
            else:
                r.b_part[2 * lt + 1, 8:24] = tile
    small = sum_refs(at, r, "b_")
    small.first()

    def entry(based, position, carry):
        i = r.table[ORDER + position]
        joins = r.table[JOINS + position].astype(F32)
        q, da = r.queries[i // KMAX], r.d_attended[i // KMAX]
        if based:
            base = jnp.where(r.table[PLACE + i] >= nwide, r.table[PLACE + i] - nwide, blocks)
            base_k, base_v = r.base_k[base], r.base_v[base]
        for g in range(HEADS // GROUP):
            wide = slice(g * gw, (g + 1) * gw)
            dk = dot_tn(r.dscore[i * 2 + g], stacked(q[:, wide]))
            dv = dot_tn(r.probs[i * 2 + g], stacked(da[:, wide]))
            total_k = joins * r.sum_k[:, wide] + dk
            total_v = joins * r.sum_v[:, wide] + dv
            if based:
                total_k = total_k + (1.0 - joins) * base_k[:, wide]
                total_v = total_v + (1.0 - joins) * base_v[:, wide]
            r.sum_k[:, wide] = total_k
            r.sum_v[:, wide] = total_v
            r.run_k[position, :, wide] = (total_k * SCALE).astype(BF)
            r.run_v[position, :, wide] = total_v.astype(BF)
        return carry

    def entries(first, last):
        middle = min(max(first, nwide), last)
        if middle > first:
            lax.fori_loop(first, middle, functools.partial(entry, False), 0, unroll=2)
        if last > middle:
            lax.fori_loop(middle, last, functools.partial(entry, True), 0, unroll=2)

    own_rows = pl.ds(pl.multiple_of(at.c * halfd, halfd), halfd)
    sib_rows = pl.ds(pl.multiple_of((1 - at.c) * halfd, halfd), halfd)
    sibling = {"narrow": at.x * 2 + 1 - at.c}
    x_steps = sorted(range(1, at.nx), key=lambda step: -min(step, at.nx - step))
    per = halfd // BR

    def grad_half(g, which):
        if g == 0:
            return dot_tn(flat(r.attended[:, :, which]), r.grad_out[...])
        if g == 1:
            return dot_tn(flat(r.nodes[:, :, which]), flat(r.dquery[...]))
        parts = r.pool_k if g == 2 else r.pool_v
        total = dot_tn(flat(r.nodes[:, :, which]), flat(parts[nwide:]))
        for first in range(0, nwide, 8):
            here = slice(first, min(first + 8, nwide))
            total = total + dot_tn(flat(r.far[here, :, which]), flat(parts[here]))
        return total

    sib_copies, x_copies = [], {}

    def kept(g):
        return (r.scores, r.dprob)[g // 2].at[(g % 2) * halfd : (g % 2 + 1) * halfd]

    def leaving(g):
        return (r.kcat, r.vcat)[g // 2].at[(g % 2) * halfd : (g % 2 + 1) * halfd]

    def x_stage(g):
        sib_copies[g].wait_recv()
        mine = slice(per * g, per * g + per)
        total = kept(g)[...] + flat(r.sib_recv[mine]).astype(F32)
        kept(g)[...] = total
        leaving(g)[...] = total.astype(BF)
        for step in x_steps:
            peer = (at.x + step) % at.nx
            x_copies[g, step] = push(
                leaving(g).at[pl.ds(pl.multiple_of(peer * band, band), band)],
                r.x_recv.at[g, step - 1],
                r.x_sems.at[g, 0, step],
                r.x_sems.at[g, 1, step],
                {"narrow": peer * 2 + at.c},
            )

    def gradient_across(g):
        mine = slice(per * g, per * g + per)
        r.sib_send[mine] = grad_half(g, sib_rows).astype(BF).reshape(per, BR, D)
        sib_copies.append(
            push(
                r.sib_send.at[mine],
                r.sib_recv.at[mine],
                r.sib_sems.at[0, g],
                r.sib_sems.at[1, g],
                sibling,
            )
        )

    def gradient_here(g):
        kept(g)[...] = grad_half(g, own_rows)

    slack = blocks * KMAX - blocks - nwide
    returns = []
    reached = 0
    groups = list(range(0, nwide, 4))
    for first in groups:
        until = slack + first + 4
        entries(reached, until)
        reached = until
        for place in range(first, first + 4):
            end = r.table[END + place]
            r.pool_k[place] = r.run_k[end]
            r.pool_v[place] = r.run_v[end]
        here = slice(first, first + 4)
        part = dot_nt(flat(r.pool_k[here]), r.w_key[...]) + dot_nt(flat(r.pool_v[here]), r.w_value[...])
        r.stage[here] = part.astype(BF).reshape(4, BR, D)
        for slot in range(first, min(first + 4, nwide - 1)):
            returns.append(
                push(
                    r.stage.at[slot],
                    r.back.at[slot],
                    r.back_sems.at[0, slot],
                    r.back_sems.at[1, slot],
                    {"wide": at.behind(slot)},
                )
            )
        if first == groups[0]:
            small.second()
        if first == groups[min(1, len(groups) - 1)]:
            gradient_across(0)
            gradient_across(1)
            gradient_here(0)
            x_stage(0)
            gradient_here(1)
            x_stage(1)
    stores.start(r.stage.at[nwide - 1], r.back_hbm.at[nwide - 1])
    entries(reached, blocks * KMAX)
    for own in range(blocks):
        end = r.table[END + nwide + own]
        has = r.table[HAS + nwide + own] > 0
        r.pool_k[nwide + own] = jnp.where(has, r.run_k[end], (r.base_k[own] * SCALE).astype(BF))
        r.pool_v[nwide + own] = jnp.where(has, r.run_v[end], r.base_v[own].astype(BF))

    gradient_across(2)
    gradient_here(2)
    gradient_across(3)
    x_stage(2)
    gradient_here(3)
    x_stage(3)
    small.third()
    pair = 2

    @pl.loop(0, blocks // pair)
    def _(i):
        here = pl.ds(i * pair, pair)
        there = pl.ds(nwide + i * pair, pair)
        total = (
            dot_nt(flat(r.dquery[here]), r.w_query[...])
            + dot_nt(flat(r.pool_k[there]), r.w_key[...])
            + dot_nt(flat(r.pool_v[there]), r.w_value[...])
        )
        r.base_v[here] = total.reshape(pair, BR, D)

    stores.start(r.base_v.at[0:blocks], r.local_hbm)

    spot = at.x * band
    for g in range(4):
        total = kept(g)[pl.ds(pl.multiple_of(spot, band), band), :]
        for step in x_steps:
            x_copies[g, step].wait()
            total = total + r.x_recv[g, step - 1].astype(F32)
        r.base_k[g * band // BR, g * band % BR : g * band % BR + band, :] = total
        r.w_send[g * band : (g + 1) * band, :] = total.astype(BF)

    w_copies = []
    for slot in range(nwide - 1):
        peer = at.ahead(slot)
        w_copies.append(
            push(
                r.w_send.at[pl.ds(pl.multiple_of(peer * chunk, chunk), chunk)],
                r.w_recv.at[slot],
                r.w_sems.at[0, slot],
                r.w_sems.at[1, slot],
                {"wide": peer},
            )
        )

    @pl.loop(0, blocks // pair)
    def _(i):
        here = pl.ds(i * pair, pair)
        out = dot(flat(r.attended[here]), r.w_out[...])
        r.attended[here] = out.astype(BF).reshape(pair, BR, D)

    stores.start(r.attended, r.out_nodes_hbm)

    spot = at.w * chunk
    total = r.base_k[spot // BR, pl.ds(pl.multiple_of(spot % BR, chunk), chunk), :]
    for slot in range(nwide - 1):
        w_copies[slot].wait_recv()
        total = total + r.w_recv[slot].astype(F32)
    done = total.astype(BF)
    r.lower[at.n, at.w] = done[:, 0:halfd]
    r.upper[at.c, at.w, at.x] = done[:, halfd:]
    up_first, low_first = [], []
    for step in x_steps:
        up_first.append(
            push(
                r.upper.at[at.c, at.w, at.x],
                r.upper.at[at.c, at.w, at.x],
                r.up_sems.at[0, 0, step],
                r.up_sems.at[0, 1, step],
                {"narrow": (at.x + step) % at.nx * 2 + at.c},
            )
        )
    for slot in range(nwide - 1):
        low_first.append(
            push(
                r.lower.at[at.n, at.w],
                r.lower.at[at.n, at.w],
                r.low_sems.at[0, 0, slot],
                r.low_sems.at[0, 1, slot],
                {"wide": at.ahead(slot)},
            )
        )
    small.finish()
    r.virt_sums[...] = r.b_summed[...]
    for copy in up_first:
        copy.wait_recv()
    up_second, low_second, across = [], {}, []
    for slot in range(nwide - 1):
        up_second.append(
            push(
                r.upper.at[at.c, at.w],
                r.upper.at[at.c, at.w],
                r.up_sems.at[1, 0, slot],
                r.up_sems.at[1, 1, slot],
                {"wide": at.ahead(slot)},
            )
        )
    for copy in low_first:
        copy.wait_recv()
    for step in x_steps:
        low_second[step] = push(
            r.lower.at[at.n],
            r.lower.at[at.n],
            r.low_sems.at[1, 0, step],
            r.low_sems.at[1, 1, step],
            {"narrow": (at.x + step) % at.nx * 2 + at.c},
        )

    def low_across(landed, step):
        across.append(
            push(
                r.lower.at[landed],
                r.lower.at[landed],
                r.across_sems.at[0, 0, step],
                r.across_sems.at[0, 1, step],
                sibling,
            )
        )

    def up_across(slot):
        landed = at.behind(slot)
        across.append(
            push(
                r.upper.at[at.c, landed],
                r.upper.at[at.c, landed],
                r.across_sems.at[1, 0, slot],
                r.across_sems.at[1, 1, slot],
                sibling,
            )
        )

    low_across(at.n, 0)
    up_across(nwide - 1)
    for slot in range(nwide - 1):
        returns[slot].wait_recv()
        stores.start(r.back.at[slot], r.back_hbm.at[slot])
    for slot in range(nwide - 1):
        up_second[slot].wait_recv()
        up_across(slot)
    for step in x_steps:
        low_second[step].wait_recv()
        low_across((at.x + at.nx - step) % at.nx * 2 + at.c, step)
    for copy in across:
        copy.wait()
    stores.start(r.lower, r.lower_hbm)
    stores.start(r.upper, r.upper_hbm)
    for copy in returns + w_copies + sib_copies + up_first + low_first + up_second:
        copy.wait_send()
    for copy in low_second.values():
        copy.wait_send()


LOADED = ("nodes", "w_key", "w_value", "virtual", "w_query", "grad_out", "w_out", "grad_virtual")


def layer_kernel(nwide, nnarrow, names, *refs):
    r = types.SimpleNamespace(**dict(zip(names, refs, strict=True)))
    at = Place(nwide, nnarrow)
    at.greet()
    started = Copies(r.load_sems)
    loads = {name: started.start(getattr(r, name + "_hbm"), getattr(r, name)) for name in LOADED}
    stores = Copies(r.store_sems)
    exchange_phase(at, r, loads)
    attend_phase(at, r)
    reduce_phase(at, r, stores)
    for copy in stores.started:
        copy.wait()


def layer(nwide, nnarrow, table, arrays):
    blocks = arrays["nodes"].shape[0]
    rows = blocks * BR
    pool = blocks + nwide
    entries = blocks * KMAX
    nx = nnarrow // 2
    band = D // 2 // nx
    chunk = 4 * band // nwide
    per = 8 // nnarrow
    sems = pltpu.SemaphoreType.DMA
    most = max(nwide, nnarrow)
    shape = jax.ShapeDtypeStruct
    outs = {
        "out_nodes_hbm": shape((blocks, BR, D), BF),
        "local_hbm": shape((blocks, BR, D), F32),
        "back_hbm": shape((nwide, BR, D), BF),
        "lower_hbm": shape((nnarrow, nwide, chunk, D // 2), BF),
        "upper_hbm": shape((2, nwide, nx, chunk, D // 2), BF),
        "virt_sums": shape((8, 24, 128), F32),
        "out_virtual": shape((VIRT, D), F32),
        "summary_out": shape((VIRT, D), BF),
        "dzeta_out": shape((VIRT, D), BF),
    }
    vmem = {name: (arrays[name].shape, arrays[name].dtype) for name in LOADED}
    vmem |= {
        "stage": ((nwide, BR, D), BF),
        "far": ((nwide, BR, D), BF),
        "queries": ((blocks, BR, D), BF),
        "d_attended": ((blocks, BR, D), BF),
        "attended": ((blocks, BR, D), BF),
        "dquery": ((blocks, BR, D), BF),
        "pool_k": ((pool, BR, D), BF),
        "pool_v": ((pool, BR, D), BF),
        "vq_bd": ((HM, D), BF),
        "vk_bd": ((HM, D), BF),
        "vv_bd": ((HM, D), BF),
        "dnum_bd": ((HM, D), BF),
        "dden": ((HM, 128), F32),
        "vq_part": ((VIRT, D), F32),
        "vk_part": ((VIRT, D), F32),
        "vv_part": ((VIRT, D), F32),
        "acc_vk": ((HM, D), F32),
        "acc_vv": ((HM, D), F32),
        "base_k": ((blocks + 1, BR, D), F32),
        "base_v": ((blocks + 1, BR, D), F32),
        "kcat": ((KMAX * BR, D), BF),
        "vcat": ((KMAX * BR, D), BF),
        "scores": ((GROUP * BR, KMAX * BR), F32),
        "dprob": ((GROUP * BR, KMAX * BR), F32),
        "probs": ((entries * 2, GROUP * BR, BR), BF),
        "dscore": ((entries * 2, GROUP * BR, BR), BF),
        "sum_k": ((BR, D), F32),
        "sum_v": ((BR, D), F32),
        "run_k": ((entries, BR, D), BF),
        "run_v": ((entries, BR, D), BF),
        "back": ((nwide, BR, D), BF),
        "sib_send": ((4 * (D // 2 // BR), BR, D), BF),
        "sib_recv": ((4 * (D // 2 // BR), BR, D), BF),
        "x_recv": ((4, nx - 1, band, D), BF),
        "w_send": ((4 * band, D), BF),
        "w_recv": ((nwide, chunk, D), BF),
        "lower": (outs["lower_hbm"].shape, BF),
        "upper": (outs["upper_hbm"].shape, BF),
    }
    for name, height in (("f_", VIRT), ("b_", 24)):
        vmem |= {
            name + "part": ((8, height, 128), F32),
            name + "one": ((nnarrow, per, height, 128), F32),
            name + "mid": ((per, height, 128), F32),
            name + "two": ((nwide, per, height, 128), F32),
            name + "summed": ((8, height, 128), F32),
        }
    sem_shapes = {
        "f_sems": (3, 2, most),
        "b_sems": (3, 2, most),
        "send_sems": (nwide,),
        "recv_sems": (nwide,),
        "back_sems": (2, nwide),
        "sib_sems": (2, 4),
        "x_sems": (4, 2, nx),
        "w_sems": (2, nwide),
        "low_sems": (2, 2, nwide),
        "up_sems": (2, 2, nwide),
        "across_sems": (2, 2, nwide),
        "load_sems": (len(LOADED),),
        "store_sems": (nwide + 4,),
    }
    names = (
        ["table"] + [name + "_hbm" for name in LOADED] + list(outs) + list(vmem) + list(sem_shapes)
    )
    results = pl.pallas_call(
        functools.partial(layer_kernel, nwide, nnarrow, names),
        out_shape=list(outs.values()),
        in_specs=[SMEM] + [ANY] * len(LOADED),
        out_specs=[ANY] * 5 + [VMEM] * 4,
        scratch_shapes=[pltpu.VMEM(*kind) for kind in vmem.values()]
        + [sems(kind) for kind in sem_shapes.values()],
        compiler_params=pltpu.CompilerParams(
            collective_id=0, has_side_effects=True, vmem_limit_bytes=VMEM_LIMIT
        ),
        name="layer",
    )(table, *[arrays[name] for name in LOADED])
    return dict(zip(outs, results))


def finish_kernel(
    nwide,
    nnarrow,
    table,
    local_hbm,
    back_hbm,
    lower_hbm,
    upper_hbm,
    out_nodes_in,
    virt_sums,
    virtual,
    summary_b,
    dzeta_b,
    out_virtual_in,
    w_query_hbm,
    w_key_hbm,
    w_value_hbm,
    out_nodes,
    grad_nodes_hbm,
    grad_query_hbm,
    grad_key_hbm,
    grad_value_hbm,
    grad_wout_hbm,
    out_virtual,
    virtual_grad,
    lower,
    upper,
    back,
    grad_nodes,
    grads,
    w_query,
    w_key,
    w_value,
    out_rows,
    load_sems,
    store_sems,
):
    at = Place(nwide, nnarrow)
    started, stores = Copies(load_sems), Copies(store_sems)
    load_local = started.start(local_hbm, grad_nodes)
    load_back = started.start(back_hbm, back)
    load_out = started.start(out_nodes_in, out_rows)
    load_low = started.start(lower_hbm, lower)
    load_up = started.start(upper_hbm, upper)
    load_w = [
        started.start(src, dst)
        for src, dst in ((w_query_hbm, w_query), (w_key_hbm, w_key), (w_value_hbm, w_value))
    ]
    out_virtual[...] = out_virtual_in[...]
    load_local.wait()
    load_back.wait()
    for slot in range(nwide):
        grad_nodes[table[PICK + slot]] += back[slot].astype(F32)
    stores.start(grad_nodes, grad_nodes_hbm)
    load_out.wait()
    stores.start(out_rows, out_nodes)
    top = jnp.concatenate([virt_sums[2 * lt] for lt in range(D // 128)], axis=1)
    bottom = jnp.concatenate([virt_sums[2 * lt + 1] for lt in range(D // 128)], axis=1)
    vq_grad = top[0:16].astype(BF)
    vk_grad = jnp.concatenate([top[16:24], bottom[0:8]], axis=0).astype(BF)
    vv_grad = bottom[8:24].astype(BF)
    halfd = D // 2
    band = halfd // at.nx
    chunk = 4 * band // nwide
    pairs = (
        (grad_wout_hbm, summary_b[...], dzeta_b[...]),
        (grad_query_hbm, virtual[...], vq_grad),
        (grad_key_hbm, virtual[...], vk_grad),
        (grad_value_hbm, virtual[...], vv_grad),
    )
    per = nwide // 4
    load_low.wait()
    load_up.wait()
    for g, (out, left, right) in enumerate(pairs):
        grads[g] = dot_tn(left, right)
        for n in range(nnarrow):
            first = (n % 2) * halfd + (n // 2) * band
            for j in range(per):
                here = slice(first + j * chunk, first + (j + 1) * chunk)
                grads[g, here, 0:halfd] += lower[n, g * per + j].astype(F32)
                grads[g, here, halfd:] += upper[n % 2, g * per + j, n // 2].astype(F32)
        stores.start(grads.at[g], out)
    for copy in load_w:
        copy.wait()
    virtual_grad[...] = (
        dot_nt(vq_grad, w_query[...]) + dot_nt(vk_grad, w_key[...]) + dot_nt(vv_grad, w_value[...])
    )
    for copy in stores.started:
        copy.wait()


def finish(nwide, nnarrow, table, got, arrays):
    shape = jax.ShapeDtypeStruct
    outs = (
        [shape(got["out_nodes_hbm"].shape, BF), shape(got["local_hbm"].shape, F32)]
        + [shape((D, D), F32)] * 4
        + [shape((VIRT, D), F32)] * 2
    )
    scratch = [(got[name].shape, got[name].dtype) for name in ("lower_hbm", "upper_hbm", "back_hbm", "local_hbm")]
    scratch += [((4, D, D), F32)] + [((D, D), BF)] * 3
    scratch += [(got["out_nodes_hbm"].shape, BF)]
    return pl.pallas_call(
        functools.partial(finish_kernel, nwide, nnarrow),
        out_shape=outs,
        in_specs=[SMEM] + [ANY] * 5 + [VMEM] * 5 + [ANY] * 3,
        out_specs=[ANY] * 6 + [VMEM] * 2,
        scratch_shapes=[pltpu.VMEM(*kind) for kind in scratch]
        + [pltpu.SemaphoreType.DMA((8,)), pltpu.SemaphoreType.DMA((6,))],
        compiler_params=pltpu.CompilerParams(vmem_limit_bytes=VMEM_LIMIT),
        name="finish",
    )(
        table,
        *[got[name] for name in ("local_hbm", "back_hbm", "lower_hbm", "upper_hbm", "out_nodes_hbm", "virt_sums")],
        arrays["virtual"],
        *[got[name] for name in ("summary_out", "dzeta_out", "out_virtual")],
        arrays["w_query"],
        arrays["w_key"],
        arrays["w_value"],
    )


def shards(
    nwide,
    nnarrow,
    nodes,
    virtual,
    w_query,
    w_key,
    w_value,
    w_out,
    col_blocks,
    col_count,
    send_sel,
    grad_out,
    grad_virtual,
):
    rows = nodes.shape[0]
    arrays = {
        "nodes": nodes.reshape(rows // BR, BR, D),
        "w_key": w_key,
        "w_value": w_value,
        "virtual": virtual,
        "w_query": w_query,
        "grad_out": grad_out,
        "w_out": w_out,
        "grad_virtual": grad_virtual,
    }
    table = tables(nwide, nnarrow, col_blocks.T, col_count, send_sel)
    got = layer(nwide, nnarrow, table, arrays)
    out_nodes, grad_nodes, grad_query, grad_key, grad_value, grad_wout, out_virtual, virtual_grad = finish(
        nwide, nnarrow, table, got, arrays
    )
    return (
        out_nodes.reshape(rows, D),
        out_virtual,
        grad_nodes.reshape(rows, D),
        virtual_grad,
        grad_query,
        grad_key,
        grad_value,
        grad_wout,
    )


def solution(mesh):
    spread = P(("wide", "narrow"), None)
    in_specs = (
        spread,
        P(),
        P(),
        P(),
        P(),
        P(),
        spread,
        P(("wide", "narrow")),
        P("wide", "narrow", None),
        spread,
        P(),
    )
    out_specs = (spread, P(), spread, P(), P(), P(), P(), P())
    return jax.shard_map(
        functools.partial(shards, mesh.shape["wide"], mesh.shape["narrow"]),
        mesh=mesh,
        in_specs=in_specs,
        out_specs=out_specs,
        check_vma=False,
    )
```
